32 devices in a mesh: dp: 8 (over y, x, core), chan: 4 (over z).
Axes of the slice: x: 2, y: 2, z: 4, core: 2. Of those that a mesh axis runs over, the one named last changes fastest.
Arguments:
- features: bfloat16 [8, 32, 32, 512], P('dp', None, None, 'chan'), may hold values from -6 to 6
- z_table: float32 [1024, 512], replicated, may hold values from -6 to 6
- seeds: int32 [8, 2], P('dp'), may hold values from 0 to 1023
- crossover: int32 [8], P('dp'), may hold values from 0 to 2
- counted: int32 [8], P('dp'), may hold values from 0 to 1, as said below
- head: bfloat16 [3, 1024], replicated, may hold values from -0.109375 to 0.109375
- w_avg: float32 [512], replicated, may hold values from -4 to 4
- map_w: float32 [8, 512, 512], P(None, 'dp'), may hold values from -0.25 to 0.25
- map_w_mom: float32 [8, 512, 512], P(None, 'dp'), may hold values from -0.125 to 0.125
- map_w_ema: float32 [8, 512, 512], P(None, 'dp'), may hold values from -0.25 to 0.25
- map_b: float32 [8, 512], replicated, may hold values from -4 to 4
- map_b_mom: float32 [8, 512], replicated, may hold values from -0.25 to 0.25
- map_b_ema: float32 [8, 512], replicated, may hold values from -4 to 4
- aff_w: float32 [2, 512, 512], P(None, None, 'chan'), may hold values from -0.25 to 0.25
- aff_w_mom: float32 [2, 512, 512], P(None, None, 'chan'), may hold values from -0.078125 to 0.078125
- aff_w_ema: float32 [2, 512, 512], P(None, None, 'chan'), may hold values from -0.25 to 0.25
- chan_bias: float32 [3, 512], P(None, 'chan'), may hold values from 0.5 to 1.5
- chan_bias_mom: float32 [3, 512], P(None, 'chan'), may hold values from -0.15625 to 0.15625
- chan_bias_ema: float32 [3, 512], P(None, 'chan'), may hold values from 0.5 to 1.5
- conv_w: float32 [3, 3, 512, 512], P(None, None, None, 'chan'), may hold values from -0.09375 to 0.09375
- conv_w_mom: float32 [3, 3, 512, 512], P(None, None, None, 'chan'), may hold values from -0.15625 to 0.15625
- conv_w_ema: float32 [3, 3, 512, 512], P(None, None, None, 'chan'), may hold values from -0.09375 to 0.09375
- rgb_w: float32 [3, 512], P(None, 'chan'), may hold values from -0.25 to 0.25
- rgb_w_mom: float32 [3, 512], P(None, 'chan'), may hold values from -3 to 3
- rgb_w_ema: float32 [3, 512], P(None, 'chan'), may hold values from -0.25 to 0.25
Outputs:
- map_w_new: float32 [8, 512, 512], P(None, 'dp')
- map_w_mom_new: float32 [8, 512, 512], P(None, 'dp')
- map_w_ema_new: float32 [8, 512, 512], P(None, 'dp')
- map_w_copy: bfloat16 [8, 512, 512], P(None, 'dp')
- map_b_new: float32 [8, 512], replicated
- map_b_mom_new: float32 [8, 512], replicated
- map_b_ema_new: float32 [8, 512], replicated
- map_b_copy: bfloat16 [8, 512], replicated
- aff_w_new: float32 [2, 512, 512], P(None, None, 'chan')
- aff_w_mom_new: float32 [2, 512, 512], P(None, None, 'chan')
- aff_w_ema_new: float32 [2, 512, 512], P(None, None, 'chan')
- aff_w_copy: bfloat16 [2, 512, 512], P(None, None, 'chan')
- chan_bias_new: float32 [3, 512], P(None, 'chan')
- chan_bias_mom_new: float32 [3, 512], P(None, 'chan')
- chan_bias_ema_new: float32 [3, 512], P(None, 'chan')
- chan_bias_copy: bfloat16 [3, 512], P(None, 'chan')
- conv_w_new: float32 [3, 3, 512, 512], P(None, None, None, 'chan')
- conv_w_mom_new: float32 [3, 3, 512, 512], P(None, None, None, 'chan')
- conv_w_ema_new: float32 [3, 3, 512, 512], P(None, None, None, 'chan')
- conv_w_copy: bfloat16 [3, 3, 512, 512], P(None, None, None, 'chan')
- rgb_w_new: float32 [3, 512], P(None, 'chan')
- rgb_w_mom_new: float32 [3, 512], P(None, 'chan')
- rgb_w_ema_new: float32 [3, 512], P(None, 'chan')
- rgb_w_copy: bfloat16 [3, 512], P(None, 'chan')
- w_avg_new: float32 [512], replicated
- loss_sum: float32 [], replicated
- loss_count: float32 [], replicated
The draws below stay inside these ranges and needn't reach their ends.
Inputs may be any that keep to these rules, and one draw needn't show every extreme that they name: `counted`: the chance that a sample counts rises from a quarter to three quarters along the samples; the last sample always counts.
All inputs are finite; a program needn't handle non-finite values.
Results may differ from the reference program's by a relative error of at most 0.012.
Values may be sent and summed in bfloat16 or wider, within the bound.
No kernel may reach another device: no remote copies, remote signals or barrier semaphores. Data moves between devices by JAX's collectives and lax.ppermute only.
A program may use at most 128 MiB of HBM per device.

```python
import jax
import jax.numpy as jnp
from jax import lax

C = 512
LAYERS = 8
RES = 32
TABLE = 1024
SAMPLES = 8


def draw_counted(key, part):
    key = jax.random.fold_in(key, 7)
    ticket = jax.random.randint(key, (SAMPLES,), 0, 1000)
    level = 250 + 500 * jnp.arange(SAMPLES, dtype=jnp.int32) // SAMPLES
    picked = (ticket < level).astype(jnp.int32)
    return picked.at[SAMPLES - 1].set(1)


def place_ends(array, key, smallest, top_value):
    shape = array.shape
    place = [jax.random.randint(jax.random.fold_in(key, axis), (), 0, shape[axis]) for axis in range(len(shape))]
    array = array.at[tuple(place)].set(smallest)
    longest = shape.index(max(shape))
    place[longest] = (place[longest] + 1) % shape[longest]
    return array.at[tuple(place)].set(top_value)


def levels(key, shape, shards, least, high):
    gain = 1.0
    for axis_at, shards_of in shards:
        heights = jax.random.uniform(jax.random.fold_in(jax.random.fold_in(key, 6), axis_at), (shards_of,), jnp.float32, least / len(shards), high / len(shards))
        gain = gain * jnp.repeat(jnp.exp(heights), shape[axis_at] // shards_of).reshape((-1,) + (1,) * (len(shape) - 1 - axis_at))
    return gain


def scatter_about(stream_key, dims, deviation, reach, pieces=(), kind=jnp.bfloat16):
    drawn = jax.random.normal(stream_key, dims, jnp.float32) * deviation
    if len(pieces) > 0:
        drawn = levels(stream_key, dims, pieces, -0.22, 0.18) * drawn
    return jnp.clip(drawn, min=-reach, max=reach).astype(kind)


def setup_inputs(seed: int = 0) -> dict:
    key_of = jax.random.split(jax.random.key(seed), 26)
    return {
        "features": scatter_about(key_of[0], (SAMPLES, RES, RES, C), 1.0, 6.0, ((0, 8), (3, 4))),
        "z_table": scatter_about(key_of[1], (TABLE, C), 1.0, 6.0, (), jnp.float32),
        "seeds": place_ends(jax.random.randint(key_of[2], (SAMPLES, 2), 0, TABLE), jax.random.fold_in(key_of[2], 1), 0, TABLE - 1).astype(jnp.int32),
        "crossover": place_ends(jax.random.randint(key_of[3], (SAMPLES,), 0, 3), jax.random.fold_in(key_of[3], 1), 0, 2).astype(jnp.int32),
        "counted": draw_counted(jax.random.fold_in(key_of[25], 71), 0),
        "head": scatter_about(key_of[5], (3, RES * RES), (3 * RES * RES) ** -0.5, 0.109375),
        "w_avg": scatter_about(key_of[6], (C,), 0.3, 4.0, (), jnp.float32),
        "map_w": scatter_about(key_of[7], (LAYERS, C, C), C ** -0.5, 0.25, ((1, 8),), jnp.float32),
        "map_w_mom": scatter_about(key_of[8], (LAYERS, C, C), (0.024 * SAMPLES ** -0.5), 0.125, ((1, 8),), jnp.float32),
        "map_w_ema": scatter_about(key_of[9], (LAYERS, C, C), C ** -0.5, 0.25, ((1, 8),), jnp.float32),
        "map_b": scatter_about(key_of[10], (LAYERS, C), 0.3, 4.0, (), jnp.float32),
        "map_b_mom": scatter_about(key_of[11], (LAYERS, C), (0.05 * SAMPLES ** -0.5), 0.25, (), jnp.float32),
        "map_b_ema": scatter_about(key_of[12], (LAYERS, C), 0.3, 4.0, (), jnp.float32),
        "aff_w": scatter_about(key_of[13], (2, C, C), C ** -0.5, 0.25, ((2, 4),), jnp.float32),
        "aff_w_mom": scatter_about(key_of[14], (2, C, C), (0.016 * SAMPLES ** -0.5), 0.078125, ((2, 4),), jnp.float32),
        "aff_w_ema": scatter_about(key_of[15], (2, C, C), C ** -0.5, 0.25, ((2, 4),), jnp.float32),
        "chan_bias": jnp.clip(1.0 + 0.1 * jax.random.normal(key_of[16], (3, C), jnp.float32), 0.5, 1.5),
        "chan_bias_mom": scatter_about(key_of[17], (3, C), (0.032 * SAMPLES ** -0.5), 0.15625, ((1, 4),), jnp.float32),
        "chan_bias_ema": jnp.clip(1.0 + 0.1 * jax.random.normal(key_of[18], (3, C), jnp.float32), 0.5, 1.5),
        "conv_w": scatter_about(key_of[19], (3, 3, C, C), (9 * C) ** -0.5, 0.09375, ((3, 4),), jnp.float32),
        "conv_w_mom": scatter_about(key_of[20], (3, 3, C, C), (0.032 * SAMPLES ** -0.5), 0.15625, ((3, 4),), jnp.float32),
        "conv_w_ema": scatter_about(key_of[21], (3, 3, C, C), (9 * C) ** -0.5, 0.09375, ((3, 4),), jnp.float32),
        "rgb_w": scatter_about(key_of[22], (3, C), C ** -0.5, 0.25, ((1, 4),), jnp.float32),
        "rgb_w_mom": scatter_about(key_of[23], (3, C), (0.58 * SAMPLES ** -0.5), 3.0, ((1, 4),), jnp.float32),
        "rgb_w_ema": scatter_about(key_of[24], (3, C), C ** -0.5, 0.25, ((1, 4),), jnp.float32),
    }


@jax.custom_vjp
def low(v):
    return lax.optimization_barrier(v.astype(jnp.bfloat16)).astype(jnp.float32)

@jax.custom_vjp
def low_back(v):
    return v

def low_keep(v):
    return (low(v), None)

def low_pass(kept, grad):
    return (grad,)

def back_keep(v):
    return (v, None)

def back_low(kept, grad):
    return (low(grad),)
low.defvjp(low_keep, low_pass)
low_back.defvjp(back_keep, back_low)
MOMENTUM = 0.9
EMA_DECAY = 0.95
AVERAGE_BETA = 0.5
HIGHEST_PRECISION = lax.Precision.HIGHEST

def forward(map_w, map_b, aff_w, chan_bias, conv_w, rgb_w, latents, crossover, weight_mask, features, head):
    hidden = latents * lax.rsqrt(lax.optimization_barrier(jnp.mean(latents * latents, axis=1, keepdims=True)) + 1e-08)
    for layer_index in range(LAYERS):
        preact = jnp.dot(low(hidden), low(map_w[layer_index]), precision=HIGHEST_PRECISION) + map_b[layer_index]
        hidden = jax.nn.silu(preact)
    pair_low = low(hidden).reshape(SAMPLES, 2, C)
    choose = crossover[:, None] > jnp.arange(2, dtype=jnp.int32)[None, :]
    picked = jnp.where(choose[:, :, None], pair_low[:, 0:1, :], pair_low[:, 1:2, :])
    style = low(jnp.einsum('sjc,jcd->sjd', picked, low(aff_w), precision=HIGHEST_PRECISION) + chan_bias[None, :2, :])
    modulated = low(features * style[:, 0, None, None, :])
    kernel = low(conv_w)
    conv_out = low_back(lax.conv_general_dilated(modulated, kernel, (1, 1), 'SAME', dimension_numbers=('NHWC', 'HWIO', 'NHWC'), precision=HIGHEST_PRECISION))
    kernel_sq = lax.optimization_barrier(jnp.sum(kernel * kernel, axis=(0, 1)))
    demod = lax.rsqrt(jnp.dot(style[:, 0] * style[:, 0], kernel_sq, precision=HIGHEST_PRECISION) + 1e-08)
    scaled = conv_out * demod[:, None, None, :] + chan_bias[2]
    act_mod = low(jax.nn.silu(scaled) * style[:, 1, None, None, :])
    colour = jnp.einsum('shwo,co->schw', act_mod, low(rgb_w), precision=HIGHEST_PRECISION)
    logit = jnp.einsum('schw,chw->s', colour, head.reshape(3, RES, RES), precision=HIGHEST_PRECISION)
    return (jnp.sum(weight_mask * jax.nn.softplus(-logit)), hidden)

def advance(param, moment, average, grad, rate):
    moment_new = MOMENTUM * moment + grad
    param_new = param - rate * (grad + MOMENTUM * moment_new)
    average_new = EMA_DECAY * average + (1.0 - EMA_DECAY) * param_new
    return (param_new, moment_new, average_new, param_new.astype(jnp.bfloat16))

def reference(features, z_table, seeds, crossover, counted, head, w_avg, map_w, map_w_mom, map_w_ema, map_b, map_b_mom, map_b_ema, aff_w, aff_w_mom, aff_w_ema, chan_bias, chan_bias_mom, chan_bias_ema, conv_w, conv_w_mom, conv_w_ema, rgb_w, rgb_w_mom, rgb_w_ema):
    latents = jnp.take(z_table, seeds.reshape(-1), axis=0)
    weight_mask = counted.astype(jnp.float32)
    total_count = jnp.sum(weight_mask)
    features_wide = features.astype(jnp.float32)
    head_wide = head.astype(jnp.float32)

    def loss_of(p_map_w, p_map_b, p_aff_w, p_chan_bias, p_conv_w, p_rgb_w):
        return forward(p_map_w, p_map_b, p_aff_w, p_chan_bias, p_conv_w, p_rgb_w, latents, crossover, weight_mask, features_wide, head_wide)
    loss_sum, pullback, latent_w = jax.vjp(loss_of, map_w, map_b, aff_w, chan_bias, conv_w, rgb_w, has_aux=True)
    grads = pullback(jnp.ones((), jnp.float32))
    inverse = 1.0 / total_count
    outputs = advance(map_w, map_w_mom, map_w_ema, grads[0] * inverse, 30.0)
    outputs = outputs + advance(map_b, map_b_mom, map_b_ema, grads[1] * inverse, 30.0)
    outputs = outputs + advance(aff_w, aff_w_mom, aff_w_ema, grads[2] * inverse, 30.0)
    outputs = outputs + advance(chan_bias, chan_bias_mom, chan_bias_ema, grads[3] * inverse, 50.0)
    outputs = outputs + advance(conv_w, conv_w_mom, conv_w_ema, grads[4] * inverse, 5.0)
    outputs = outputs + advance(rgb_w, rgb_w_mom, rgb_w_ema, grads[5] * inverse, 1.0)
    w_avg_new = w_avg + (1.0 - AVERAGE_BETA) * (lax.optimization_barrier(jnp.mean(latent_w, axis=0)) - w_avg)
    return outputs + (w_avg_new, loss_sum, total_count)
```

```python
import functools

import jax
import jax.numpy as jnp
from jax import lax
from jax.experimental import pallas as pl
from jax.experimental.pallas import tpu as pltpu
from jax.sharding import PartitionSpec as P

MOMENTUM = 0.9
EMA_DECAY = 0.95
AVERAGE_BETA = 0.5
BF16 = jnp.bfloat16
F32 = jnp.float32
TAPS = 9
LANES = 128
COUNT_ROWS = 32
VMEM = pl.BlockSpec(memory_space=pltpu.VMEM)
SMEM = pl.BlockSpec(memory_space=pltpu.SMEM)
HBM = pl.BlockSpec(memory_space=pl.ANY)


def shape(dims, dtype):
    return jax.ShapeDtypeStruct(dims, dtype)


def params(mib):
    return pltpu.CompilerParams(vmem_limit_bytes=mib * 1024 * 1024)


def swap(value, axis, distance):
    return lax.ppermute(
        value, axis, [(i, i ^ distance) for i in range(lax.axis_size(axis))]
    )


def spread(value, axis):
    size = lax.axis_size(axis)
    parts = [value] * size
    for k in range(2, size, 2):
        parts[k] = swap(value, axis, k)
    for k in range(0, size, 2):
        parts[k + 1] = swap(parts[k], axis, 1)
    return parts


def spread_direct(value, axis):
    return [value] + [swap(value, axis, k) for k in range(1, lax.axis_size(axis))]


def silu_slope(preact):
    sig = jax.nn.sigmoid(preact)
    return sig * (1.0 + preact * (1.0 - sig))


def pieces(value, count):
    out = []
    for _ in range(count):
        part = value.astype(BF16)
        out.append(part)
        value = value - part.astype(F32)
    return out


def advance(param, moment, average, grad, rate):
    moment_new = MOMENTUM * moment + grad
    param_new = param - rate * (grad + MOMENTUM * moment_new)
    average_new = EMA_DECAY * average + (1.0 - EMA_DECAY) * param_new
    return param_new, moment_new, average_new, param_new.astype(BF16)


def dot(a, b):
    return jnp.dot(a, b, preferred_element_type=F32)


def dot_nt(a, b):
    return lax.dot_general(a, b, (((1,), (1,)), ((), ())), preferred_element_type=F32)


def dot_tn(a, b):
    return lax.dot_general(a, b, (((0,), (0,)), ((), ())), preferred_element_type=F32)


def prepare_kernel(where, map_w, aff_w, bias, map_low, aff_part):
    map_low[...] = map_w[...].astype(BF16)
    half = aff_part.shape[0] - 16
    start = pl.multiple_of(lax.rem(where[0], 2) * half, half)
    aff_part[pl.ds(0, half), :] = aff_w[0, pl.ds(start, half), :].astype(BF16)
    hi, mid, lo = pieces(bias[0:1, :], 3)
    rows = jnp.concatenate(
        [hi.astype(F32), mid.astype(F32), lo.astype(F32), jnp.zeros((13, LANES), F32)], axis=0
    )
    aff_part[pl.ds(half, 16), :] = rows.astype(BF16)


def main_kernel(n_dp, n_ch, samples, side, *refs):
    refs = list(refs)

    def take(count):
        got = refs[:count]
        del refs[:count]
        return got

    where, seeds, crossover = take(3)
    map_parts = take(n_dp)
    feat_parts = take(n_ch)
    aff_own, aff_pair = take(n_ch), take(n_ch)
    z_table, conv_w = take(2)
    aff_w, map_b, bias, head, head_t, rgb_w = take(6)
    unit, to_sum, pre_out, hid_out, top_out, picked_out, small, map_out, aff_out = take(9)
    (
        map_full,
        aff_full,
        bias_full,
        feat,
        feat_t,
        kernel_f,
        kernel,
        padded,
        taps,
        shifted,
        wide,
        rows,
        sem_map,
        sem_feat,
        sem_aff,
        sem_z,
        sem_conv,
        sem_out,
    ) = refs
    layers, share, width = map_parts[0].shape
    pixels = side * side
    latents = 2 * samples
    half = aff_own[0].shape[0] - 16
    dp, ch = where[0], where[1]
    pair = lax.rem(dp, 2)

    z_copies = []
    for n in range(latents):
        at = pl.multiple_of((seeds[n] // 8) * 8, 8)
        z_copies.append(pltpu.make_async_copy(z_table.at[pl.ds(at, 8), :], rows.at[n], sem_z.at[n]))
    map_copies = []
    for k in range(n_dp):
        at = pl.multiple_of(lax.bitwise_xor(dp, k) * share, share)
        map_copies.append(
            pltpu.make_async_copy(
                map_parts[k], map_full.at[:, pl.ds(at, share), :], sem_map.at[k]
            )
        )
    aff_copies, feat_copies = [], []
    for k in range(n_ch):
        lane = pl.ds(pl.multiple_of(lax.bitwise_xor(ch, k) * LANES, LANES), LANES)
        mine = pl.ds(pl.multiple_of(pair * half, half), half)
        other = pl.ds(pl.multiple_of((1 - pair) * half, half), half)
        aff_copies.append(
            pltpu.make_async_copy(
                aff_own[k].at[pl.ds(0, half), :], aff_full.at[mine, lane], sem_aff.at[3 * k]
            )
        )
        aff_copies.append(
            pltpu.make_async_copy(
                aff_pair[k].at[pl.ds(0, half), :], aff_full.at[other, lane], sem_aff.at[3 * k + 1]
            )
        )
        aff_copies.append(
            pltpu.make_async_copy(
                aff_own[k].at[pl.ds(half, 16), :], bias_full.at[:, lane], sem_aff.at[3 * k + 2]
            )
        )
        feat_copies.append(
            pltpu.make_async_copy(feat_parts[k], feat.at[:, :, lane], sem_feat.at[k])
        )
    conv_copy = pltpu.make_async_copy(conv_w, kernel_f, sem_conv)
    for copy in z_copies + map_copies + aff_copies + feat_copies + [conv_copy]:
        copy.start()

    hidden_rows = []
    for n in range(latents):
        z_copies[n].wait()
        row = rows[n, pl.ds(lax.rem(seeds[n], 8), 1), :]
        scale = lax.rsqrt(jnp.mean(row * row, axis=1, keepdims=True) + 1e-08)
        hidden_rows.append(row * scale)
    hidden_rows.append(jnp.zeros((16 - latents, width), F32))
    hidden = jnp.concatenate(hidden_rows, axis=0)
    for copy in map_copies:
        copy.wait()
    keep_map = pltpu.make_async_copy(map_full, map_out, sem_out.at[0])
    keep_map.start()
    for layer in range(layers):
        low = hidden.astype(BF16)
        preact = dot(low, map_full[layer]) + map_b[pl.ds(layer, 1), :]
        hid_out[layer] = low.astype(F32)[0:8]
        pre_out[layer] = preact[0:8]
        hidden = preact * jax.nn.sigmoid(preact)
    top_out[...] = hidden[0:8]
    low = hidden.astype(BF16).astype(F32)

    conv_copy.wait()
    square = jnp.zeros((width, LANES), F32)
    for tap in range(TAPS):
        tap_low = kernel_f[tap].astype(BF16)
        kernel[tap // 3, :, pl.ds((tap % 3) * LANES, LANES)] = tap_low
        wide_tap = tap_low.astype(F32)
        square = square + wide_tap * wide_tap
    for copy in feat_copies:
        copy.wait()
    for s in range(samples):
        feat_t[s] = feat[s].T

    for copy in aff_copies:
        copy.wait()
    keep_aff = pltpu.make_async_copy(aff_full, aff_out, sem_out.at[1])
    keep_aff.start()
    for j in range(2):
        chosen = []
        for s in range(samples):
            first = crossover[s] > j
            chosen.append(
                jnp.where(first, low[2 * s : 2 * s + 1, :], low[2 * s + 1 : 2 * s + 2, :])
            )
        chosen.append(jnp.zeros((8 - samples, width), F32))
        picked_out[j] = jnp.concatenate(chosen, axis=0)
    wide_bias = bias_full[...].astype(F32)
    bias_row = wide_bias[0:1] + wide_bias[1:2] + wide_bias[2:3]
    style0 = (dot(picked_out[0].astype(BF16), aff_full[...]) + bias_row).astype(BF16)
    colour_aff = aff_w[1].astype(BF16)
    style1 = dot(picked_out[1].astype(BF16), colour_aff) + bias[1:2, :]
    style0_wide = style0.astype(F32)
    style1 = style1.astype(BF16).astype(F32)
    colour_aff = colour_aff.astype(F32)
    colour = rgb_w[...].astype(BF16)
    colour_wide = colour.astype(F32)
    colour_rows = jnp.concatenate(
        [colour_wide, jnp.zeros((LANES - 3, LANES), F32)], axis=0
    ).astype(BF16)
    conv_bias = bias[2:3, :]
    chunk = min(256, pixels)
    steps = pixels // chunk
    column = lax.rem(lax.broadcasted_iota(jnp.int32, (chunk, LANES), 0), side)
    not_first, not_last = column > 0, column < side - 1
    small[...] = jnp.zeros_like(small)
    to_sum[...] = jnp.zeros_like(to_sum)
    padded[pl.ds(0, side), :] = jnp.zeros((side, width), BF16)
    padded[pl.ds(side + pixels, side), :] = jnp.zeros((side, width), BF16)
    taps[pl.ds(0, 8), :] = jnp.zeros((8, 3 * LANES), F32)
    taps[pl.ds(8 + pixels, 8), :] = jnp.zeros((8, 3 * LANES), F32)
    wide[pl.ds(0, 8), :] = jnp.zeros((8, LANES), F32)
    wide[pl.ds(8 + pixels, 8), :] = jnp.zeros((8, LANES), F32)

    for s in range(samples):
        style_row = style0[s : s + 1, :]
        for r in range(steps):
            padded[pl.ds(side + r * chunk, chunk), :] = feat[s, pl.ds(r * chunk, chunk), :] * style_row
        style_col = jnp.broadcast_to(style0_wide[s : s + 1, :], (LANES, width)).T
        demod = lax.rsqrt(
            jnp.sum(style_col * style_col * square, axis=0, keepdims=True) + 1e-08
        )
        style_colour = style1[s : s + 1, :]
        for r in range(steps):
            total = dot(padded[pl.ds(r * chunk, chunk), :], kernel[0])
            total = total + dot(padded[pl.ds(side + r * chunk, chunk), :], kernel[1])
            total = total + dot(padded[pl.ds(2 * side + r * chunk, chunk), :], kernel[2])
            taps[pl.ds(8 + r * chunk, chunk), :] = total
        mixed = jnp.zeros((3, LANES), F32)
        g_style1 = jnp.zeros((1, LANES), F32)
        g_bias = jnp.zeros((1, LANES), F32)
        g_demod = jnp.zeros((1, LANES), F32)
        for r in range(steps):
            left = taps[pl.ds(7 + r * chunk, chunk), pl.ds(0, LANES)]
            centre = taps[pl.ds(8 + r * chunk, chunk), pl.ds(LANES, LANES)]
            right = taps[pl.ds(9 + r * chunk, chunk), pl.ds(2 * LANES, LANES)]
            conv_out = centre + jnp.where(not_first, left, 0.0) + jnp.where(not_last, right, 0.0)
            scaled = conv_out * demod + conv_bias
            sig = jax.nn.sigmoid(scaled)
            activated = scaled * sig
            act_mod = (activated * style_colour).astype(BF16)
            mixed = mixed + dot(head[:, pl.ds(r * chunk, chunk)], act_mod)
            g_act = dot(head_t[pl.ds(r * chunk, chunk), :], colour_rows)
            g_style1 = g_style1 + jnp.sum(g_act * activated, axis=0, keepdims=True)
            g_scaled = g_act * style_colour * (sig * (1.0 + scaled * (1.0 - sig)))
            g_bias = g_bias + jnp.sum(g_scaled, axis=0, keepdims=True)
            g_demod = g_demod + jnp.sum(g_scaled * conv_out, axis=0, keepdims=True)
            wide[pl.ds(8 + r * chunk, chunk), :] = g_scaled * demod
        for r in range(steps):
            before = jnp.where(not_last, wide[pl.ds(9 + r * chunk, chunk), :], 0.0)
            centre = wide[pl.ds(8 + r * chunk, chunk), :]
            after = jnp.where(not_first, wide[pl.ds(7 + r * chunk, chunk), :], 0.0)
            for dx, value in enumerate((before, centre, after)):
                value = value.astype(BF16)
                for dy in range(3):
                    lane = pl.ds((3 * dy + dx) * LANES, LANES)
                    start = r * chunk + (dy - 1) * side
                    low_at, high_at = max(start, 0), min(start + chunk, pixels)
                    shifted[pl.ds(low_at, high_at - low_at), lane] = value[
                        low_at - start : high_at - start, :
                    ]
        for dx in range(3):
            shifted[pl.ds(pixels - side, side), pl.ds(dx * LANES, LANES)] = jnp.zeros(
                (side, LANES), BF16
            )
            shifted[pl.ds(0, side), pl.ds((6 + dx) * LANES, LANES)] = jnp.zeros(
                (side, LANES), BF16
            )
        factor = g_demod * demod * demod * demod
        g_style = jnp.zeros((width, LANES), F32)
        for first in range(0, TAPS, 2):
            count = min(2, TAPS - first)
            block = dot(feat_t[s], shifted[:, pl.ds(first * LANES, count * LANES)])
            for tap in range(first, first + count):
                raw = block[:, (tap - first) * LANES : (tap - first + 1) * LANES]
                weight = kernel[tap // 3, :, pl.ds((tap % 3) * LANES, LANES)].astype(F32)
                inner = raw - style_col * (weight * factor)
                g_style = g_style + weight * inner
                unit[s, pl.ds(tap * width, width), :] = (style_col * inner).astype(BF16)
        g_style_row = jnp.sum(g_style.T, axis=0, keepdims=True)
        g_colour_row = jnp.sum((colour_aff * g_style1).T, axis=0, keepdims=True)
        logit = jnp.sum(
            jnp.sum(mixed * colour_wide, axis=0, keepdims=True), axis=1, keepdims=True
        )
        to_sum[pl.ds(8 * s, 1), :] = jnp.broadcast_to(logit, (1, width))
        to_sum[pl.ds(8 * s + 1, 1), :] = g_style_row
        to_sum[pl.ds(8 * s + 2, 1), :] = g_colour_row
        small[pl.ds(8 * s, 1), :] = g_style1
        small[pl.ds(8 * s + 1, 1), :] = g_bias
        small[pl.ds(8 * s + 2, 3), :] = mixed
    keep_map.wait()
    keep_aff.wait()


def summed(parts, row):
    values = [part[pl.ds(row, 1), :] for part in parts]
    while len(values) > 1:
        values = [values[i] + values[i + 1] for i in range(0, len(values), 2)]
    return values[0]


def logit_grad(parts, counted, s):
    logit = summed(parts, 8 * s)
    mask = jnp.full(logit.shape, counted[s], jnp.int32).astype(F32)
    return -mask * jax.nn.sigmoid(-logit), mask * jax.nn.softplus(-logit), mask


def scale_kernel(n_ch, samples, where, counted, *refs):
    parts, (unit, kept, sent) = refs[:n_ch], refs[n_ch:]
    pair = lax.rem(where[0], 2)
    half = unit.shape[1] // 2
    grads, total = [], jnp.zeros((1, LANES), F32)
    for s in range(samples):
        grad, _, mask = logit_grad(parts, counted, s)
        grads.append(grad[:, :LANES])
        total = total + mask[:, :LANES]
    block = half // 9
    for out, owner in ((kept, pair), (sent, 1 - pair)):
        for b in range(9):
            at = pl.multiple_of(owner * half + b * block, block)
            value = grads[0] * unit[0, pl.ds(at, block), :].astype(F32)
            for s in range(1, samples):
                value = value + grads[s] * unit[s, pl.ds(at, block), :].astype(F32)
            out[pl.ds(b * block, block), :] = value.astype(BF16)
        out[pl.ds(half, COUNT_ROWS), :] = jnp.broadcast_to(total, (COUNT_ROWS, LANES)).astype(BF16)


def mapping_kernel(n_ch, samples, where, counted, crossover, *refs):
    parts = refs[:n_ch]
    pre, hid, top, picked, small, map_full, aff_full, pack, rows = refs[n_ch:]
    layers, _, width = map_full.shape
    latents = 2 * samples
    ch = where[1]
    grads = [logit_grad(parts, counted, s) for s in range(samples)]
    pack[...] = jnp.zeros_like(pack)
    base = 2 * layers * latents
    style_rows = []
    for s in range(samples):
        grad = grads[s][0]
        style_row = grad * summed(parts, 8 * s + 1)
        rows[pl.ds(s, 1), :] = style_row
        style_rows.append(style_row)
        line = base + latents + 2 * s
        own = rows[pl.ds(s, 1), pl.ds(pl.multiple_of(ch * LANES, LANES), LANES)]
        short = grad[:, :LANES]
        pack[pl.ds(line, 1), pl.ds(0, LANES)] = own
        pack[pl.ds(line, 1), pl.ds(LANES, LANES)] = short * small[pl.ds(8 * s, 1), :]
        pack[pl.ds(line, 1), pl.ds(2 * LANES, LANES)] = short * small[pl.ds(8 * s + 1, 1), :]
        half_lane = lax.broadcasted_iota(jnp.int32, (1, LANES), 1) < LANES // 2
        pack[pl.ds(line, 1), pl.ds(3 * LANES, LANES)] = jnp.where(
            half_lane, grads[s][1][:, :LANES], grads[s][2][:, :LANES]
        )
        for c in range(3):
            pack[pl.ds(line + 1, 1), pl.ds(c * LANES, LANES)] = short * small[
                pl.ds(8 * s + 2 + c, 1), :
            ]
        for j in range(2):
            pack[pl.ds(base + 2 * s + j, 1), :] = picked[j, pl.ds(s, 1), :]
    w_total = top[pl.ds(0, 1), :]
    for n in range(1, latents):
        w_total = w_total + top[pl.ds(n, 1), :]
    pack[pl.ds(base + latents + 2 * samples, 1), :] = w_total

    def back(value, weights):
        hi, lo = pieces(value, 2)
        both = jnp.concatenate([hi.astype(F32), lo.astype(F32)], axis=0).astype(BF16)
        out = dot_nt(both, weights)
        return out[0:8] + out[8:16]

    pad = [jnp.zeros((8 - samples, width), F32)]
    from_conv = back(jnp.concatenate(style_rows + pad, axis=0), aff_full[...])
    g_rows = []
    for s in range(samples):
        conv_row = from_conv[s : s + 1, :]
        colour_row = grads[s][0] * summed(parts, 8 * s + 2)
        to_first = [jnp.full((1, width), crossover[s], jnp.int32) > j for j in range(2)]
        g_rows.append(
            jnp.where(to_first[0], conv_row, 0.0) + jnp.where(to_first[1], colour_row, 0.0)
        )
        g_rows.append(
            jnp.where(to_first[0], 0.0, conv_row) + jnp.where(to_first[1], 0.0, colour_row)
        )
    g_rows.append(jnp.zeros((8 - latents, width), F32))
    g_hidden = jnp.concatenate(g_rows, axis=0)
    for layer in reversed(range(layers)):
        g_pre = g_hidden * silu_slope(pre[layer])
        pack[pl.ds(layer * latents, latents), :] = g_pre[0:latents]
        pack[pl.ds((layers + layer) * latents, latents), :] = hid[layer][0:latents]
        if layer > 0:
            g_hidden = back(g_pre, map_full[layer])


def update_kernel(n_dp, samples, layers, where, *refs):
    packs, refs = refs[:n_dp], refs[n_dp:]
    (map_w, map_m, map_e, aff_w, aff_m, aff_e) = refs[:6]
    (map_b, map_bm, map_be, bias, bias_m, bias_e, rgb, rgb_m, rgb_e, w_avg) = refs[6:16]
    outs, scratch = refs[16:-7], refs[-7:]
    map_outs, aff_outs = outs[0:4], outs[4:8]
    map_b_outs, bias_outs, rgb_outs = outs[8:12], outs[12:16], outs[16:20]
    w_avg_out, loss_out, count_out = outs[20:23]
    g_pre, hid, picked, style, rgb_all, sums, w_sums = scratch
    latents = 2 * samples
    every = n_dp * latents
    dp = where[0]
    step = pl.program_id(0)
    base = 2 * layers * latents
    share = map_w.shape[1]
    width = map_w.shape[2]

    @pl.when(step == 0)
    def _():
        for k in range(n_dp):
            owner = lax.bitwise_xor(dp, k)
            for layer in range(layers):
                for n in range(latents):
                    at = owner * latents + n
                    g_pre[layer, pl.ds(at, 1), :] = packs[k][pl.ds(layer * latents + n, 1), :]
                    hid[layer, pl.ds(at, 1), :] = packs[k][
                        pl.ds((layers + layer) * latents + n, 1), :
                    ]
            for s in range(samples):
                at = owner * samples + s
                line = base + latents + 2 * s
                for j in range(2):
                    picked[j, pl.ds(at, 1), :] = packs[k][pl.ds(base + 2 * s + j, 1), :]
                style[pl.ds(at, 1), :] = packs[k][pl.ds(line, 1), :]
                rgb_all[pl.ds(at, 1), :] = packs[k][pl.ds(line + 1, 1), :]
            w_sums[pl.ds(owner, 1), :] = packs[k][pl.ds(base + latents + 2 * samples, 1), :]
        sums[pl.ds(0, 1), :] = jnp.sum(style[...], axis=0, keepdims=True)
        sums[pl.ds(1, 1), :] = jnp.sum(rgb_all[...], axis=0, keepdims=True)
        total = sums[pl.ds(0, 1), :]
        count = total[:, width - LANES // 2 : width - LANES // 2 + 1]
        inverse = 1.0 / count
        for layer in range(layers):
            grad = jnp.sum(g_pre[layer], axis=0, keepdims=True) * inverse
            new = advance(
                map_b[pl.ds(layer, 1), :], map_bm[pl.ds(layer, 1), :], map_be[pl.ds(layer, 1), :], grad, 30.0
            )
            for out, value in zip(map_b_outs[:3], new[:3]):
                out[pl.ds(layer, 1), :] = value
        map_b_outs[3][...] = map_b_outs[0][...].astype(BF16)
        colour = sums[pl.ds(1, 1), :]
        for c in range(3):
            row = pl.ds(c, 1)
            lane = slice(c * LANES, (c + 1) * LANES)
            new = advance(bias[row, :], bias_m[row, :], bias_e[row, :], total[:, lane] * inverse, 50.0)
            for out, value in zip(bias_outs[:3], new[:3]):
                out[row, :] = value
            new = advance(rgb[row, :], rgb_m[row, :], rgb_e[row, :], colour[:, lane] * inverse, 1.0)
            for out, value in zip(rgb_outs[:3], new[:3]):
                out[row, :] = value
        bias_outs[3][...] = bias_outs[0][...].astype(BF16)
        rgb_outs[3][...] = rgb_outs[0][...].astype(BF16)
        mean = jnp.sum(w_sums[...], axis=0, keepdims=True) * (1.0 / every)
        w_avg_out[...] = w_avg[...] + (1.0 - AVERAGE_BETA) * (mean - w_avg[...])
        loss_out[0] = jnp.sum(total[:, width - LANES : width - LANES + 1])
        count_out[0] = jnp.sum(count)

    count = sums[pl.ds(0, 1), pl.ds(width - LANES, LANES)][:, LANES // 2 : LANES // 2 + 1]
    inverse = 1.0 / count
    own = pltpu.roll(hid[step], lax.rem(width - dp * share, width), 1)[:, :LANES]
    own = jnp.concatenate([own] * 3, axis=0).astype(BF16)
    split = jnp.concatenate([p.astype(F32) for p in pieces(g_pre[step], 3)], axis=0).astype(BF16)
    grad = dot_tn(own, split)[0:share] * inverse
    new = advance(map_w[0], map_m[0], map_e[0], grad, 30.0)
    for out, value in zip(map_outs, new):
        out[0] = value
    depth = aff_w.shape[0]
    per = width // depth
    j = step // per
    start = pl.multiple_of(lax.rem(step, per) * depth, depth)
    chosen = picked[j, :, pl.ds(start, depth)]
    chosen = jnp.concatenate([chosen] * 3, axis=0)
    grad_style = style[:, pl.ds(pl.multiple_of(j * LANES, LANES), LANES)]
    split = jnp.concatenate([p.astype(F32) for p in pieces(grad_style, 3)], axis=0)
    fill = -chosen.shape[0] % 16
    if fill:
        chosen = jnp.concatenate([chosen, jnp.zeros((fill, depth), F32)], axis=0)
        split = jnp.concatenate([split, jnp.zeros((fill, LANES), F32)], axis=0)
    grad = dot_tn(chosen.astype(BF16), split.astype(BF16)) * inverse
    new = advance(aff_w[...], aff_m[...], aff_e[...], grad, 30.0)
    for out, value in zip(aff_outs, new):
        out[...] = value


def conv_kernel(where, mine_a, mine_b, other_a, other_b, param, moment, average, *outs):
    outs, grad = outs[:4], outs[4]
    pair = lax.rem(where[0], 2)
    rows = mine_a.shape[0]
    half = 2 * rows - COUNT_ROWS
    step = pl.program_id(0)

    @pl.when(step == 0)
    def _():
        for first, second, owner in ((mine_a, mine_b, pair), (other_a, other_b, 1 - pair)):
            at = owner * half
            grad[pl.ds(pl.multiple_of(at, 16), rows), :] = first[...]
            grad[pl.ds(pl.multiple_of(at + rows, 16), rows - COUNT_ROWS), :] = second[
                pl.ds(0, rows - COUNT_ROWS), :
            ]

    inverse = 1.0 / mine_b[pl.ds(rows - COUNT_ROWS, 16), :].astype(F32)[0:1]
    depth = param.shape[0]
    at = pl.multiple_of(step * depth, depth)
    value = grad[pl.ds(at, depth), :].astype(F32) * inverse
    new = advance(param[...], moment[...], average[...], value, 5.0)
    for out, item in zip(outs, new):
        out[...] = item


def local(
    features,
    z_table,
    seeds,
    crossover,
    counted,
    head,
    w_avg,
    map_w,
    map_w_mom,
    map_w_ema,
    map_b,
    map_b_mom,
    map_b_ema,
    aff_w,
    aff_w_mom,
    aff_w_ema,
    chan_bias,
    chan_bias_mom,
    chan_bias_ema,
    conv_w,
    conv_w_mom,
    conv_w_ema,
    rgb_w,
    rgb_w_mom,
    rgb_w_ema,
):
    samples, side = features.shape[0], features.shape[1]
    pixels = side * side
    layers, share, width = map_w.shape
    n_dp, n_ch = lax.axis_size("dp"), lax.axis_size("chan")
    latents = 2 * samples
    where = jnp.stack([lax.axis_index("dp"), lax.axis_index("chan")]).astype(jnp.int32)
    flat = lambda a: a.reshape(TAPS * width, LANES)

    half = width // 2
    map_low, aff_part = pl.pallas_call(
        prepare_kernel,
        out_shape=(shape(map_w.shape, BF16), shape((half + 16, LANES), BF16)),
        in_specs=[SMEM, VMEM, VMEM, VMEM],
        out_specs=(VMEM, VMEM),
        compiler_params=params(32),
        name="prepare",
    )(where, map_w, aff_w, chan_bias)
    aff_own = spread_direct(aff_part, "chan")
    map_parts = spread(map_low, "dp")
    feat_parts = spread_direct(features.reshape(samples, pixels, LANES), "chan")
    aff_pair = [swap(part, "dp", 1) for part in aff_own]
    head_t = jnp.pad(head.T, ((0, 0), (0, LANES - 3)))

    main_out = (
        shape((samples, TAPS * width, LANES), BF16),
        shape((8 * samples, width), F32),
        shape((layers, 8, width), F32),
        shape((layers, 8, width), F32),
        shape((8, width), F32),
        shape((2, 8, width), F32),
        shape((8 * samples, LANES), F32),
        shape((layers, width, width), BF16),
        shape((width, width), BF16),
    )
    unit, to_sum, pre, hid, top, picked, small, map_full, aff_full = pl.pallas_call(
        functools.partial(main_kernel, n_dp, n_ch, samples, side),
        out_shape=main_out,
        in_specs=[SMEM] * 3 + [HBM] * (n_dp + 3 * n_ch + 2) + [VMEM] * 6,
        out_specs=(VMEM,) * 7 + (HBM,) * 2,
        scratch_shapes=[
            pltpu.VMEM((layers, width, width), BF16),
            pltpu.VMEM((width, width), BF16),
            pltpu.VMEM((16, width), BF16),
            pltpu.VMEM((samples, pixels, width), BF16),
            pltpu.VMEM((samples, width, pixels), BF16),
            pltpu.VMEM((TAPS, width, LANES), F32),
            pltpu.VMEM((3, width, 3 * LANES), BF16),
            pltpu.VMEM((pixels + 2 * side, width), BF16),
            pltpu.VMEM((pixels + 16, 3 * LANES), F32),
            pltpu.VMEM((pixels, TAPS * LANES), BF16),
            pltpu.VMEM((pixels + 16, LANES), F32),
            pltpu.VMEM((latents, 8, width), F32),
            pltpu.SemaphoreType.DMA((n_dp,)),
            pltpu.SemaphoreType.DMA((n_ch,)),
            pltpu.SemaphoreType.DMA((3 * n_ch,)),
            pltpu.SemaphoreType.DMA((latents,)),
            pltpu.SemaphoreType.DMA,
            pltpu.SemaphoreType.DMA((2,)),
        ],
        compiler_params=params(52),
        name="main",
    )(
        where,
        seeds.reshape(-1),
        crossover,
        *map_parts,
        *feat_parts,
        *aff_own,
        *aff_pair,
        z_table,
        conv_w.reshape(TAPS, width, LANES),
        aff_w,
        map_b,
        chan_bias,
        head,
        head_t,
        rgb_w,
    )

    sum_parts = spread_direct(to_sum, "chan")
    half_rows = TAPS * width // 2 + COUNT_ROWS
    kept, sent = pl.pallas_call(
        functools.partial(scale_kernel, n_ch, samples),
        out_shape=(shape((half_rows, LANES), BF16),) * 2,
        in_specs=[SMEM] * 2 + [VMEM] * (n_ch + 1),
        out_specs=(VMEM, VMEM),
        compiler_params=params(32),
        name="scale",
    )(where, counted, *sum_parts, unit)

    got = swap(sent, "dp", 1)
    total = (kept.astype(F32) + got.astype(F32)).astype(BF16)
    quarter = half_rows // 2
    quarters = [total[:quarter], total[quarter:]]
    bits = [1 << b for b in range(1, n_dp.bit_length() - 1)]
    orders = [bits, bits[::-1]]
    for turn in range(len(bits)):
        got = [swap(quarters[q], "dp", orders[q][turn]) for q in range(2)]
        quarters = [
            (quarters[q].astype(F32) + got[q].astype(F32)).astype(BF16) for q in range(2)
        ]
    others = [swap(quarter_sum, "dp", 1) for quarter_sum in quarters]

    lines = 2 * layers * latents + latents + 2 * samples + 1
    lines = -(-lines // 8) * 8
    pack = pl.pallas_call(
        functools.partial(mapping_kernel, n_ch, samples),
        out_shape=shape((lines, width), F32),
        in_specs=[SMEM] * 3 + [VMEM] * (n_ch + 7),
        out_specs=VMEM,
        scratch_shapes=[pltpu.VMEM((8, width), F32)],
        compiler_params=params(32),
        name="mapping_back",
    )(where, counted, crossover, *sum_parts, pre, hid, top, picked, small, map_full, aff_full)
    packs = spread(pack, "dp")

    whole = lambda a: pl.BlockSpec(a.shape, lambda i: (0,) * len(a.shape))
    map_spec = pl.BlockSpec((1, share, width), lambda i: (i, 0, 0))
    aff_rows = 2 * width // layers
    aff_spec = pl.BlockSpec((aff_rows, LANES), lambda i: (i, 0))
    flat_aff = [a.reshape(2 * width, LANES) for a in (aff_w, aff_w_mom, aff_w_ema)]
    tiny = [
        map_b,
        map_b_mom,
        map_b_ema,
        chan_bias,
        chan_bias_mom,
        chan_bias_ema,
        rgb_w,
        rgb_w_mom,
        rgb_w_ema,
        w_avg.reshape(1, width),
    ]
    types = (F32, F32, F32, BF16)
    out_shape = (
        [shape(map_w.shape, t) for t in types]
        + [shape((2 * width, LANES), t) for t in types]
        + [shape(map_b.shape, t) for t in types]
        + [shape(chan_bias.shape, t) for t in types]
        + [shape(rgb_w.shape, t) for t in types]
        + [shape((1, width), F32), shape((1,), F32), shape((1,), F32)]
    )
    every = n_dp * latents
    outs = pl.pallas_call(
        functools.partial(update_kernel, n_dp, samples, layers),
        grid=(layers,),
        out_shape=out_shape,
        in_specs=[SMEM]
        + [whole(p) for p in packs]
        + [map_spec] * 3
        + [aff_spec] * 3
        + [whole(a) for a in tiny],
        out_specs=[map_spec] * 4
        + [aff_spec] * 4
        + [whole(s) for s in out_shape[8:21]]
        + [SMEM, SMEM],
        scratch_shapes=[
            pltpu.VMEM((layers, every, width), F32),
            pltpu.VMEM((layers, every, width), F32),
            pltpu.VMEM((2, n_dp * samples, width), F32),
            pltpu.VMEM((n_dp * samples, width), F32),
            pltpu.VMEM((n_dp * samples, width), F32),
            pltpu.VMEM((8, width), F32),
            pltpu.VMEM((n_dp, width), F32),
        ],
        compiler_params=params(48),
        name="update",
    )(where, *packs, map_w, map_w_mom, map_w_ema, *flat_aff, *tiny)

    conv_spec = pl.BlockSpec((width, LANES), lambda i: (i, 0))
    conv_outs = pl.pallas_call(
        conv_kernel,
        grid=(TAPS,),
        out_shape=[shape((TAPS * width, LANES), t) for t in types],
        in_specs=[SMEM] + [whole(quarters[0])] * 4 + [conv_spec] * 3,
        out_specs=[conv_spec] * 4,
        scratch_shapes=[pltpu.VMEM((TAPS * width, LANES), BF16)],
        compiler_params=params(32),
        name="conv_update",
    )(where, *quarters, *others, flat(conv_w), flat(conv_w_mom), flat(conv_w_ema))

    map_outs, aff_outs = outs[0:4], [a.reshape(aff_w.shape) for a in outs[4:8]]
    conv_outs = [a.reshape(conv_w.shape) for a in conv_outs]
    return (
        *map_outs,
        *outs[8:12],
        *aff_outs,
        *outs[12:16],
        *conv_outs,
        *outs[16:20],
        outs[20].reshape(width),
        outs[21].reshape(()),
        outs[22].reshape(()),
    )


def solution(mesh):
    in_specs = (
        P("dp", None, None, "chan"),
        P(),
        P("dp", None),
        P("dp"),
        P("dp"),
        P(),
        P(),
        P(None, "dp", None),
        P(None, "dp", None),
        P(None, "dp", None),
        P(),
        P(),
        P(),
        P(None, None, "chan"),
        P(None, None, "chan"),
        P(None, None, "chan"),
        P(None, "chan"),
        P(None, "chan"),
        P(None, "chan"),
        P(None, None, None, "chan"),
        P(None, None, None, "chan"),
        P(None, None, None, "chan"),
        P(None, "chan"),
        P(None, "chan"),
        P(None, "chan"),
    )
    out_specs = (
        P(None, "dp", None),
        P(None, "dp", None),
        P(None, "dp", None),
        P(None, "dp", None),
        P(),
        P(),
        P(),
        P(),
        P(None, None, "chan"),
        P(None, None, "chan"),
        P(None, None, "chan"),
        P(None, None, "chan"),
        P(None, "chan"),
        P(None, "chan"),
        P(None, "chan"),
        P(None, "chan"),
        P(None, None, None, "chan"),
        P(None, None, None, "chan"),
        P(None, None, None, "chan"),
        P(None, None, None, "chan"),
        P(None, "chan"),
        P(None, "chan"),
        P(None, "chan"),
        P(None, "chan"),
        P(),
        P(),
        P(),
    )
    return jax.shard_map(local, mesh=mesh, in_specs=in_specs, out_specs=out_specs, check_vma=False)
```

```python
import functools

import jax
import jax.numpy as jnp
from jax import lax
from jax.experimental import pallas as pl
from jax.experimental.pallas import tpu as pltpu
from jax.sharding import PartitionSpec as P

MOMENTUM = 0.9
EMA_DECAY = 0.95
AVERAGE_BETA = 0.5
BF16 = jnp.bfloat16
F32 = jnp.float32
TAPS = 9
LANES = 128
COUNT_ROWS = 32
VMEM = pl.BlockSpec(memory_space=pltpu.VMEM)
SMEM = pl.BlockSpec(memory_space=pltpu.SMEM)
ANY = pl.BlockSpec(memory_space=pl.ANY)


def shape(dims, dtype):
    return jax.ShapeDtypeStruct(dims, dtype)


def params(mib):
    return pltpu.CompilerParams(vmem_limit_bytes=mib * 1024 * 1024)


def cost(micros):
    return pl.CostEstimate(flops=0, bytes_accessed=int(micros * 3.5e6), transcendentals=0)


def hbm(*values):
    return [pltpu.with_memory_space_constraint(value, pltpu.HBM) for value in values]


def after(values, *others):
    return lax.optimization_barrier((values, others))[0]


def swap(value, axis, distance):
    return lax.ppermute(
        value, axis, [(i, i ^ distance) for i in range(lax.axis_size(axis))]
    )


def spread(value, axis):
    size = lax.axis_size(axis)
    beside = swap(value, axis, 1)
    if size != 8:
        parts = [(value, [(0, 0)]), (beside, [(1, 1)])]
        for k in range(2, size, 2):
            part = swap(value, axis, k)
            parts += [(part, [(k, k)]), (swap(part, axis, 1), [(k + 1, k + 1)])]
        return parts
    near = jnp.concatenate([value, beside])
    far = crossed(near, axis, 2, 4)
    corner = crossed(far, axis, 4, 2)
    return [
        (near, [(0, 0), (1, 1)]),
        (far, [(2, 4), (3, 5)]),
        (corner, [(6, 6), (7, 7)]),
        (swap(far, axis, 1), [(5, 3), (4, 2)]),
    ]


def spread_direct(value, axis):
    return [value] + [swap(value, axis, k) for k in range(1, lax.axis_size(axis))]


def crossed(value, axis, even_distance, odd_distance):
    size = lax.axis_size(axis)
    pairs = [(i, i ^ (odd_distance if i % 2 else even_distance)) for i in range(size)]
    return lax.ppermute(value, axis, pairs)


def spread_layers(value, axis, others):
    size, layers = lax.axis_size(axis), value.shape[0]
    beside = swap(value, axis, 1)
    if size != 8:
        far = [swap(value, axis, k) for k in range(2, size, 2)]
        parts = [(value, [(0, 0, 0)]), (beside, [(0, 1, 1)])]
        for k, part in zip(range(2, size, 2), far):
            parts.append((part, [(0, k, k)]))
            parts.append((swap(part, axis, 1), [(0, k + 1, k + 1)]))
        return parts
    far = crossed(jnp.concatenate([value, beside]), axis, 2, 4)
    half = layers // 2
    low, high = (crossed(far[at : at + half], axis, 4, 2) for at in (0, half))
    far_low = after(far, others[0])
    low, high = after([low, high], *others[1:])
    return [
        (value, [(0, 0, 0)]),
        (beside, [(0, 1, 1)]),
        (far, [(0, 2, 4), (0, 3, 5)]),
        (low, [(0, 6, 6)]),
        (high, [(half, 6, 6)]),
        (swap(far_low, axis, 1), [(0, 5, 3), (0, 4, 2)]),
        (swap(low, axis, 1), [(0, 7, 7)]),
        (swap(high, axis, 1), [(half, 7, 7)]),
    ]


def silu_slope(preact):
    sig = jax.nn.sigmoid(preact)
    return sig * (1.0 + preact * (1.0 - sig))


def pieces(value, count):
    out = []
    for _ in range(count):
        part = value.astype(BF16)
        out.append(part)
        value = value - part.astype(F32)
    return out


def advance(param, moment, average, grad, rate):
    moment_new = MOMENTUM * moment + grad
    param_new = param - rate * (grad + MOMENTUM * moment_new)
    average_new = EMA_DECAY * average + (1.0 - EMA_DECAY) * param_new
    return param_new, moment_new, average_new, param_new.astype(BF16)


def dot(a, b):
    return jnp.dot(a, b, preferred_element_type=F32)


def dot_nt(a, b):
    return lax.dot_general(a, b, (((1,), (1,)), ((), ())), preferred_element_type=F32)


def dot_tn(a, b):
    return lax.dot_general(a, b, (((0,), (0,)), ((), ())), preferred_element_type=F32)


def prepare_kernel(where, map_w, aff_w, bias, features, map_low, pack, stage, aff_stage, bias_stage, sems):
    layers = map_w.shape[0]
    half = aff_stage.shape[0]
    rows = features.shape[0]
    start = pl.multiple_of(lax.rem(where[0], 2) * half, half)
    copies = [
        pltpu.make_async_copy(map_w.at[layer], stage.at[layer], sems.at[layer])
        for layer in range(layers)
    ]
    aff_copy = pltpu.make_async_copy(aff_w.at[0, pl.ds(start, half), :], aff_stage, sems.at[layers])
    bias_copy = pltpu.make_async_copy(bias, bias_stage, sems.at[layers + 1])
    feat_copy = pltpu.make_async_copy(features, pack.at[pl.ds(0, rows), :], sems.at[layers + 2])
    for copy in copies + [aff_copy, bias_copy, feat_copy]:
        copy.start()
    for layer in range(layers):
        copies[layer].wait()
        map_low[layer] = stage[layer].astype(BF16)
    aff_copy.wait()
    pack[pl.ds(rows, half), :] = aff_stage[...].astype(BF16)
    bias_copy.wait()
    hi, mid, lo = pieces(bias_stage[0:1, :], 3)
    lines = jnp.concatenate(
        [hi.astype(F32), mid.astype(F32), lo.astype(F32), jnp.zeros((13, LANES), F32)], axis=0
    )
    pack[pl.ds(rows + half, 16), :] = lines.astype(BF16)
    feat_copy.wait()


def mapping_kernel(n_dp, samples, places, *refs):
    refs = list(refs)

    def take(count):
        got = refs[:count]
        del refs[:count]
        return got

    where, seeds, crossover = take(3)
    parts = take(len(places))
    z_table, map_b = take(2)
    pre_out, hid_out, top_out, picked_out, map_out = take(5)
    map_full, rows, sem_map, sem_z, sem_out = refs
    layers, share, width = parts[0].shape
    latents = 2 * samples
    dp = where[0]
    z_copies = []
    for n in range(latents):
        at = pl.multiple_of((seeds[n] // 8) * 8, 8)
        z_copies.append(pltpu.make_async_copy(z_table.at[pl.ds(at, 8), :], rows.at[n], sem_z.at[n]))
    map_copies = []
    odd = lax.rem(dp, 2)
    for part, place in zip(parts, places):
        depth = part.shape[0] // len(place)
        for i, (first, even_k, odd_k) in enumerate(place):
            k = jnp.where(odd == 1, odd_k, even_k)
            at = pl.multiple_of(lax.bitwise_xor(dp, k) * share, share)
            map_copies.append(
                pltpu.make_async_copy(
                    part.at[pl.ds(i * depth, depth)],
                    map_full.at[pl.ds(first, depth), pl.ds(at, share), :],
                    sem_map.at[len(map_copies)],
                )
            )
    for copy in z_copies + map_copies:
        copy.start()
    hidden_rows = []
    for n in range(latents):
        z_copies[n].wait()
        row = rows[n, pl.ds(lax.rem(seeds[n], 8), 1), :]
        scale = lax.rsqrt(jnp.mean(row * row, axis=1, keepdims=True) + 1e-08)
        hidden_rows.append(row * scale)
    hidden_rows.append(jnp.zeros((16 - latents, width), F32))
    hidden = jnp.concatenate(hidden_rows, axis=0)
    for copy in map_copies:
        copy.wait()
    keep_map = pltpu.make_async_copy(map_full, map_out, sem_out)
    keep_map.start()
    for layer in range(layers):
        low = hidden.astype(BF16)
        preact = dot(low, map_full[layer]) + map_b[pl.ds(layer, 1), :]
        hid_out[layer] = low.astype(F32)[0:8]
        pre_out[layer] = preact[0:8]
        hidden = preact * jax.nn.sigmoid(preact)
    top_out[...] = hidden[0:8]
    low = hidden.astype(BF16).astype(F32)
    for j in range(2):
        chosen = []
        for s in range(samples):
            first = crossover[s] > j
            chosen.append(
                jnp.where(first, low[2 * s : 2 * s + 1, :], low[2 * s + 1 : 2 * s + 2, :])
            )
        chosen.append(jnp.zeros((8 - samples, width), F32))
        picked_out[j] = jnp.concatenate(chosen, axis=0)
    keep_map.wait()


def main_kernel(n_ch, samples, side, *refs):
    refs = list(refs)

    def take(count):
        got = refs[:count]
        del refs[:count]
        return got

    (where,) = take(1)
    packs = take(n_ch)[::-1]
    pair_packs = take(n_ch)
    (conv_w,) = take(1)
    aff_w, picked, bias, head, rgb_w = take(5)
    unit, to_sum, small, aff_out = take(4)
    (
        aff_full,
        bias_full,
        feat,
        feat_t,
        kernel_f,
        kernel,
        padded,
        taps,
        shifted,
        wide,
        sem_feat,
        sem_aff,
        sem_conv,
        sem_out,
    ) = refs
    width = aff_full.shape[0]
    pixels = side * side
    half = width // 2
    dp, ch = where[0], where[1]
    pair = lax.rem(dp, 2)
    mine = pl.ds(pl.multiple_of(pair * half, half), half)
    other = pl.ds(pl.multiple_of((1 - pair) * half, half), half)

    def arrivals(source, beside, k):
        lane = pl.ds(pl.multiple_of(lax.bitwise_xor(ch, k) * LANES, LANES), LANES)
        copies = [
            pltpu.make_async_copy(
                source.at[pl.ds(s * pixels, pixels), :], feat.at[s, :, lane], sem_feat.at[samples * k + s]
            )
            for s in range(samples)
        ]
        at = samples * pixels
        copies.append(
            pltpu.make_async_copy(
                source.at[pl.ds(at, half), :], aff_full.at[mine, lane], sem_aff.at[3 * k]
            )
        )
        copies.append(
            pltpu.make_async_copy(
                source.at[pl.ds(at + half, 16), :], bias_full.at[:, lane], sem_aff.at[3 * k + 1]
            )
        )
        copies.append(
            pltpu.make_async_copy(
                beside.at[pl.ds(at, half), :], aff_full.at[other, lane], sem_aff.at[3 * k + 2]
            )
        )
        return copies

    conv_copies = [
        pltpu.make_async_copy(conv_w.at[tap], kernel_f.at[tap], sem_conv.at[tap]) for tap in range(TAPS)
    ]
    copies = [copy for k in range(n_ch) for copy in arrivals(packs[k], pair_packs[k], k)]
    for copy in copies + conv_copies:
        copy.start()
    square = jnp.zeros((width, LANES), F32)
    for tap in range(TAPS):
        conv_copies[tap].wait()
        tap_low = kernel_f[tap].astype(BF16)
        kernel[tap // 3, :, pl.ds((tap % 3) * LANES, LANES)] = tap_low
        wide_tap = tap_low.astype(F32)
        square = square + wide_tap * wide_tap
    for copy in copies:
        copy.wait()
    keep_aff = pltpu.make_async_copy(aff_full, aff_out, sem_out)
    keep_aff.start()
    for s in range(samples):
        feat_t[s] = feat[s].T
    wide_bias = bias_full[...].astype(F32)
    bias_row = wide_bias[0:1] + wide_bias[1:2] + wide_bias[2:3]
    style0 = (dot(picked[0].astype(BF16), aff_full[...]) + bias_row).astype(BF16)
    colour_aff = aff_w[1].astype(BF16)
    style1 = dot(picked[1].astype(BF16), colour_aff) + bias[1:2, :]
    style0_wide = style0.astype(F32)
    style1 = style1.astype(BF16).astype(F32)
    colour_aff = colour_aff.astype(F32)
    colour = rgb_w[...].astype(BF16)
    colour_wide = colour.astype(F32)
    colour_rows = jnp.concatenate([colour_wide, jnp.zeros((13, LANES), F32)], axis=0).astype(BF16)
    head_rows = jnp.concatenate(
        [head[...].astype(F32), jnp.zeros((13, pixels), F32)], axis=0
    ).astype(BF16)
    conv_bias = bias[2:3, :]
    chunk = min(256, pixels)
    steps = pixels // chunk
    column = lax.rem(lax.broadcasted_iota(jnp.int32, (chunk, LANES), 0), side)
    not_first, not_last = column > 0, column < side - 1
    small[...] = jnp.zeros_like(small)
    to_sum[...] = jnp.zeros_like(to_sum)
    padded[pl.ds(0, side), :] = jnp.zeros((side, width), BF16)
    padded[pl.ds(side + pixels, side), :] = jnp.zeros((side, width), BF16)
    taps[pl.ds(0, 8), :] = jnp.zeros((8, 3 * LANES), F32)
    taps[pl.ds(8 + pixels, 8), :] = jnp.zeros((8, 3 * LANES), F32)
    wide[pl.ds(0, 8), :] = jnp.zeros((8, LANES), F32)
    wide[pl.ds(8 + pixels, 8), :] = jnp.zeros((8, LANES), F32)

    for s in range(samples):
        style_row = style0[s : s + 1, :]
        for r in range(steps):
            padded[pl.ds(side + r * chunk, chunk), :] = feat[s, pl.ds(r * chunk, chunk), :] * style_row
        style_col = jnp.broadcast_to(style0_wide[s : s + 1, :], (LANES, width)).T
        demod = lax.rsqrt(
            jnp.sum(style_col * style_col * square, axis=0, keepdims=True) + 1e-08
        )
        style_colour = style1[s : s + 1, :]
        for r in range(steps):
            total = dot(padded[pl.ds(r * chunk, chunk), :], kernel[0])
            total = total + dot(padded[pl.ds(side + r * chunk, chunk), :], kernel[1])
            total = total + dot(padded[pl.ds(2 * side + r * chunk, chunk), :], kernel[2])
            taps[pl.ds(8 + r * chunk, chunk), :] = total
        mixed = jnp.zeros((3, LANES), F32)
        g_style1 = jnp.zeros((1, LANES), F32)
        g_bias = jnp.zeros((1, LANES), F32)
        g_demod = jnp.zeros((1, LANES), F32)
        for r in range(steps):
            left = taps[pl.ds(7 + r * chunk, chunk), pl.ds(0, LANES)]
            centre = taps[pl.ds(8 + r * chunk, chunk), pl.ds(LANES, LANES)]
            right = taps[pl.ds(9 + r * chunk, chunk), pl.ds(2 * LANES, LANES)]
            conv_out = centre + jnp.where(not_first, left, 0.0) + jnp.where(not_last, right, 0.0)
            scaled = conv_out * demod + conv_bias
            sig = jax.nn.sigmoid(scaled)
            activated = scaled * sig
            act_mod = (activated * style_colour).astype(BF16)
            mixed = mixed + dot(head_rows[:, r * chunk : (r + 1) * chunk], act_mod)[0:3]
            g_act = dot_tn(head_rows[:, r * chunk : (r + 1) * chunk], colour_rows)
            g_style1 = g_style1 + jnp.sum(g_act * activated, axis=0, keepdims=True)
            g_scaled = g_act * style_colour * (sig * (1.0 + scaled * (1.0 - sig)))
            g_bias = g_bias + jnp.sum(g_scaled, axis=0, keepdims=True)
            g_demod = g_demod + jnp.sum(g_scaled * conv_out, axis=0, keepdims=True)
            wide[pl.ds(8 + r * chunk, chunk), :] = g_scaled * demod
        for r in range(steps):
            before = jnp.where(not_last, wide[pl.ds(9 + r * chunk, chunk), :], 0.0)
            centre = wide[pl.ds(8 + r * chunk, chunk), :]
            after = jnp.where(not_first, wide[pl.ds(7 + r * chunk, chunk), :], 0.0)
            for dx, value in enumerate((before, centre, after)):
                value = value.astype(BF16)
                for dy in range(3):
                    lane = pl.ds((3 * dy + dx) * LANES, LANES)
                    start = r * chunk + (dy - 1) * side
                    low_at, high_at = max(start, 0), min(start + chunk, pixels)
                    shifted[pl.ds(low_at, high_at - low_at), lane] = value[
                        low_at - start : high_at - start, :
                    ]
        for dx in range(3):
            shifted[pl.ds(pixels - side, side), pl.ds(dx * LANES, LANES)] = jnp.zeros(
                (side, LANES), BF16
            )
            shifted[pl.ds(0, side), pl.ds((6 + dx) * LANES, LANES)] = jnp.zeros(
                (side, LANES), BF16
            )
        factor = g_demod * demod * demod * demod
        g_style = jnp.zeros((width, LANES), F32)
        for first in range(0, TAPS, 2):
            count = min(2, TAPS - first)
            block = dot(feat_t[s], shifted[:, pl.ds(first * LANES, count * LANES)])
            for tap in range(first, first + count):
                raw = block[:, (tap - first) * LANES : (tap - first + 1) * LANES]
                weight = kernel[tap // 3, :, pl.ds((tap % 3) * LANES, LANES)].astype(F32)
                inner = raw - style_col * (weight * factor)
                g_style = g_style + weight * inner
                unit[s, pl.ds(tap * width, width), :] = (style_col * inner).astype(BF16)
        g_style_row = jnp.sum(g_style.T, axis=0, keepdims=True)
        g_colour_row = jnp.sum((colour_aff * g_style1).T, axis=0, keepdims=True)
        logit = jnp.sum(
            jnp.sum(mixed * colour_wide, axis=0, keepdims=True), axis=1, keepdims=True
        )
        to_sum[pl.ds(8 * s, 1), :] = jnp.broadcast_to(logit, (1, width))
        to_sum[pl.ds(8 * s + 1, 1), :] = g_style_row
        to_sum[pl.ds(8 * s + 2, 1), :] = g_colour_row
        small[pl.ds(8 * s, 1), :] = g_style1
        small[pl.ds(8 * s + 1, 1), :] = g_bias
        small[pl.ds(8 * s + 2, 3), :] = mixed
    keep_aff.wait()


def summed(parts, row):
    values = [part[pl.ds(row, 1), :] for part in parts]
    while len(values) > 1:
        values = [values[i] + values[i + 1] for i in range(0, len(values), 2)]
    return values[0]


def logit_grad(parts, counted, s):
    logit = summed(parts, 8 * s)
    mask = jnp.full(logit.shape, counted[s], jnp.int32).astype(F32)
    return -mask * jax.nn.sigmoid(-logit), mask * jax.nn.softplus(-logit), mask


def scale_kernel(n_ch, samples, where, counted, *refs):
    parts, (unit, kept, sent) = refs[:n_ch], refs[n_ch:]
    pair = lax.rem(where[0], 2)
    half = unit.shape[1] // 2
    grads, total = [], jnp.zeros((1, LANES), F32)
    for s in range(samples):
        grad, _, mask = logit_grad(parts, counted, s)
        grads.append(grad[:, :LANES])
        total = total + mask[:, :LANES]
    block = half // 9
    for out, owner in ((kept, pair), (sent, 1 - pair)):
        for b in range(9):
            at = pl.multiple_of(owner * half + b * block, block)
            value = grads[0] * unit[0, pl.ds(at, block), :].astype(F32)
            for s in range(1, samples):
                value = value + grads[s] * unit[s, pl.ds(at, block), :].astype(F32)
            out[pl.ds(b * block, block), :] = value.astype(BF16)
        out[pl.ds(half, COUNT_ROWS), :] = jnp.broadcast_to(total, (COUNT_ROWS, LANES)).astype(BF16)


def pack_places(samples, layers):
    latents = 2 * samples
    style = 2 * layers * latents + latents
    colour = style + 2 * samples
    w_total = colour + 2 * samples
    return style, colour, w_total, -(-(w_total + 3) // 16) * 16


def mapping_back_kernel(n_ch, samples, where, counted, crossover, *refs):
    parts = refs[:n_ch]
    pre, hid, top, picked, small, map_full, aff_full, pack_out, rows, pack = refs[n_ch:]
    layers, _, width = map_full.shape
    latents = 2 * samples
    style_at, colour_at, w_at, _ = pack_places(samples, layers)
    ch = where[1]
    grads = [logit_grad(parts, counted, s) for s in range(samples)]
    pack[...] = jnp.zeros_like(pack)

    def put(line, lane, size, value, count):
        for i, part in enumerate(pieces(value, count)):
            pack[pl.ds(line + i, 1), pl.ds(lane, size)] = part.astype(F32)

    style_rows = []
    half_lane = lax.broadcasted_iota(jnp.int32, (1, LANES), 1) < LANES // 2
    for s in range(samples):
        grad = grads[s][0]
        style_row = grad * summed(parts, 8 * s + 1)
        rows[pl.ds(s, 1), :] = style_row
        style_rows.append(style_row)
        own = rows[pl.ds(s, 1), pl.ds(pl.multiple_of(ch * LANES, LANES), LANES)]
        short = grad[:, :LANES]
        put(style_at + 2 * s, 0, LANES, own, 2)
        put(style_at + 2 * s, LANES, LANES, short * small[pl.ds(8 * s, 1), :], 2)
        put(style_at + 2 * s, 2 * LANES, LANES, short * small[pl.ds(8 * s + 1, 1), :], 2)
        loss_count = jnp.where(half_lane, grads[s][1][:, :LANES], grads[s][2][:, :LANES])
        put(style_at + 2 * s, 3 * LANES, LANES, loss_count, 2)
        for c in range(3):
            value = short * small[pl.ds(8 * s + 2 + c, 1), :]
            put(colour_at + 2 * s, c * LANES, LANES, value, 2)
        for j in range(2):
            line = 2 * layers * latents + 2 * s + j
            pack[pl.ds(line, 1), :] = picked[j, pl.ds(s, 1), :]
    w_total = top[pl.ds(0, 1), :]
    for n in range(1, latents):
        w_total = w_total + top[pl.ds(n, 1), :]
    put(w_at, 0, width, w_total, 3)

    def back(value, weights):
        hi, lo = pieces(value, 2)
        both = jnp.concatenate([hi.astype(F32), lo.astype(F32)], axis=0).astype(BF16)
        out = dot_nt(both, weights)
        return out[0:8] + out[8:16]

    pad = [jnp.zeros((8 - samples, width), F32)]
    from_conv = back(jnp.concatenate(style_rows + pad, axis=0), aff_full[...])
    g_rows = []
    for s in range(samples):
        conv_row = from_conv[s : s + 1, :]
        colour_row = grads[s][0] * summed(parts, 8 * s + 2)
        to_first = [jnp.full((1, width), crossover[s], jnp.int32) > j for j in range(2)]
        g_rows.append(
            jnp.where(to_first[0], conv_row, 0.0) + jnp.where(to_first[1], colour_row, 0.0)
        )
        g_rows.append(
            jnp.where(to_first[0], 0.0, conv_row) + jnp.where(to_first[1], 0.0, colour_row)
        )
    g_rows.append(jnp.zeros((8 - latents, width), F32))
    g_hidden = jnp.concatenate(g_rows, axis=0)
    for layer in reversed(range(layers)):
        g_pre = g_hidden * silu_slope(pre[layer])
        pack[pl.ds(layer * latents, latents), :] = g_pre[0:latents]
        pack[pl.ds((layers + layer) * latents, latents), :] = hid[layer][0:latents]
        if layer > 0:
            g_hidden = back(g_pre, map_full[layer])
    pack_out[...] = pack[...].astype(BF16)


def update_kernel(n_dp, samples, layers, places, where, *refs):
    packs, refs = refs[: len(places)], refs[len(places) :]
    (map_w, map_m, map_e, aff_w, aff_m, aff_e) = refs[:6]
    (map_b, map_bm, map_be, bias, bias_m, bias_e, rgb, rgb_m, rgb_e, w_avg) = refs[6:16]
    outs, scratch = refs[16:-7], refs[-7:]
    map_outs, aff_outs = outs[0:4], outs[4:8]
    map_b_outs, bias_outs, rgb_outs = outs[8:12], outs[12:16], outs[16:20]
    w_avg_out, loss_out, count_out = outs[20:23]
    g_pre, hid, picked, style, rgb_all, sums, w_sums = scratch
    latents = 2 * samples
    style_at, colour_at, w_at, lines = pack_places(samples, layers)
    every = n_dp * latents
    dp = where[0]
    step = pl.program_id(0)
    share = map_w.shape[1]
    width = map_w.shape[2]

    @pl.when(step == 0)
    def _():
        odd = lax.rem(dp, 2)
        for part, place in zip(packs, places):
            for index, (even_k, odd_k) in enumerate(place):
                owner = lax.bitwise_xor(dp, jnp.where(odd == 1, odd_k, even_k))
                got = part[pl.ds(index * lines, lines), :].astype(F32)
                for layer in range(layers):
                    for n in range(latents):
                        at = pl.ds(owner * latents + n, 1)
                        line = layer * latents + n
                        g_pre[layer, at, :] = got[line : line + 1]
                        line += layers * latents
                        hid[layer, at, :] = got[line : line + 1]
                for s in range(samples):
                    at = pl.ds(owner * samples + s, 1)
                    line = 2 * layers * latents + 2 * s
                    for j in range(2):
                        picked[j, at, :] = got[line + j : line + j + 1]
                    line = style_at + 2 * s
                    style[at, :] = got[line : line + 1] + got[line + 1 : line + 2]
                    line = colour_at + 2 * s
                    rgb_all[at, :] = got[line : line + 1] + got[line + 1 : line + 2]
                w_sums[pl.ds(owner, 1), :] = (
                    got[w_at : w_at + 1] + got[w_at + 1 : w_at + 2] + got[w_at + 2 : w_at + 3]
                )
        sums[pl.ds(0, 1), :] = jnp.sum(style[...], axis=0, keepdims=True)
        sums[pl.ds(1, 1), :] = jnp.sum(rgb_all[...], axis=0, keepdims=True)
        total = sums[pl.ds(0, 1), :]
        count = total[:, width - LANES // 2 : width - LANES // 2 + 1]
        inverse = 1.0 / count
        for layer in range(layers):
            grad = jnp.sum(g_pre[layer], axis=0, keepdims=True) * inverse
            row = pl.ds(layer, 1)
            new = advance(map_b[row, :], map_bm[row, :], map_be[row, :], grad, 30.0)
            for out, value in zip(map_b_outs[:3], new[:3]):
                out[row, :] = value
        map_b_outs[3][...] = map_b_outs[0][...].astype(BF16)
        colour = sums[pl.ds(1, 1), :]
        for c in range(3):
            row = pl.ds(c, 1)
            lane = slice(c * LANES, (c + 1) * LANES)
            new = advance(bias[row, :], bias_m[row, :], bias_e[row, :], total[:, lane] * inverse, 50.0)
            for out, value in zip(bias_outs[:3], new[:3]):
                out[row, :] = value
            new = advance(rgb[row, :], rgb_m[row, :], rgb_e[row, :], colour[:, lane] * inverse, 1.0)
            for out, value in zip(rgb_outs[:3], new[:3]):
                out[row, :] = value
        bias_outs[3][...] = bias_outs[0][...].astype(BF16)
        rgb_outs[3][...] = rgb_outs[0][...].astype(BF16)
        mean = jnp.sum(w_sums[...], axis=0, keepdims=True) * (1.0 / every)
        w_avg_out[...] = w_avg[...] + (1.0 - AVERAGE_BETA) * (mean - w_avg[...])
        loss_out[0] = jnp.sum(total[:, width - LANES : width - LANES + 1])
        count_out[0] = jnp.sum(count)

    count = sums[pl.ds(0, 1), pl.ds(width - LANES, LANES)][:, LANES // 2 : LANES // 2 + 1]
    inverse = 1.0 / count
    each = map_outs[0].shape[0]
    for index in range(each):
        layer = step * each + index
        own = pltpu.roll(hid[layer], lax.rem(width - dp * share, width), 1)[:, :LANES]
        grad = dot_tn(own.astype(BF16), g_pre[layer].astype(BF16))[0:share] * inverse
        new = advance(map_w[layer], map_m[layer], map_e[layer], grad, 30.0)
        for out, value in zip(map_outs, new):
            out[index] = value
    chosen = jnp.concatenate([picked[step]] * 2, axis=0)
    grad_style = style[:, pl.ds(pl.multiple_of(step * LANES, LANES), LANES)]
    split = jnp.concatenate([p.astype(F32) for p in pieces(grad_style, 2)], axis=0)
    grad = dot_tn(chosen.astype(BF16), split.astype(BF16)) * inverse
    here = pl.ds(pl.multiple_of(step * width, width), width)
    new = advance(aff_w[here, :], aff_m[here, :], aff_e[here, :], grad, 30.0)
    for out, value in zip(aff_outs, new):
        out[...] = value


def conv_kernel(mine, where, grad, param, moment, average, *refs):
    refs = refs if mine else refs[4:]
    outs, buffers, sems = refs[0:4], refs[4:8], refs[8]
    half = grad.shape[0] - COUNT_ROWS
    pair = lax.rem(where[0], 2)
    start = pl.multiple_of((pair if mine else 1 - pair) * half, half)
    inverse = 1.0 / grad[pl.ds(half, 16), :].astype(F32)[0:1]
    chunks = sems.shape[0]
    depth = half // chunks
    copies = []
    for c in range(chunks):
        here = pl.ds(c * depth, depth)
        there = pl.ds(pl.multiple_of(start + c * depth, depth), depth)
        value = grad[here, :].astype(F32) * inverse
        new = advance(param[there, :], moment[there, :], average[there, :], value, 5.0)
        for k in range(4):
            buffers[k][here, :] = new[k]
            copy = pltpu.make_async_copy(buffers[k].at[here, :], outs[k].at[there, :], sems.at[c, k])
            copy.start()
            copies.append(copy)
    for copy in copies:
        copy.wait()


def local(
    features,
    z_table,
    seeds,
    crossover,
    counted,
    head,
    w_avg,
    map_w,
    map_w_mom,
    map_w_ema,
    map_b,
    map_b_mom,
    map_b_ema,
    aff_w,
    aff_w_mom,
    aff_w_ema,
    chan_bias,
    chan_bias_mom,
    chan_bias_ema,
    conv_w,
    conv_w_mom,
    conv_w_ema,
    rgb_w,
    rgb_w_mom,
    rgb_w_ema,
):
    samples, side = features.shape[0], features.shape[1]
    pixels = side * side
    layers, share, width = map_w.shape
    n_dp, n_ch = lax.axis_size("dp"), lax.axis_size("chan")
    latents = 2 * samples
    where = jnp.stack([lax.axis_index("dp"), lax.axis_index("chan")]).astype(jnp.int32)
    flat = lambda a: a.reshape(TAPS * width, LANES)

    half = width // 2
    pack_rows = samples * pixels + half + 16
    map_low, pack = pl.pallas_call(
        prepare_kernel,
        out_shape=(shape(map_w.shape, BF16), shape((pack_rows, LANES), BF16)),
        in_specs=[SMEM] + [ANY] * 4,
        out_specs=(VMEM, VMEM),
        scratch_shapes=[
            pltpu.VMEM(map_w.shape, F32),
            pltpu.VMEM((half, LANES), F32),
            pltpu.VMEM(chan_bias.shape, F32),
            pltpu.SemaphoreType.DMA((layers + 3,)),
        ],
        compiler_params=params(8),
        name="prepare",
    )(where, *hbm(map_w, aff_w, chan_bias, features.reshape(samples * pixels, LANES)))
    packs = spread_direct(pack, "chan")
    blocks = spread_layers(map_low, "dp", packs[1:])
    places = [place for _, place in blocks]

    pre, hid, top, picked, map_full = pl.pallas_call(
        functools.partial(mapping_kernel, n_dp, samples, places),
        out_shape=(
            shape((layers, 8, width), F32),
            shape((layers, 8, width), F32),
            shape((8, width), F32),
            shape((2, 8, width), F32),
            shape((layers, width, width), BF16),
        ),
        in_specs=[SMEM] * 3 + [ANY] * (len(blocks) + 1) + [VMEM],
        out_specs=(VMEM,) * 4 + (ANY,),
        scratch_shapes=[
            pltpu.VMEM((layers, width, width), BF16),
            pltpu.VMEM((latents, 8, width), F32),
            pltpu.SemaphoreType.DMA((sum(len(place) for place in places),)),
            pltpu.SemaphoreType.DMA((latents,)),
            pltpu.SemaphoreType.DMA,
        ],
        compiler_params=params(12),
        cost_estimate=cost(1),
        name="mapping",
    )(where, seeds.reshape(-1), crossover, *[block for block, _ in blocks], *hbm(z_table), map_b)

    pack_pair = [swap(part, "dp", 1) for part in packs]
    unit, to_sum, small, aff_full = pl.pallas_call(
        functools.partial(main_kernel, n_ch, samples, side),
        out_shape=(
            shape((samples, TAPS * width, LANES), BF16),
            shape((8 * samples, width), F32),
            shape((8 * samples, LANES), F32),
            shape((width, width), BF16),
        ),
        in_specs=[SMEM] + [ANY] * (2 * n_ch + 1) + [VMEM] * 5,
        out_specs=(VMEM,) * 3 + (ANY,),
        scratch_shapes=[
            pltpu.VMEM((width, width), BF16),
            pltpu.VMEM((16, width), BF16),
            pltpu.VMEM((samples, pixels, width), BF16),
            pltpu.VMEM((samples, width, pixels), BF16),
            pltpu.VMEM((TAPS, width, LANES), F32),
            pltpu.VMEM((3, width, 3 * LANES), BF16),
            pltpu.VMEM((pixels + 2 * side, width), BF16),
            pltpu.VMEM((pixels + 16, 3 * LANES), F32),
            pltpu.VMEM((pixels, TAPS * LANES), BF16),
            pltpu.VMEM((pixels + 16, LANES), F32),
            pltpu.SemaphoreType.DMA((samples * n_ch,)),
            pltpu.SemaphoreType.DMA((3 * n_ch,)),
            pltpu.SemaphoreType.DMA((TAPS,)),
            pltpu.SemaphoreType.DMA,
        ],
        compiler_params=params(28),
        cost_estimate=cost(8),
        name="main",
    )(
        where,
        *packs[::-1],
        *pack_pair,
        *hbm(conv_w.reshape(TAPS, width, LANES)),
        aff_w,
        picked,
        chan_bias,
        head,
        rgb_w,
    )

    sum_parts = spread_direct(to_sum, "chan")
    half_rows = TAPS * width // 2 + COUNT_ROWS
    kept, sent = pl.pallas_call(
        functools.partial(scale_kernel, n_ch, samples),
        out_shape=(shape((half_rows, LANES), BF16),) * 2,
        in_specs=[SMEM] * 2 + [VMEM] * (n_ch + 1),
        out_specs=(VMEM, VMEM),
        compiler_params=params(8),
        cost_estimate=cost(1),
        name="scale",
    )(where, counted, *sum_parts, unit)

    lines = pack_places(samples, layers)[-1]
    pack = pl.pallas_call(
        functools.partial(mapping_back_kernel, n_ch, samples),
        out_shape=shape((lines, width), BF16),
        in_specs=[SMEM] * 3 + [VMEM] * (n_ch + 7),
        out_specs=VMEM,
        scratch_shapes=[pltpu.VMEM((8, width), F32), pltpu.VMEM((lines, width), F32)],
        compiler_params=params(12),
        cost_estimate=cost(2),
        name="mapping_back",
    )(where, counted, crossover, *sum_parts, pre, hid, top, picked, small, map_full, aff_full)
    spread_pack = spread(pack, "dp")
    packs = [part for part, _ in spread_pack]

    whole = lambda a: pl.BlockSpec(a.shape, lambda i: (0,) * len(a.shape))
    map_spec = pl.BlockSpec((layers // 2, share, width), lambda i: (i, 0, 0))
    aff_spec = pl.BlockSpec((width, LANES), lambda i: (i, 0))
    flat_aff = [a.reshape(2 * width, LANES) for a in (aff_w, aff_w_mom, aff_w_ema)]
    tiny = [
        map_b,
        map_b_mom,
        map_b_ema,
        chan_bias,
        chan_bias_mom,
        chan_bias_ema,
        rgb_w,
        rgb_w_mom,
        rgb_w_ema,
        w_avg.reshape(1, width),
    ]
    types = (F32, F32, F32, BF16)
    out_shape = (
        [shape(map_w.shape, t) for t in types]
        + [shape((2 * width, LANES), t) for t in types]
        + [shape(map_b.shape, t) for t in types]
        + [shape(chan_bias.shape, t) for t in types]
        + [shape(rgb_w.shape, t) for t in types]
        + [shape((1, width), F32), shape((1,), F32), shape((1,), F32)]
    )
    every = n_dp * latents
    update = lambda: pl.pallas_call(
        functools.partial(update_kernel, n_dp, samples, layers, [p for _, p in spread_pack]),
        grid=(2,),
        out_shape=out_shape,
        in_specs=[SMEM]
        + [VMEM] * len(packs)
        + [VMEM] * (6 + len(tiny)),
        out_specs=[map_spec] * 4
        + [aff_spec] * 4
        + [whole(s) for s in out_shape[8:21]]
        + [SMEM, SMEM],
        scratch_shapes=[
            pltpu.VMEM((layers, every, width), F32),
            pltpu.VMEM((layers, every, width), F32),
            pltpu.VMEM((2, n_dp * samples, width), F32),
            pltpu.VMEM((n_dp * samples, width), F32),
            pltpu.VMEM((n_dp * samples, width), F32),
            pltpu.VMEM((8, width), F32),
            pltpu.VMEM((n_dp, width), F32),
        ],
        compiler_params=params(20),
        cost_estimate=cost(5),
        name="update",
    )(where, *packs, map_w, map_w_mom, map_w_ema, *flat_aff, *tiny)

    got = after(swap(sent, "dp", 1), pack)
    total = (kept.astype(F32) + got.astype(F32)).astype(BF16)
    bits = [1 << b for b in range(1, n_dp.bit_length() - 1)]
    for turn, (even_bit, odd_bit) in enumerate(zip(bits, bits[::-1])):
        got = crossed(total, "dp", even_bit, odd_bit)
        if turn == len(bits) - 2:
            got = after(got, packs[1])
        if turn == len(bits) - 1:
            outs = update()
            got = after(got, *outs)
        total = (total.astype(F32) + got.astype(F32)).astype(BF16)
    other = swap(total, "dp", 1)

    conv_params = [flat(conv_w), flat(conv_w_mom), flat(conv_w_ema)]
    half_rows = TAPS * width // 2

    def conv_half(grad, *earlier):
        return pl.pallas_call(
            functools.partial(conv_kernel, not earlier),
            out_shape=[shape((TAPS * width, LANES), t) for t in types],
            in_specs=[SMEM] + [VMEM] * 4 + [ANY] * len(earlier),
            out_specs=[ANY] * 4,
            scratch_shapes=[pltpu.VMEM((half_rows, LANES), t) for t in types]
            + [pltpu.SemaphoreType.DMA((3, 4))],
            input_output_aliases={5 + k: k for k in range(len(earlier))},
            compiler_params=params(12),
            cost_estimate=cost(2),
            name="conv_other" if earlier else "conv_own",
        )(where, grad, *conv_params, *earlier)

    conv_outs = conv_half(other, *conv_half(total))

    map_outs, aff_outs = outs[0:4], [a.reshape(aff_w.shape) for a in outs[4:8]]
    conv_outs = [a.reshape(conv_w.shape) for a in conv_outs]
    return (
        *map_outs,
        *outs[8:12],
        *aff_outs,
        *outs[12:16],
        *conv_outs,
        *outs[16:20],
        outs[20].reshape(width),
        outs[21].reshape(()),
        outs[22].reshape(()),
    )


def solution(mesh):
    in_specs = (
        P("dp", None, None, "chan"),
        P(),
        P("dp", None),
        P("dp"),
        P("dp"),
        P(),
        P(),
        P(None, "dp", None),
        P(None, "dp", None),
        P(None, "dp", None),
        P(),
        P(),
        P(),
        P(None, None, "chan"),
        P(None, None, "chan"),
        P(None, None, "chan"),
        P(None, "chan"),
        P(None, "chan"),
        P(None, "chan"),
        P(None, None, None, "chan"),
        P(None, None, None, "chan"),
        P(None, None, None, "chan"),
        P(None, "chan"),
        P(None, "chan"),
        P(None, "chan"),
    )
    out_specs = (
        P(None, "dp", None),
        P(None, "dp", None),
        P(None, "dp", None),
        P(None, "dp", None),
        P(),
        P(),
        P(),
        P(),
        P(None, None, "chan"),
        P(None, None, "chan"),
        P(None, None, "chan"),
        P(None, None, "chan"),
        P(None, "chan"),
        P(None, "chan"),
        P(None, "chan"),
        P(None, "chan"),
        P(None, None, None, "chan"),
        P(None, None, None, "chan"),
        P(None, None, None, "chan"),
        P(None, None, None, "chan"),
        P(None, "chan"),
        P(None, "chan"),
        P(None, "chan"),
        P(None, "chan"),
        P(),
        P(),
        P(),
    )
    return jax.shard_map(local, mesh=mesh, in_specs=in_specs, out_specs=out_specs, check_vma=False)
```

```python
import functools

import jax
import jax.numpy as jnp
from jax import lax
from jax.experimental import pallas as pl
from jax.experimental.pallas import tpu as pltpu
from jax.sharding import PartitionSpec as P

MOMENTUM = 0.9
EMA_DECAY = 0.95
AVERAGE_BETA = 0.5
BF16 = jnp.bfloat16
F32 = jnp.float32
TAPS = 9
LANES = 128
COUNT_ROWS = 32
VMEM = pl.BlockSpec(memory_space=pltpu.VMEM)
SMEM = pl.BlockSpec(memory_space=pltpu.SMEM)
ANY = pl.BlockSpec(memory_space=pl.ANY)


def shape(dims, dtype):
    return jax.ShapeDtypeStruct(dims, dtype)


def params(mib):
    return pltpu.CompilerParams(vmem_limit_bytes=mib * 1024 * 1024)


def cost(micros):
    return pl.CostEstimate(flops=0, bytes_accessed=int(micros * 3.5e6), transcendentals=0)


def hbm(*values):
    return [pltpu.with_memory_space_constraint(value, pltpu.HBM) for value in values]


def after(values, *others):
    return lax.optimization_barrier((values, others))[0]


def swap(value, axis, distance):
    return lax.ppermute(
        value, axis, [(i, i ^ distance) for i in range(lax.axis_size(axis))]
    )


def spread(value, axis):
    size = lax.axis_size(axis)
    beside = swap(value, axis, 1)
    if size != 8:
        parts = [(value, [(0, 0)]), (beside, [(1, 1)])]
        for k in range(2, size, 2):
            part = swap(value, axis, k)
            parts += [(part, [(k, k)]), (swap(part, axis, 1), [(k + 1, k + 1)])]
        return parts
    near = jnp.concatenate([value, beside])
    far = crossed(near, axis, 4, 2)
    corner = crossed(far, axis, 2, 4)
    return [
        (near, [(0, 0), (1, 1)]),
        (far, [(4, 2), (5, 3)]),
        (corner, [(6, 6), (7, 7)]),
        (swap(far, axis, 1), [(3, 5), (2, 4)]),
    ]


def spread_direct(value, axis):
    return [value] + [swap(value, axis, k) for k in range(1, lax.axis_size(axis))]


def spread_over_chan(pack, tail, ready):
    n_dp, n_ch = lax.axis_size("dp"), lax.axis_size("chan")
    cut = pack.shape[0] - tail
    other = swap(pack, "dp", 1)
    both = after(jnp.concatenate([pack, other[cut:], other[:cut]]), ready)

    def joint(value, moves):
        pairs = [
            (d * n_ch + a, d * n_ch + b) for d in range(n_dp) for a, b in moves[d % 2]
        ]
        return lax.ppermute(value, ("dp", "chan"), pairs)

    first = joint(both, ([(c, c ^ 1) for c in range(4)], [(c, c ^ 2) for c in range(4)]))
    first_pair = swap(first[cut:], "dp", 1)
    odd = lax.rem(lax.axis_index("dp"), 2) == 1

    def last_step(*others):
        value = after(jnp.where(odd, first, both), *others)
        return joint(value, ([(1, 2), (2, 1)], [(1, 0), (2, 3)]))

    return both, first, first_pair, last_step


def crossed(value, axis, even_distance, odd_distance):
    size = lax.axis_size(axis)
    pairs = [(i, i ^ (odd_distance if i % 2 else even_distance)) for i in range(size)]
    return lax.ppermute(value, axis, pairs)


def spread_layers(value, axis):
    size = lax.axis_size(axis)
    beside = swap(value, axis, 1)
    parts = [(value, (0, 0, 0)), (beside, (0, 1, 1))]
    if size != 8:
        for k in range(2, size, 2):
            part = swap(value, axis, k)
            parts += [(part, (0, k, k)), (swap(part, axis, 1), (0, k + 1, k + 1))]
        return parts
    far = crossed(value, axis, 2, 4)
    far_beside = crossed(beside, axis, 2, 4)
    corner = crossed(far, axis, 4, 2)
    parts += [(far, (0, 2, 4)), (far_beside, (0, 3, 5)), (corner, (0, 6, 6))]
    parts += [(swap(far, axis, 1), (0, 5, 3)), (swap(far_beside, axis, 1), (0, 4, 2))]
    parts += [(swap(corner, axis, 1), (0, 7, 7))]
    return parts


def silu_slope(preact):
    sig = jax.nn.sigmoid(preact)
    return sig * (1.0 + preact * (1.0 - sig))


def pieces(value, count):
    out = []
    for _ in range(count):
        part = value.astype(BF16)
        out.append(part)
        value = value - part.astype(F32)
    return out


def advance(param, moment, average, grad, rate):
    moment_new = MOMENTUM * moment + grad
    param_new = param - rate * (grad + MOMENTUM * moment_new)
    average_new = EMA_DECAY * average + (1.0 - EMA_DECAY) * param_new
    return param_new, moment_new, average_new, param_new.astype(BF16)


def dot(a, b):
    return jnp.dot(a, b, preferred_element_type=F32)


def dot_nt(a, b):
    return lax.dot_general(a, b, (((1,), (1,)), ((), ())), preferred_element_type=F32)


def dot_tn(a, b):
    return lax.dot_general(a, b, (((0,), (0,)), ((), ())), preferred_element_type=F32)


def pack_kernel(where, aff_w, bias, features, pack, aff_stage, bias_stage, sems):
    half = aff_stage.shape[0]
    rows = features.shape[0]
    start = pl.multiple_of(lax.rem(where[0], 2) * half, half)
    feat_copy = pltpu.make_async_copy(features, pack.at[pl.ds(0, rows), :], sems.at[0])
    aff_copy = pltpu.make_async_copy(aff_w.at[0, pl.ds(start, half), :], aff_stage, sems.at[1])
    bias_copy = pltpu.make_async_copy(bias, bias_stage, sems.at[2])
    for copy in (feat_copy, aff_copy, bias_copy):
        copy.start()
    bias_copy.wait()
    hi, mid, lo = pieces(bias_stage[0:1, :], 3)
    lines = jnp.concatenate(
        [hi.astype(F32), mid.astype(F32), lo.astype(F32), jnp.zeros((13, LANES), F32)], axis=0
    )
    pack[pl.ds(rows + half, 16), :] = lines.astype(BF16)
    aff_copy.wait()
    pack[pl.ds(rows, half), :] = aff_stage[...].astype(BF16)
    feat_copy.wait()


def low_kernel(map_w, map_low, stage, sems):
    layers = map_w.shape[0]
    copies = [
        pltpu.make_async_copy(map_w.at[layer], stage.at[layer], sems.at[layer])
        for layer in range(layers)
    ]
    for copy in copies:
        copy.start()
    for layer in range(layers):
        copies[layer].wait()
        map_low[layer] = stage[layer].astype(BF16)


def mapping_kernel(n_dp, samples, places, *refs):
    refs = list(refs)

    def take(count):
        got = refs[:count]
        del refs[:count]
        return got

    where, seeds, crossover = take(3)
    parts = take(len(places))
    z_table, map_b = take(2)
    pre_out, hid_out, top_out, picked_out, map_full = take(5)
    rows, sem_map, sem_z = refs
    layers, share, width = parts[0].shape
    latents = 2 * samples
    dp = where[0]
    z_copies = []
    for n in range(latents):
        at = pl.multiple_of((seeds[n] // 8) * 8, 8)
        z_copies.append(pltpu.make_async_copy(z_table.at[pl.ds(at, 8), :], rows.at[n], sem_z.at[n]))
        z_copies[n].start()
    odd = lax.rem(dp, 2)
    moves = []
    for part, (first, even_k, odd_k) in zip(parts, places):
        k = jnp.where(odd == 1, odd_k, even_k)
        at = pl.multiple_of(lax.bitwise_xor(dp, k) * share, share)
        moves.append((part, first, pl.ds(at, share)))
    whole_tiles = share % 16 == 0
    if not whole_tiles:
        copies = [
            pltpu.make_async_copy(
                part, map_full.at[pl.ds(first, part.shape[0]), at, :], sem_map.at[i]
            )
            for i, (part, first, at) in enumerate(moves)
        ]
        for copy in copies:
            copy.start()
        for copy in copies:
            copy.wait()

    def bring(layer):
        for part, first, at in moves:
            if whole_tiles and first <= layer < first + part.shape[0]:
                map_full[layer, at, :] = part[layer - first]

    bring(0)
    bring(1)
    hidden_rows = []
    for n in range(latents):
        z_copies[n].wait()
        row = rows[n, pl.ds(lax.rem(seeds[n], 8), 1), :]
        scale = lax.rsqrt(jnp.mean(row * row, axis=1, keepdims=True) + 1e-08)
        hidden_rows.append(row * scale)
    hidden_rows.append(jnp.zeros((16 - latents, width), F32))
    hidden = jnp.concatenate(hidden_rows, axis=0)
    for layer in range(layers):
        low = hidden.astype(BF16)
        preact = dot(low, map_full[layer]) + map_b[pl.ds(layer, 1), :]
        if layer + 2 < layers:
            bring(layer + 2)
        hid_out[layer] = low.astype(F32)[0:8]
        pre_out[layer] = preact[0:8]
        hidden = preact * jax.nn.sigmoid(preact)
    top_out[...] = hidden[0:8]
    low = hidden.astype(BF16).astype(F32)
    for j in range(2):
        chosen = []
        for s in range(samples):
            first = crossover[s] > j
            chosen.append(
                jnp.where(first, low[2 * s : 2 * s + 1, :], low[2 * s + 1 : 2 * s + 2, :])
            )
        chosen.append(jnp.zeros((8 - samples, width), F32))
        picked_out[j] = jnp.concatenate(chosen, axis=0)


def weights_kernel(conv_w, kernel, square, stage, sems):
    copies = [pltpu.make_async_copy(conv_w.at[t], stage.at[t], sems.at[t]) for t in range(TAPS)]
    for copy in copies:
        copy.start()
    total = jnp.zeros(square.shape, F32)
    for tap in range(TAPS):
        copies[tap].wait()
        low = stage[tap].astype(BF16)
        kernel[tap // 3, :, pl.ds((tap % 3) * LANES, LANES)] = low
        wide = low.astype(F32)
        total = total + wide * wide
    square[...] = total


def main_kernel(n_ch, samples, side, *refs):
    refs = list(refs)

    def take(count):
        got = refs[:count]
        del refs[:count]
        return got

    (where,) = take(1)
    both, first, first_pair, second, second_pair = take(5)
    kernel, square_in = take(2)
    aff_w, picked, bias, head, rgb_w = take(5)
    unit, to_sum, small, aff_full = take(4)
    bias_full, style_rows, late, late_tail, feat_t, padded, taps, shifted, wide = refs
    width = aff_full.shape[0]
    pixels = side * side
    half = width // 2
    dp, ch = where[0], where[1]
    pair = lax.rem(dp, 2)
    mine = pl.ds(pl.multiple_of(pair * half, half), half)
    other = pl.ds(pl.multiple_of((1 - pair) * half, half), half)

    tail_rows = half + 16
    feats = samples * pixels
    cut = first.shape[0] - first_pair.shape[0]
    partner_tail, partner_feats = feats + tail_rows, feats + 2 * tail_rows
    at_end = jnp.logical_or(ch == 0, ch == n_ch - 1)
    is_held = at_end == (pair == 1)

    @pl.when(is_held)
    def _():
        late[...] = second[pl.ds(0, feats + tail_rows), :]
        late_tail[...] = second[pl.ds(partner_tail, tail_rows), :]

    @pl.when(jnp.logical_not(is_held))
    def _():
        late[pl.ds(0, feats), :] = second_pair[pl.ds(partner_feats - cut, feats), :]
        late[pl.ds(feats, tail_rows), :] = second_pair[pl.ds(partner_tail - cut, tail_rows), :]
        late_tail[...] = second_pair[pl.ds(feats - cut, tail_rows), :]

    blocks = []
    for source, top, tail_at, other_source, other_tail_at, k in (
        (both, 0, feats, both, partner_tail, 0),
        (first, 0, feats, first, partner_tail, 1 + pair),
        (first_pair, partner_feats - cut, partner_tail - cut, first_pair, feats - cut, 2 - pair),
        (late, 0, feats, late_tail, 0, 3),
    ):
        at = pl.multiple_of(lax.bitwise_xor(ch, k) * LANES, LANES)
        lane = pl.ds(at, LANES)
        aff_full[mine, lane] = source[pl.ds(tail_at, half), :]
        aff_full[other, lane] = other_source[pl.ds(other_tail_at, half), :]
        bias_full[:, lane] = source[pl.ds(tail_at + half, 16), :]
        for s in range(samples):
            value = source[pl.ds(top + s * pixels, pixels), :]
            feat_t[s, lane, :] = value.T
        blocks.append((source, top, lane))
    square = square_in[...]

    wide_bias = bias_full[...].astype(F32)
    bias_row = wide_bias[0:1] + wide_bias[1:2] + wide_bias[2:3]
    style0 = (dot(picked[0].astype(BF16), aff_full[...]) + bias_row).astype(BF16)
    colour_aff = aff_w[1].astype(BF16)
    style1 = dot(picked[1].astype(BF16), colour_aff) + bias[1:2, :]
    style0_wide = style0.astype(F32)
    style1 = style1.astype(BF16).astype(F32)
    colour_aff = colour_aff.astype(F32)
    colour = rgb_w[...].astype(BF16)
    colour_wide = colour.astype(F32)
    colour_rows = jnp.concatenate([colour_wide, jnp.zeros((13, LANES), F32)], axis=0).astype(BF16)
    head_rows = jnp.concatenate(
        [head[...].astype(F32), jnp.zeros((13, pixels), F32)], axis=0
    ).astype(BF16)
    conv_bias = bias[2:3, :]
    chunk = min(256, pixels)
    steps = pixels // chunk
    column = lax.rem(lax.broadcasted_iota(jnp.int32, (chunk, LANES), 0), side)
    not_first, not_last = column > 0, column < side - 1
    small[...] = jnp.zeros_like(small)
    to_sum[...] = jnp.zeros_like(to_sum)
    padded[pl.ds(0, side), :] = jnp.zeros((side, width), BF16)
    padded[pl.ds(side + pixels, side), :] = jnp.zeros((side, width), BF16)
    taps[pl.ds(0, 8), :] = jnp.zeros((8, 3 * LANES), F32)
    taps[pl.ds(8 + pixels, 8), :] = jnp.zeros((8, 3 * LANES), F32)
    wide[pl.ds(0, 8), :] = jnp.zeros((8, LANES), F32)
    wide[pl.ds(8 + pixels, 8), :] = jnp.zeros((8, LANES), F32)

    for s in range(samples):
        style_rows[...] = style0_wide
        for source, top, lane in blocks:
            factor_row = style_rows[pl.ds(s, 1), lane].astype(BF16)
            padded[pl.ds(side, pixels), lane] = (
                source[pl.ds(top + s * pixels, pixels), :] * factor_row
            )
        style_col = jnp.broadcast_to(style0_wide[s : s + 1, :], (LANES, width)).T
        demod = lax.rsqrt(
            jnp.sum(style_col * style_col * square, axis=0, keepdims=True) + 1e-08
        )
        style_colour = style1[s : s + 1, :]
        for r in range(steps):
            total = dot(padded[pl.ds(r * chunk, chunk), :], kernel[0])
            total = total + dot(padded[pl.ds(side + r * chunk, chunk), :], kernel[1])
            total = total + dot(padded[pl.ds(2 * side + r * chunk, chunk), :], kernel[2])
            taps[pl.ds(8 + r * chunk, chunk), :] = total
        mixed = jnp.zeros((3, LANES), F32)
        g_style1 = jnp.zeros((1, LANES), F32)
        g_bias = jnp.zeros((1, LANES), F32)
        g_demod = jnp.zeros((1, LANES), F32)
        for r in range(steps):
            left = taps[pl.ds(7 + r * chunk, chunk), pl.ds(0, LANES)]
            centre = taps[pl.ds(8 + r * chunk, chunk), pl.ds(LANES, LANES)]
            right = taps[pl.ds(9 + r * chunk, chunk), pl.ds(2 * LANES, LANES)]
            conv_out = centre + jnp.where(not_first, left, 0.0) + jnp.where(not_last, right, 0.0)
            scaled = conv_out * demod + conv_bias
            sig = jax.nn.sigmoid(scaled)
            activated = scaled * sig
            act_mod = (activated * style_colour).astype(BF16)
            mixed = mixed + dot(head_rows[:, r * chunk : (r + 1) * chunk], act_mod)[0:3]
            g_act = dot_tn(head_rows[:, r * chunk : (r + 1) * chunk], colour_rows)
            g_style1 = g_style1 + jnp.sum(g_act * activated, axis=0, keepdims=True)
            g_scaled = g_act * style_colour * (sig * (1.0 + scaled * (1.0 - sig)))
            g_bias = g_bias + jnp.sum(g_scaled, axis=0, keepdims=True)
            g_demod = g_demod + jnp.sum(g_scaled * conv_out, axis=0, keepdims=True)
            wide[pl.ds(8 + r * chunk, chunk), :] = g_scaled * demod
        for r in range(steps):
            before = jnp.where(not_last, wide[pl.ds(9 + r * chunk, chunk), :], 0.0)
            centre = wide[pl.ds(8 + r * chunk, chunk), :]
            after = jnp.where(not_first, wide[pl.ds(7 + r * chunk, chunk), :], 0.0)
            for dx, value in enumerate((before, centre, after)):
                value = value.astype(BF16)
                for dy in range(3):
                    lane = pl.ds((3 * dy + dx) * LANES, LANES)
                    start = r * chunk + (dy - 1) * side
                    low_at, high_at = max(start, 0), min(start + chunk, pixels)
                    shifted[pl.ds(low_at, high_at - low_at), lane] = value[
                        low_at - start : high_at - start, :
                    ]
        for dx in range(3):
            shifted[pl.ds(pixels - side, side), pl.ds(dx * LANES, LANES)] = jnp.zeros(
                (side, LANES), BF16
            )
            shifted[pl.ds(0, side), pl.ds((6 + dx) * LANES, LANES)] = jnp.zeros(
                (side, LANES), BF16
            )
        factor = g_demod * demod * demod * demod
        g_style = jnp.zeros((width, LANES), F32)
        for first in range(0, TAPS, 2):
            count = min(2, TAPS - first)
            block = dot(feat_t[s], shifted[:, pl.ds(first * LANES, count * LANES)])
            for tap in range(first, first + count):
                raw = block[:, (tap - first) * LANES : (tap - first + 1) * LANES]
                weight = kernel[tap // 3, :, pl.ds((tap % 3) * LANES, LANES)].astype(F32)
                inner = raw - style_col * (weight * factor)
                g_style = g_style + weight * inner
                unit[s, pl.ds(tap * width, width), :] = (style_col * inner).astype(BF16)
        g_style_row = jnp.sum(g_style.T, axis=0, keepdims=True)
        g_colour_row = jnp.sum((colour_aff * g_style1).T, axis=0, keepdims=True)
        logit = jnp.sum(
            jnp.sum(mixed * colour_wide, axis=0, keepdims=True), axis=1, keepdims=True
        )
        to_sum[pl.ds(8 * s, 1), :] = jnp.broadcast_to(logit, (1, width))
        to_sum[pl.ds(8 * s + 1, 1), :] = g_style_row
        to_sum[pl.ds(8 * s + 2, 1), :] = g_colour_row
        small[pl.ds(8 * s, 1), :] = g_style1
        small[pl.ds(8 * s + 1, 1), :] = g_bias
        small[pl.ds(8 * s + 2, 3), :] = mixed


def summed(parts, row):
    values = [part[pl.ds(row, 1), :] for part in parts]
    while len(values) > 1:
        values = [values[i] + values[i + 1] for i in range(0, len(values), 2)]
    return values[0]


def logit_grad(parts, counted, s):
    logit = summed(parts, 8 * s)
    mask = jnp.full(logit.shape, counted[s], jnp.int32).astype(F32)
    return -mask * jax.nn.sigmoid(-logit), mask * jax.nn.softplus(-logit), mask


def scale_kernel(n_ch, samples, where, counted, *refs):
    parts, (unit, kept, sent) = refs[:n_ch], refs[n_ch:]
    pair = lax.rem(where[0], 2)
    half = unit.shape[1] // 2
    grads, total = [], jnp.zeros((1, LANES), F32)
    for s in range(samples):
        grad, _, mask = logit_grad(parts, counted, s)
        grads.append(grad[:, :LANES])
        total = total + mask[:, :LANES]
    block = half // 9
    for out, owner in ((kept, pair), (sent, 1 - pair)):
        for b in range(9):
            at = pl.multiple_of(owner * half + b * block, block)
            value = grads[0] * unit[0, pl.ds(at, block), :].astype(F32)
            for s in range(1, samples):
                value = value + grads[s] * unit[s, pl.ds(at, block), :].astype(F32)
            out[pl.ds(b * block, block), :] = value.astype(BF16)
        out[pl.ds(half, COUNT_ROWS), :] = jnp.broadcast_to(total, (COUNT_ROWS, LANES)).astype(BF16)


def pack_places(samples, layers):
    latents = 2 * samples
    style = 2 * layers * latents + latents
    colour = style + 2 * samples
    w_total = colour + 2 * samples
    return style, colour, w_total, -(-(w_total + 3) // 16) * 16


def mapping_back_kernel(n_ch, samples, where, counted, crossover, *refs):
    parts = refs[:n_ch]
    pre, hid, top, picked, small, map_full, aff_full, pack_out, rows, pack = refs[n_ch:]
    layers, _, width = map_full.shape
    latents = 2 * samples
    style_at, colour_at, w_at, _ = pack_places(samples, layers)
    ch = where[1]
    grads = [logit_grad(parts, counted, s) for s in range(samples)]
    pack[...] = jnp.zeros_like(pack)

    def put(line, lane, size, value, count):
        for i, part in enumerate(pieces(value, count)):
            pack[pl.ds(line + i, 1), pl.ds(lane, size)] = part.astype(F32)

    style_rows = []
    half_lane = lax.broadcasted_iota(jnp.int32, (1, LANES), 1) < LANES // 2
    for s in range(samples):
        grad = grads[s][0]
        style_row = grad * summed(parts, 8 * s + 1)
        rows[pl.ds(s, 1), :] = style_row
        style_rows.append(style_row)
        own = rows[pl.ds(s, 1), pl.ds(pl.multiple_of(ch * LANES, LANES), LANES)]
        short = grad[:, :LANES]
        put(style_at + 2 * s, 0, LANES, own, 2)
        put(style_at + 2 * s, LANES, LANES, short * small[pl.ds(8 * s, 1), :], 2)
        put(style_at + 2 * s, 2 * LANES, LANES, short * small[pl.ds(8 * s + 1, 1), :], 2)
        loss_count = jnp.where(half_lane, grads[s][1][:, :LANES], grads[s][2][:, :LANES])
        put(style_at + 2 * s, 3 * LANES, LANES, loss_count, 2)
        for c in range(3):
            value = short * small[pl.ds(8 * s + 2 + c, 1), :]
            put(colour_at + 2 * s, c * LANES, LANES, value, 2)
        for j in range(2):
            line = 2 * layers * latents + 2 * s + j
            pack[pl.ds(line, 1), :] = picked[j, pl.ds(s, 1), :]
    w_total = top[pl.ds(0, 1), :]
    for n in range(1, latents):
        w_total = w_total + top[pl.ds(n, 1), :]
    put(w_at, 0, width, w_total, 3)

    def back(value, weights):
        hi, lo = pieces(value, 2)
        both = jnp.concatenate([hi.astype(F32), lo.astype(F32)], axis=0).astype(BF16)
        out = dot_nt(both, weights)
        return out[0:8] + out[8:16]

    pad = [jnp.zeros((8 - samples, width), F32)]
    from_conv = back(jnp.concatenate(style_rows + pad, axis=0), aff_full[...])
    g_rows = []
    for s in range(samples):
        conv_row = from_conv[s : s + 1, :]
        colour_row = grads[s][0] * summed(parts, 8 * s + 2)
        to_first = [jnp.full((1, width), crossover[s], jnp.int32) > j for j in range(2)]
        g_rows.append(
            jnp.where(to_first[0], conv_row, 0.0) + jnp.where(to_first[1], colour_row, 0.0)
        )
        g_rows.append(
            jnp.where(to_first[0], 0.0, conv_row) + jnp.where(to_first[1], 0.0, colour_row)
        )
    g_rows.append(jnp.zeros((8 - latents, width), F32))
    g_hidden = jnp.concatenate(g_rows, axis=0)
    for layer in reversed(range(layers)):
        g_pre = g_hidden * silu_slope(pre[layer])
        pack[pl.ds(layer * latents, latents), :] = g_pre[0:latents]
        pack[pl.ds((layers + layer) * latents, latents), :] = hid[layer][0:latents]
        if layer > 0:
            g_hidden = back(g_pre, map_full[layer])
    pack_out[...] = pack[...].astype(BF16)


def update_kernel(n_dp, samples, layers, places, where, *refs):
    packs, refs = refs[: len(places)], refs[len(places) :]
    (map_w, map_m, map_e, aff_w, aff_m, aff_e) = refs[:6]
    (map_b, map_bm, map_be, bias, bias_m, bias_e, rgb, rgb_m, rgb_e, w_avg) = refs[6:16]
    outs, scratch = refs[16:-7], refs[-7:]
    map_outs, aff_outs = outs[0:4], outs[4:8]
    map_b_outs, bias_outs, rgb_outs = outs[8:12], outs[12:16], outs[16:20]
    w_avg_out, loss_out, count_out = outs[20:23]
    g_pre, hid, picked, style, rgb_all, sums, w_sums = scratch
    latents = 2 * samples
    style_at, colour_at, w_at, lines = pack_places(samples, layers)
    every = n_dp * latents
    dp = where[0]
    step = pl.program_id(0)
    share = map_w.shape[1]
    width = map_w.shape[2]

    @pl.when(step == 0)
    def _():
        odd = lax.rem(dp, 2)
        for part, place in zip(packs, places):
            for index, (even_k, odd_k) in enumerate(place):
                owner = lax.bitwise_xor(dp, jnp.where(odd == 1, odd_k, even_k))
                got = part[pl.ds(index * lines, lines), :].astype(F32)
                for layer in range(layers):
                    for n in range(latents):
                        at = pl.ds(owner * latents + n, 1)
                        line = layer * latents + n
                        g_pre[layer, at, :] = got[line : line + 1]
                        line += layers * latents
                        hid[layer, at, :] = got[line : line + 1]
                for s in range(samples):
                    at = pl.ds(owner * samples + s, 1)
                    line = 2 * layers * latents + 2 * s
                    for j in range(2):
                        picked[j, at, :] = got[line + j : line + j + 1]
                    line = style_at + 2 * s
                    style[at, :] = got[line : line + 1] + got[line + 1 : line + 2]
                    line = colour_at + 2 * s
                    rgb_all[at, :] = got[line : line + 1] + got[line + 1 : line + 2]
                w_sums[pl.ds(owner, 1), :] = (
                    got[w_at : w_at + 1] + got[w_at + 1 : w_at + 2] + got[w_at + 2 : w_at + 3]
                )
        sums[pl.ds(0, 1), :] = jnp.sum(style[...], axis=0, keepdims=True)
        sums[pl.ds(1, 1), :] = jnp.sum(rgb_all[...], axis=0, keepdims=True)
        total = sums[pl.ds(0, 1), :]
        count = total[:, width - LANES // 2 : width - LANES // 2 + 1]
        inverse = 1.0 / count
        for layer in range(layers):
            grad = jnp.sum(g_pre[layer], axis=0, keepdims=True) * inverse
            row = pl.ds(layer, 1)
            new = advance(map_b[row, :], map_bm[row, :], map_be[row, :], grad, 30.0)
            for out, value in zip(map_b_outs[:3], new[:3]):
                out[row, :] = value
        map_b_outs[3][...] = map_b_outs[0][...].astype(BF16)
        colour = sums[pl.ds(1, 1), :]
        for c in range(3):
            row = pl.ds(c, 1)
            lane = slice(c * LANES, (c + 1) * LANES)
            new = advance(bias[row, :], bias_m[row, :], bias_e[row, :], total[:, lane] * inverse, 50.0)
            for out, value in zip(bias_outs[:3], new[:3]):
                out[row, :] = value
            new = advance(rgb[row, :], rgb_m[row, :], rgb_e[row, :], colour[:, lane] * inverse, 1.0)
            for out, value in zip(rgb_outs[:3], new[:3]):
                out[row, :] = value
        bias_outs[3][...] = bias_outs[0][...].astype(BF16)
        rgb_outs[3][...] = rgb_outs[0][...].astype(BF16)
        mean = jnp.sum(w_sums[...], axis=0, keepdims=True) * (1.0 / every)
        w_avg_out[...] = w_avg[...] + (1.0 - AVERAGE_BETA) * (mean - w_avg[...])
        loss_out[0] = jnp.sum(total[:, width - LANES : width - LANES + 1])
        count_out[0] = jnp.sum(count)

    count = sums[pl.ds(0, 1), pl.ds(width - LANES, LANES)][:, LANES // 2 : LANES // 2 + 1]
    inverse = 1.0 / count
    each = map_outs[0].shape[0]
    for index in range(each):
        layer = step * each + index
        own = pltpu.roll(hid[layer], lax.rem(width - dp * share, width), 1)[:, :LANES]
        grad = dot_tn(own.astype(BF16), g_pre[layer].astype(BF16))[0:share] * inverse
        new = advance(map_w[layer], map_m[layer], map_e[layer], grad, 30.0)
        for out, value in zip(map_outs, new):
            out[index] = value
    chosen = jnp.concatenate([picked[step]] * 2, axis=0)
    grad_style = style[:, pl.ds(pl.multiple_of(step * LANES, LANES), LANES)]
    split = jnp.concatenate([p.astype(F32) for p in pieces(grad_style, 2)], axis=0)
    grad = dot_tn(chosen.astype(BF16), split.astype(BF16)) * inverse
    here = pl.ds(pl.multiple_of(step * width, width), width)
    new = advance(aff_w[here, :], aff_m[here, :], aff_e[here, :], grad, 30.0)
    for out, value in zip(aff_outs, new):
        out[...] = value


def conv_kernel(mine, where, grad, param, moment, average, *refs):
    refs = refs if mine else refs[4:]
    outs, buffers, sems = refs[0:4], refs[4:8], refs[8]
    half = grad.shape[0] - COUNT_ROWS
    pair = lax.rem(where[0], 2)
    start = pl.multiple_of((pair if mine else 1 - pair) * half, half)
    inverse = 1.0 / grad[pl.ds(half, 16), :].astype(F32)[0:1]
    chunks = sems.shape[0]
    depth = half // chunks
    copies = []
    for c in range(chunks):
        here = pl.ds(c * depth, depth)
        there = pl.ds(pl.multiple_of(start + c * depth, depth), depth)
        value = grad[here, :].astype(F32) * inverse
        new = advance(param[there, :], moment[there, :], average[there, :], value, 5.0)
        for k in range(4):
            buffers[k][here, :] = new[k]
            copy = pltpu.make_async_copy(buffers[k].at[here, :], outs[k].at[there, :], sems.at[c, k])
            copy.start()
            copies.append(copy)
    for copy in copies:
        copy.wait()


def local(
    features,
    z_table,
    seeds,
    crossover,
    counted,
    head,
    w_avg,
    map_w,
    map_w_mom,
    map_w_ema,
    map_b,
    map_b_mom,
    map_b_ema,
    aff_w,
    aff_w_mom,
    aff_w_ema,
    chan_bias,
    chan_bias_mom,
    chan_bias_ema,
    conv_w,
    conv_w_mom,
    conv_w_ema,
    rgb_w,
    rgb_w_mom,
    rgb_w_ema,
):
    samples, side = features.shape[0], features.shape[1]
    pixels = side * side
    layers, share, width = map_w.shape
    n_dp, n_ch = lax.axis_size("dp"), lax.axis_size("chan")
    latents = 2 * samples
    where = jnp.stack([lax.axis_index("dp"), lax.axis_index("chan")]).astype(jnp.int32)
    flat = lambda a: a.reshape(TAPS * width, LANES)

    half = width // 2
    pack_rows = samples * pixels + half + 16
    pack = pl.pallas_call(
        pack_kernel,
        out_shape=shape((pack_rows, LANES), BF16),
        in_specs=[SMEM] + [ANY] * 3,
        out_specs=VMEM,
        scratch_shapes=[
            pltpu.VMEM((half, LANES), F32),
            pltpu.VMEM(chan_bias.shape, F32),
            pltpu.SemaphoreType.DMA((3,)),
        ],
        compiler_params=params(4),
        cost_estimate=cost(1),
        name="pack",
    )(where, *hbm(aff_w, chan_bias, features.reshape(samples * pixels, LANES)))
    map_low = pl.pallas_call(
        low_kernel,
        out_shape=shape(map_w.shape, BF16),
        in_specs=[ANY],
        out_specs=VMEM,
        scratch_shapes=[pltpu.VMEM(map_w.shape, F32), pltpu.SemaphoreType.DMA((layers,))],
        compiler_params=params(8),
        cost_estimate=cost(1),
        name="low",
    )(*hbm(map_w))
    *chan_packs, last_step = spread_over_chan(pack, half + 16, map_low)
    blocks = spread_layers(map_low, "dp")
    kernel, square = pl.pallas_call(
        weights_kernel,
        out_shape=(shape((3, width, 3 * LANES), BF16), shape((width, LANES), F32)),
        in_specs=[ANY],
        out_specs=(VMEM, VMEM),
        scratch_shapes=[
            pltpu.VMEM((TAPS, width, LANES), F32),
            pltpu.SemaphoreType.DMA((TAPS,)),
        ],
        compiler_params=params(8),
        cost_estimate=cost(2),
        name="weights",
    )(*hbm(after(conv_w.reshape(TAPS, width, LANES), blocks[1][0])))
    second = last_step(blocks[2][0], kernel)
    places = [place for _, place in blocks]

    pre, hid, top, picked, map_full = pl.pallas_call(
        functools.partial(mapping_kernel, n_dp, samples, places),
        out_shape=(
            shape((layers, 8, width), F32),
            shape((layers, 8, width), F32),
            shape((8, width), F32),
            shape((2, 8, width), F32),
            shape((layers, width, width), BF16),
        ),
        in_specs=[SMEM] * 3 + [VMEM] * len(blocks) + [ANY, VMEM],
        out_specs=(VMEM,) * 5,
        scratch_shapes=[
            pltpu.VMEM((latents, 8, width), F32),
            pltpu.SemaphoreType.DMA((len(places),)),
            pltpu.SemaphoreType.DMA((latents,)),
        ],
        compiler_params=params(12),
        cost_estimate=cost(1),
        name="mapping",
    )(where, seeds.reshape(-1), crossover, *[block for block, _ in blocks], *hbm(z_table), map_b)

    chan_packs += [second, swap(after(second, picked)[samples * pixels :], "dp", 1)]
    unit, to_sum, small, aff_full = pl.pallas_call(
        functools.partial(main_kernel, n_ch, samples, side),
        out_shape=(
            shape((samples, TAPS * width, LANES), BF16),
            shape((8 * samples, width), F32),
            shape((8 * samples, LANES), F32),
            shape((width, width), BF16),
        ),
        in_specs=[SMEM] + [VMEM] * 12,
        out_specs=(VMEM,) * 4,
        scratch_shapes=[
            pltpu.VMEM((16, width), BF16),
            pltpu.VMEM((8, width), F32),
            pltpu.VMEM((pack_rows, LANES), BF16),
            pltpu.VMEM((half + 16, LANES), BF16),
            pltpu.VMEM((samples, width, pixels), BF16),
            pltpu.VMEM((pixels + 2 * side, width), BF16),
            pltpu.VMEM((pixels + 16, 3 * LANES), F32),
            pltpu.VMEM((pixels, TAPS * LANES), BF16),
            pltpu.VMEM((pixels + 16, LANES), F32),
        ],
        compiler_params=params(20),
        cost_estimate=cost(8),
        name="main",
    )(
        where,
        *chan_packs,
        kernel,
        square,
        aff_w,
        picked,
        chan_bias,
        head,
        rgb_w,
    )

    sum_parts = spread_direct(to_sum, "chan")
    half_rows = TAPS * width // 2 + COUNT_ROWS
    kept, sent = pl.pallas_call(
        functools.partial(scale_kernel, n_ch, samples),
        out_shape=(shape((half_rows, LANES), BF16),) * 2,
        in_specs=[SMEM] * 2 + [VMEM] * (n_ch + 1),
        out_specs=(VMEM, VMEM),
        compiler_params=params(8),
        cost_estimate=cost(1),
        name="scale",
    )(where, counted, *sum_parts, unit)

    lines = pack_places(samples, layers)[-1]
    pack = pl.pallas_call(
        functools.partial(mapping_back_kernel, n_ch, samples),
        out_shape=shape((lines, width), BF16),
        in_specs=[SMEM] * 3 + [VMEM] * (n_ch + 7),
        out_specs=VMEM,
        scratch_shapes=[pltpu.VMEM((8, width), F32), pltpu.VMEM((lines, width), F32)],
        compiler_params=params(12),
        cost_estimate=cost(2),
        name="mapping_back",
    )(where, counted, crossover, *sum_parts, pre, hid, top, picked, small, map_full, aff_full)
    spread_pack = spread(pack, "dp")
    packs = [part for part, _ in spread_pack]

    whole = lambda a: pl.BlockSpec(a.shape, lambda i: (0,) * len(a.shape))
    map_spec = pl.BlockSpec((layers // 2, share, width), lambda i: (i, 0, 0))
    aff_spec = pl.BlockSpec((width, LANES), lambda i: (i, 0))
    flat_aff = [a.reshape(2 * width, LANES) for a in (aff_w, aff_w_mom, aff_w_ema)]
    tiny = [
        map_b,
        map_b_mom,
        map_b_ema,
        chan_bias,
        chan_bias_mom,
        chan_bias_ema,
        rgb_w,
        rgb_w_mom,
        rgb_w_ema,
        w_avg.reshape(1, width),
    ]
    types = (F32, F32, F32, BF16)
    out_shape = (
        [shape(map_w.shape, t) for t in types]
        + [shape((2 * width, LANES), t) for t in types]
        + [shape(map_b.shape, t) for t in types]
        + [shape(chan_bias.shape, t) for t in types]
        + [shape(rgb_w.shape, t) for t in types]
        + [shape((1, width), F32), shape((1,), F32), shape((1,), F32)]
    )
    every = n_dp * latents
    update = lambda: pl.pallas_call(
        functools.partial(update_kernel, n_dp, samples, layers, [p for _, p in spread_pack]),
        grid=(2,),
        out_shape=out_shape,
        in_specs=[SMEM]
        + [VMEM] * len(packs)
        + [VMEM] * (6 + len(tiny)),
        out_specs=[map_spec] * 4
        + [aff_spec] * 4
        + [whole(s) for s in out_shape[8:21]]
        + [SMEM, SMEM],
        scratch_shapes=[
            pltpu.VMEM((layers, every, width), F32),
            pltpu.VMEM((layers, every, width), F32),
            pltpu.VMEM((2, n_dp * samples, width), F32),
            pltpu.VMEM((n_dp * samples, width), F32),
            pltpu.VMEM((n_dp * samples, width), F32),
            pltpu.VMEM((8, width), F32),
            pltpu.VMEM((n_dp, width), F32),
        ],
        compiler_params=params(20),
        cost_estimate=cost(5),
        name="update",
    )(where, *packs, map_w, map_w_mom, map_w_ema, *flat_aff, *tiny)

    got = after(swap(sent, "dp", 1), pack)
    total = (kept.astype(F32) + got.astype(F32)).astype(BF16)
    bits = [1 << b for b in range(1, n_dp.bit_length() - 1)]
    for turn, (even_bit, odd_bit) in enumerate(zip(bits, bits[::-1])):
        got = crossed(total, "dp", even_bit, odd_bit)
        if turn == len(bits) - 2:
            got = after(got, packs[1])
        if turn == len(bits) - 1:
            outs = update()
            got = after(got, *outs)
        total = (total.astype(F32) + got.astype(F32)).astype(BF16)
    other = swap(total, "dp", 1)

    conv_params = [flat(conv_w), flat(conv_w_mom), flat(conv_w_ema)]
    half_rows = TAPS * width // 2

    def conv_half(grad, *earlier):
        return pl.pallas_call(
            functools.partial(conv_kernel, not earlier),
            out_shape=[shape((TAPS * width, LANES), t) for t in types],
            in_specs=[SMEM] + [VMEM] * 4 + [ANY] * len(earlier),
            out_specs=[ANY] * 4,
            scratch_shapes=[pltpu.VMEM((half_rows, LANES), t) for t in types]
            + [pltpu.SemaphoreType.DMA((3, 4))],
            input_output_aliases={5 + k: k for k in range(len(earlier))},
            compiler_params=params(12),
            cost_estimate=cost(2),
            name="conv_other" if earlier else "conv_own",
        )(where, grad, *conv_params, *earlier)

    conv_outs = conv_half(other, *conv_half(total))

    map_outs, aff_outs = outs[0:4], [a.reshape(aff_w.shape) for a in outs[4:8]]
    conv_outs = [a.reshape(conv_w.shape) for a in conv_outs]
    return (
        *map_outs,
        *outs[8:12],
        *aff_outs,
        *outs[12:16],
        *conv_outs,
        *outs[16:20],
        outs[20].reshape(width),
        outs[21].reshape(()),
        outs[22].reshape(()),
    )


def solution(mesh):
    in_specs = (
        P("dp", None, None, "chan"),
        P(),
        P("dp", None),
        P("dp"),
        P("dp"),
        P(),
        P(),
        P(None, "dp", None),
        P(None, "dp", None),
        P(None, "dp", None),
        P(),
        P(),
        P(),
        P(None, None, "chan"),
        P(None, None, "chan"),
        P(None, None, "chan"),
        P(None, "chan"),
        P(None, "chan"),
        P(None, "chan"),
        P(None, None, None, "chan"),
        P(None, None, None, "chan"),
        P(None, None, None, "chan"),
        P(None, "chan"),
        P(None, "chan"),
        P(None, "chan"),
    )
    out_specs = (
        P(None, "dp", None),
        P(None, "dp", None),
        P(None, "dp", None),
        P(None, "dp", None),
        P(),
        P(),
        P(),
        P(),
        P(None, None, "chan"),
        P(None, None, "chan"),
        P(None, None, "chan"),
        P(None, None, "chan"),
        P(None, "chan"),
        P(None, "chan"),
        P(None, "chan"),
        P(None, "chan"),
        P(None, None, None, "chan"),
        P(None, None, None, "chan"),
        P(None, None, None, "chan"),
        P(None, None, None, "chan"),
        P(None, "chan"),
        P(None, "chan"),
        P(None, "chan"),
        P(None, "chan"),
        P(),
        P(),
        P(),
    )
    return jax.shard_map(local, mesh=mesh, in_specs=in_specs, out_specs=out_specs, check_vma=False)
```

```python
import functools

import jax
import jax.numpy as jnp
from jax import lax
from jax.experimental import pallas as pl
from jax.experimental.pallas import tpu as pltpu
from jax.sharding import PartitionSpec as P

MOMENTUM = 0.9
EMA_DECAY = 0.95
AVERAGE_BETA = 0.5
BF16 = jnp.bfloat16
F32 = jnp.float32
TAPS = 9
LANES = 128
COUNT_ROWS = 32
VMEM = pl.BlockSpec(memory_space=pltpu.VMEM)
SMEM = pl.BlockSpec(memory_space=pltpu.SMEM)
ANY = pl.BlockSpec(memory_space=pl.ANY)


def shape(dims, dtype):
    return jax.ShapeDtypeStruct(dims, dtype)


def params(mib):
    return pltpu.CompilerParams(vmem_limit_bytes=mib * 1024 * 1024)


def cost(micros):
    return pl.CostEstimate(flops=0, bytes_accessed=int(micros * 3.5e6), transcendentals=0)


def hbm(*values):
    return [pltpu.with_memory_space_constraint(value, pltpu.HBM) for value in values]


def after(values, *others):
    return lax.optimization_barrier((values, others))[0]


def swap(value, axis, distance):
    return lax.ppermute(
        value, axis, [(i, i ^ distance) for i in range(lax.axis_size(axis))]
    )


def spread(value, axis):
    size = lax.axis_size(axis)
    beside = swap(value, axis, 1)
    if size != 8:
        parts = [(value, [(0, 0)]), (beside, [(1, 1)])]
        for k in range(2, size, 2):
            part = swap(value, axis, k)
            parts += [(part, [(k, k)]), (swap(part, axis, 1), [(k + 1, k + 1)])]
        return parts
    near = jnp.concatenate([value, beside])
    far = crossed(near, axis, 4, 2)
    corner = crossed(far, axis, 2, 4)
    return [
        (near, [(0, 0), (1, 1)]),
        (far, [(4, 2), (5, 3)]),
        (corner, [(6, 6), (7, 7)]),
        (swap(far, axis, 1), [(3, 5), (2, 4)]),
    ]


def spread_direct(value, axis):
    return [value] + [swap(value, axis, k) for k in range(1, lax.axis_size(axis))]


def spread_over_chan(pack, tail, ready):
    n_dp, n_ch = lax.axis_size("dp"), lax.axis_size("chan")
    cut = pack.shape[0] - tail
    other = swap(pack, "dp", 1)
    both = after(jnp.concatenate([pack, other[cut:], other[:cut]]), ready)

    def joint(value, moves):
        pairs = [
            (d * n_ch + a, d * n_ch + b) for d in range(n_dp) for a, b in moves[d % 2]
        ]
        return lax.ppermute(value, ("dp", "chan"), pairs)

    first = joint(both, ([(c, c ^ 1) for c in range(4)], [(c, c ^ 2) for c in range(4)]))
    first_pair = swap(first[cut:], "dp", 1)
    odd = lax.rem(lax.axis_index("dp"), 2) == 1

    def last_step(*others):
        value = after(jnp.where(odd, first, both), *others)
        return joint(value, ([(1, 2), (2, 1)], [(1, 0), (2, 3)]))

    return both, first, first_pair, last_step


def crossed(value, axis, even_distance, odd_distance):
    size = lax.axis_size(axis)
    pairs = [(i, i ^ (odd_distance if i % 2 else even_distance)) for i in range(size)]
    return lax.ppermute(value, axis, pairs)


def spread_layers(value, axis):
    size = lax.axis_size(axis)
    beside = swap(value, axis, 1)
    parts = [(value, (0, 0, 0)), (beside, (0, 1, 1))]
    if size != 8:
        for k in range(2, size, 2):
            part = swap(value, axis, k)
            parts += [(part, (0, k, k)), (swap(part, axis, 1), (0, k + 1, k + 1))]
        return parts
    far = crossed(value, axis, 2, 4)
    far_beside = crossed(beside, axis, 2, 4)
    corner = crossed(far, axis, 4, 2)
    parts += [(far, (0, 2, 4)), (far_beside, (0, 3, 5)), (corner, (0, 6, 6))]
    parts += [(swap(far, axis, 1), (0, 5, 3)), (swap(far_beside, axis, 1), (0, 4, 2))]
    parts += [(swap(corner, axis, 1), (0, 7, 7))]
    return parts


def silu_slope(preact):
    sig = jax.nn.sigmoid(preact)
    return sig * (1.0 + preact * (1.0 - sig))


def pieces(value, count):
    out = []
    for _ in range(count):
        part = value.astype(BF16)
        out.append(part)
        value = value - part.astype(F32)
    return out


def advance(param, moment, average, grad, rate):
    moment_new = MOMENTUM * moment + grad
    param_new = param - rate * (grad + MOMENTUM * moment_new)
    average_new = EMA_DECAY * average + (1.0 - EMA_DECAY) * param_new
    return param_new, moment_new, average_new, param_new.astype(BF16)


def dot(a, b):
    return jnp.dot(a, b, preferred_element_type=F32)


def dot_nt(a, b):
    return lax.dot_general(a, b, (((1,), (1,)), ((), ())), preferred_element_type=F32)


def dot_tn(a, b):
    return lax.dot_general(a, b, (((0,), (0,)), ((), ())), preferred_element_type=F32)


def pack_kernel(where, aff_w, bias, features, pack, aff_stage, bias_stage, sems):
    half = aff_stage.shape[0]
    rows = features.shape[0]
    start = pl.multiple_of(lax.rem(where[0], 2) * half, half)
    feat_copy = pltpu.make_async_copy(features, pack.at[pl.ds(0, rows), :], sems.at[0])
    aff_copy = pltpu.make_async_copy(aff_w.at[0, pl.ds(start, half), :], aff_stage, sems.at[1])
    bias_copy = pltpu.make_async_copy(bias, bias_stage, sems.at[2])
    for copy in (feat_copy, aff_copy, bias_copy):
        copy.start()
    bias_copy.wait()
    hi, mid, lo = pieces(bias_stage[0:1, :], 3)
    lines = jnp.concatenate(
        [hi.astype(F32), mid.astype(F32), lo.astype(F32), jnp.zeros((13, LANES), F32)], axis=0
    )
    pack[pl.ds(rows + half, 16), :] = lines.astype(BF16)
    aff_copy.wait()
    pack[pl.ds(rows, half), :] = aff_stage[...].astype(BF16)
    feat_copy.wait()


def low_kernel(map_w, map_low, stage, sems):
    layers = map_w.shape[0]
    copies = [
        pltpu.make_async_copy(map_w.at[layer], stage.at[layer], sems.at[layer])
        for layer in range(layers)
    ]
    for copy in copies:
        copy.start()
    for layer in range(layers):
        copies[layer].wait()
        map_low[layer] = stage[layer].astype(BF16)


def mapping_kernel(n_dp, samples, places, *refs):
    refs = list(refs)

    def take(count):
        got = refs[:count]
        del refs[:count]
        return got

    where, seeds, crossover = take(3)
    parts = take(len(places))
    z_table, map_b = take(2)
    pre_out, hid_out, top_out, picked_out, map_full = take(5)
    rows, sem_map, sem_z = refs
    layers, share, width = parts[0].shape
    latents = 2 * samples
    dp = where[0]
    z_copies = []
    for n in range(latents):
        at = pl.multiple_of((seeds[n] // 8) * 8, 8)
        z_copies.append(pltpu.make_async_copy(z_table.at[pl.ds(at, 8), :], rows.at[n], sem_z.at[n]))
        z_copies[n].start()
    odd = lax.rem(dp, 2)
    moves = []
    for part, (first, even_k, odd_k) in zip(parts, places):
        k = jnp.where(odd == 1, odd_k, even_k)
        at = pl.multiple_of(lax.bitwise_xor(dp, k) * share, share)
        moves.append((part, first, pl.ds(at, share)))
    whole_tiles = share % 16 == 0
    if not whole_tiles:
        copies = [
            pltpu.make_async_copy(
                part, map_full.at[pl.ds(first, part.shape[0]), at, :], sem_map.at[i]
            )
            for i, (part, first, at) in enumerate(moves)
        ]
        for copy in copies:
            copy.start()
        for copy in copies:
            copy.wait()

    def bring(layer):
        for part, first, at in moves:
            if whole_tiles and first <= layer < first + part.shape[0]:
                map_full[layer, at, :] = part[layer - first]

    bring(0)
    bring(1)
    hidden_rows = []
    for n in range(latents):
        z_copies[n].wait()
        row = rows[n, pl.ds(lax.rem(seeds[n], 8), 1), :]
        scale = lax.rsqrt(jnp.mean(row * row, axis=1, keepdims=True) + 1e-08)
        hidden_rows.append(row * scale)
    hidden_rows.append(jnp.zeros((16 - latents, width), F32))
    hidden = jnp.concatenate(hidden_rows, axis=0)
    for layer in range(layers):
        low = hidden.astype(BF16)
        preact = dot(low, map_full[layer]) + map_b[pl.ds(layer, 1), :]
        if layer + 2 < layers:
            bring(layer + 2)
        hid_out[layer] = low.astype(F32)[0:8]
        pre_out[layer] = preact[0:8]
        hidden = preact * jax.nn.sigmoid(preact)
    top_out[...] = hidden[0:8]
    low = hidden.astype(BF16).astype(F32)
    for j in range(2):
        chosen = []
        for s in range(samples):
            first = crossover[s] > j
            chosen.append(
                jnp.where(first, low[2 * s : 2 * s + 1, :], low[2 * s + 1 : 2 * s + 2, :])
            )
        chosen.append(jnp.zeros((8 - samples, width), F32))
        picked_out[j] = jnp.concatenate(chosen, axis=0)


def weights_kernel(conv_w, kernel, square, stage, sems):
    copies = [pltpu.make_async_copy(conv_w.at[t], stage.at[t], sems.at[t]) for t in range(TAPS)]
    for copy in copies:
        copy.start()
    total = jnp.zeros(square.shape, F32)
    for tap in range(TAPS):
        copies[tap].wait()
        low = stage[tap].astype(BF16)
        kernel[tap // 3, :, pl.ds((tap % 3) * LANES, LANES)] = low
        wide = low.astype(F32)
        total = total + wide * wide
    square[...] = total


def bring_blocks(blocks, samples, side, where, picked, bias_full, style_rows, feat_t, aff_full, padded):
    width = aff_full.shape[0]
    half, pixels = width // 2, side * side
    dp, ch = where[0], where[1]
    pair = lax.rem(dp, 2)
    mine = pl.ds(pl.multiple_of(pair * half, half), half)
    other = pl.ds(pl.multiple_of((1 - pair) * half, half), half)
    chosen = picked[0].astype(BF16)
    for source, top, tail_at, other_source, other_tail_at, k in blocks:
        lane = pl.ds(pl.multiple_of(lax.bitwise_xor(ch, k) * LANES, LANES), LANES)
        aff_full[mine, lane] = source[pl.ds(tail_at, half), :]
        aff_full[other, lane] = other_source[pl.ds(other_tail_at, half), :]
        bias_full[...] = source[pl.ds(tail_at + half, 16), :].astype(F32)
        bias_row = bias_full[0:1, :] + bias_full[1:2, :] + bias_full[2:3, :]
        style = (dot(chosen, aff_full[:, lane]) + bias_row).astype(BF16)
        style_rows[:, lane] = style.astype(F32)
        for s in range(samples):
            value = source[pl.ds(top + s * pixels, pixels), :]
            feat_t[s, lane, :] = value.T
            padded[s, pl.ds(side, pixels), lane] = value * style[s : s + 1, :]


def begin_kernel(n_ch, samples, side, *refs):
    where, both, first, first_pair, kernel, picked = refs[:6]
    feat_t, taps, style_rows, aff_full, bias_full, padded = refs[6:]
    width = aff_full.shape[0]
    half, pixels = width // 2, side * side
    feats, tail_rows = samples * pixels, half + 16
    cut = first.shape[0] - first_pair.shape[0]
    partner_tail, partner_feats = feats + tail_rows, feats + 2 * tail_rows
    pair = lax.rem(where[0], 2)
    last = pl.ds(pl.multiple_of(lax.bitwise_xor(where[1], 3) * LANES, LANES), LANES)
    for s in range(samples):
        padded[s, pl.ds(0, side), :] = jnp.zeros((side, width), BF16)
        padded[s, pl.ds(side + pixels, side), :] = jnp.zeros((side, width), BF16)
        padded[s, pl.ds(side, pixels), last] = jnp.zeros((pixels, LANES), BF16)
    style_rows[...] = jnp.zeros_like(style_rows)
    blocks = (
        (both, 0, feats, both, partner_tail, 0),
        (first, 0, feats, first, partner_tail, 1 + pair),
        (first_pair, partner_feats - cut, partner_tail - cut, first_pair, feats - cut, 2 - pair),
    )
    bring_blocks(
        blocks, samples, side, where, picked, bias_full, style_rows, feat_t, aff_full, padded
    )
    chunk = min(256, pixels)
    for s in range(samples):
        for r in range(pixels // chunk):
            total = dot(padded[s, pl.ds(r * chunk, chunk), :], kernel[0])
            total = total + dot(padded[s, pl.ds(side + r * chunk, chunk), :], kernel[1])
            total = total + dot(padded[s, pl.ds(2 * side + r * chunk, chunk), :], kernel[2])
            taps[s, pl.ds(r * chunk, chunk), :] = total


def main_kernel(n_ch, samples, side, *refs):
    where, second, second_pair, earlier, kernel, square_in = refs[:6]
    aff_w, picked, bias, head, rgb_w, counted = refs[6:12]
    feat_t, style_rows, aff_full, wide, small, loss_rows = refs[15:21]
    bias_full, late, late_tail, padded, taps = refs[21:]
    width = aff_full.shape[0]
    half, pixels = width // 2, side * side
    feats, tail_rows = samples * pixels, half + 16
    cut = second.shape[0] - second_pair.shape[0]
    partner_tail, partner_feats = feats + tail_rows, feats + 2 * tail_rows
    dp, ch = where[0], where[1]
    pair = lax.rem(dp, 2)
    at_end = jnp.logical_or(ch == 0, ch == n_ch - 1)
    is_held = at_end == (pair == 1)

    @pl.when(is_held)
    def _():
        late[...] = second[pl.ds(0, feats + tail_rows), :]
        late_tail[...] = second[pl.ds(partner_tail, tail_rows), :]

    @pl.when(jnp.logical_not(is_held))
    def _():
        late[pl.ds(0, feats), :] = second_pair[pl.ds(partner_feats - cut, feats), :]
        late[pl.ds(feats, tail_rows), :] = second_pair[pl.ds(partner_tail - cut, tail_rows), :]
        late_tail[...] = second_pair[pl.ds(feats - cut, tail_rows), :]

    for s in range(samples):
        padded[s, pl.ds(0, side), :] = jnp.zeros((side, LANES), BF16)
        padded[s, pl.ds(side + pixels, side), :] = jnp.zeros((side, LANES), BF16)
    mine = pl.ds(pl.multiple_of(pair * half, half), half)
    other = pl.ds(pl.multiple_of((1 - pair) * half, half), half)
    lane = pl.ds(pl.multiple_of(lax.bitwise_xor(ch, 3) * LANES, LANES), LANES)
    aff_full[mine, lane] = late[pl.ds(feats, half), :]
    aff_full[other, lane] = late_tail[pl.ds(0, half), :]
    bias_full[...] = late[pl.ds(feats + half, 16), :].astype(F32)
    bias_row = bias_full[0:1, :] + bias_full[1:2, :] + bias_full[2:3, :]
    style = (dot(picked[0].astype(BF16), aff_full[:, lane]) + bias_row).astype(BF16)
    style_rows[:, lane] = style.astype(F32)
    for s in range(samples):
        value = late[pl.ds(s * pixels, pixels), :]
        feat_t[s, lane, :] = value.T
        padded[s, pl.ds(side, pixels), :] = value * style[s : s + 1, :]
    square = square_in[...]
    colour_aff = aff_w[1].astype(BF16)
    style1 = dot(picked[1].astype(BF16), colour_aff) + bias[1:2, :]
    style1 = style1.astype(BF16).astype(F32)
    colour = rgb_w[...].astype(BF16)
    colour_wide = colour.astype(F32)
    colour_rows = jnp.concatenate([colour_wide, jnp.zeros((13, LANES), F32)], axis=0).astype(BF16)
    head_rows = jnp.concatenate(
        [head[...].astype(F32), jnp.zeros((13, pixels), F32)], axis=0
    ).astype(BF16)
    conv_bias = bias[2:3, :]
    chunk = min(256, pixels)
    steps = pixels // chunk
    column = lax.rem(lax.broadcasted_iota(jnp.int32, (chunk, LANES), 0), side)
    not_first, not_last = column > 0, column < side - 1
    small[...] = jnp.zeros_like(small)
    loss_rows[...] = jnp.zeros_like(loss_rows)
    taps[pl.ds(0, 8), :] = jnp.zeros((8, 3 * LANES), F32)
    taps[pl.ds(8 + pixels, 8), :] = jnp.zeros((8, 3 * LANES), F32)

    for s in range(samples):
        wide[s, pl.ds(0, 8), :] = jnp.zeros((8, LANES), F32)
        wide[s, pl.ds(8 + pixels, 8), :] = jnp.zeros((8, LANES), F32)
        style_col = jnp.broadcast_to(style_rows[pl.ds(s, 1), :], (LANES, width)).T
        demod = lax.rsqrt(
            jnp.sum(style_col * style_col * square, axis=0, keepdims=True) + 1e-08
        )
        style_colour = style1[s : s + 1, :]
        for r in range(steps):
            total = earlier[s, pl.ds(r * chunk, chunk), :]
            for dy in range(3):
                total = total + dot(
                    padded[s, pl.ds(dy * side + r * chunk, chunk), :], kernel[dy, lane, :]
                )
            taps[pl.ds(8 + r * chunk, chunk), :] = total
        mixed = jnp.zeros((3, LANES), F32)
        g_style1 = jnp.zeros((1, LANES), F32)
        g_bias = jnp.zeros((1, LANES), F32)
        g_demod = jnp.zeros((1, LANES), F32)
        for r in range(steps):
            left = taps[pl.ds(7 + r * chunk, chunk), pl.ds(0, LANES)]
            centre = taps[pl.ds(8 + r * chunk, chunk), pl.ds(LANES, LANES)]
            right = taps[pl.ds(9 + r * chunk, chunk), pl.ds(2 * LANES, LANES)]
            conv_out = centre + jnp.where(not_first, left, 0.0) + jnp.where(not_last, right, 0.0)
            scaled = conv_out * demod + conv_bias
            sig = jax.nn.sigmoid(scaled)
            activated = scaled * sig
            act_mod = (activated * style_colour).astype(BF16)
            mixed = mixed + dot(head_rows[:, r * chunk : (r + 1) * chunk], act_mod)[0:3]
            g_act = dot_tn(head_rows[:, r * chunk : (r + 1) * chunk], colour_rows)
            g_style1 = g_style1 + jnp.sum(g_act * activated, axis=0, keepdims=True)
            g_scaled = g_act * style_colour * (sig * (1.0 + scaled * (1.0 - sig)))
            g_bias = g_bias + jnp.sum(g_scaled, axis=0, keepdims=True)
            g_demod = g_demod + jnp.sum(g_scaled * conv_out, axis=0, keepdims=True)
            wide[s, pl.ds(8 + r * chunk, chunk), :] = g_scaled * demod
        logit = jnp.sum(
            jnp.sum(mixed * colour_wide, axis=0, keepdims=True), axis=1, keepdims=True
        )
        loss_rows[pl.ds(s, 1), :] = jnp.broadcast_to(logit, (1, LANES))
        loss_rows[pl.ds(4 * samples + s, 1), :] = jnp.full((1, LANES), counted[s], jnp.int32).astype(F32)
        small[pl.ds(8 * s, 1), :] = g_style1
        small[pl.ds(8 * s + 1, 1), :] = g_bias
        small[pl.ds(8 * s + 2, 3), :] = mixed
        small[pl.ds(8 * s + 5, 1), :] = g_demod * demod * demod * demod


def factor_kernel(samples, side, where, feat_t, wide, small, style_rows, kernel, aff_w, unit, to_sum, shifted):
    width = feat_t.shape[1]
    pixels = side * side
    pair = lax.rem(where[0], 2)
    half = TAPS * width // 2
    chunk = min(256, pixels)
    steps = pixels // chunk
    column = lax.rem(lax.broadcasted_iota(jnp.int32, (chunk, LANES), 0), side)
    not_first, not_last = column > 0, column < side - 1
    to_sum[...] = jnp.zeros_like(to_sum)
    colour_aff = aff_w[1].astype(BF16).astype(F32)
    for s in range(samples):
        style_col = jnp.broadcast_to(style_rows[pl.ds(s, 1), :], (LANES, width)).T
        for r in range(steps):
            before = jnp.where(not_last, wide[s, pl.ds(9 + r * chunk, chunk), :], 0.0)
            centre = wide[s, pl.ds(8 + r * chunk, chunk), :]
            after_it = jnp.where(not_first, wide[s, pl.ds(7 + r * chunk, chunk), :], 0.0)
            for dx, value in enumerate((before, centre, after_it)):
                value = value.astype(BF16)
                for dy in range(3):
                    lane = pl.ds((3 * dy + dx) * LANES, LANES)
                    start = r * chunk + (dy - 1) * side
                    low_at, high_at = max(start, 0), min(start + chunk, pixels)
                    shifted[pl.ds(low_at, high_at - low_at), lane] = value[
                        low_at - start : high_at - start, :
                    ]
        for dx in range(3):
            blank = jnp.zeros((side, LANES), BF16)
            shifted[pl.ds(pixels - side, side), pl.ds(dx * LANES, LANES)] = blank
            shifted[pl.ds(0, side), pl.ds((6 + dx) * LANES, LANES)] = blank
        factor = small[pl.ds(8 * s + 5, 1), :]
        g_style = jnp.zeros((width, LANES), F32)
        for first in range(0, TAPS, 2):
            count = min(2, TAPS - first)
            block = dot(feat_t[s], shifted[:, pl.ds(first * LANES, count * LANES)])
            for tap in range(first, first + count):
                raw = block[:, (tap - first) * LANES : (tap - first + 1) * LANES]
                weight = kernel[tap // 3, :, pl.ds((tap % 3) * LANES, LANES)].astype(F32)
                inner = raw - style_col * (weight * factor)
                g_style = g_style + weight * inner
                value = (style_col * inner).astype(BF16)
                top = tap * width
                for h in range(2):
                    low_at, high_at = max(top, h * half), min(top + width, (h + 1) * half)
                    if low_at < high_at:
                        slot = 1 - pair if h else pair
                        unit[s, slot, pl.ds(low_at - h * half, high_at - low_at), :] = value[
                            low_at - top : high_at - top, :
                        ]
        for at, value in ((0, g_style), (4, colour_aff * small[pl.ds(8 * s, 1), :])):
            row = jnp.sum(value.T, axis=0, keepdims=True)
            for part in range(width // LANES):
                to_sum[pl.ds(8 * s + at + part, 1), :] = row[:, part * LANES : (part + 1) * LANES]


def summed(parts, row):
    values = [part[pl.ds(row, 1), :] for part in parts]
    while len(values) > 1:
        values = [values[i] + values[i + 1] for i in range(0, len(values), 2)]
    return values[0]


def logit_grad(parts, masks, samples, s):
    at = 4 * samples * (s // samples) + s % samples
    logit = summed(parts, 8 * samples + at)
    mask = masks[pl.ds(at, 1), :]
    return -mask * jax.nn.sigmoid(-logit), mask * jax.nn.softplus(-logit), mask


def combine_kernel(n_ch, samples, *refs):
    parts, (masks, unit, unit_pair, out) = refs[:n_ch], refs[n_ch:]
    half = unit_pair.shape[1]
    grads, total = [], jnp.zeros((1, LANES), F32)
    for s in range(2 * samples):
        grad, _, mask = logit_grad(parts, masks, samples, s)
        grads.append(grad)
        total = total + mask
    block = half // 9
    for b in range(9):
        here = pl.ds(b * block, block)
        value = jnp.zeros((block, LANES), F32)
        for s in range(samples):
            value = value + grads[s] * unit[s, 0, here, :].astype(F32)
            value = value + grads[samples + s] * unit_pair[s, here, :].astype(F32)
        out[here, :] = value.astype(BF16)
    out[pl.ds(half, COUNT_ROWS), :] = jnp.broadcast_to(total, (COUNT_ROWS, LANES)).astype(BF16)


def pack_places(samples, layers):
    latents = 2 * samples
    style = 2 * layers * latents + latents
    colour = style + 2 * samples
    w_total = colour + 2 * samples
    return style, colour, w_total, -(-(w_total + 3) // 16) * 16


def mapping_back_kernel(n_ch, samples, where, crossover, *refs):
    parts = refs[:n_ch]
    masks, pre, hid, top, picked, small, map_full, aff_full, pack_out, rows, pack = refs[n_ch:]
    layers, _, width = map_full.shape
    latents = 2 * samples
    style_at, colour_at, w_at, _ = pack_places(samples, layers)
    ch = where[1]
    grads = [logit_grad(parts, masks, samples, s) for s in range(samples)]

    def wide_sum(at):
        return jnp.concatenate([summed(parts, at + part) for part in range(width // LANES)], axis=1)

    pack[...] = jnp.zeros_like(pack)

    def put(line, lane, size, value, count):
        for i, part in enumerate(pieces(value, count)):
            pack[pl.ds(line + i, 1), pl.ds(lane, size)] = part.astype(F32)

    style_rows = []
    half_lane = lax.broadcasted_iota(jnp.int32, (1, LANES), 1) < LANES // 2
    for s in range(samples):
        grad = grads[s][0]
        style_row = grad[:, :1] * wide_sum(8 * s)
        rows[pl.ds(s, 1), :] = style_row
        style_rows.append(style_row)
        own = rows[pl.ds(s, 1), pl.ds(pl.multiple_of(ch * LANES, LANES), LANES)]
        short = grad
        put(style_at + 2 * s, 0, LANES, own, 2)
        put(style_at + 2 * s, LANES, LANES, short * small[pl.ds(8 * s, 1), :], 2)
        put(style_at + 2 * s, 2 * LANES, LANES, short * small[pl.ds(8 * s + 1, 1), :], 2)
        loss_count = jnp.where(half_lane, grads[s][1], grads[s][2])
        put(style_at + 2 * s, 3 * LANES, LANES, loss_count, 2)
        for c in range(3):
            value = short * small[pl.ds(8 * s + 2 + c, 1), :]
            put(colour_at + 2 * s, c * LANES, LANES, value, 2)
        for j in range(2):
            line = 2 * layers * latents + 2 * s + j
            pack[pl.ds(line, 1), :] = picked[j, pl.ds(s, 1), :]
    w_total = top[pl.ds(0, 1), :]
    for n in range(1, latents):
        w_total = w_total + top[pl.ds(n, 1), :]
    put(w_at, 0, width, w_total, 3)

    def back(value, weights):
        hi, lo = pieces(value, 2)
        both = jnp.concatenate([hi.astype(F32), lo.astype(F32)], axis=0).astype(BF16)
        out = dot_nt(both, weights)
        return out[0:8] + out[8:16]

    pad = [jnp.zeros((8 - samples, width), F32)]
    from_conv = back(jnp.concatenate(style_rows + pad, axis=0), aff_full[...])
    g_rows = []
    for s in range(samples):
        conv_row = from_conv[s : s + 1, :]
        colour_row = grads[s][0][:, :1] * wide_sum(8 * s + 4)
        to_first = [jnp.full((1, width), crossover[s], jnp.int32) > j for j in range(2)]
        g_rows.append(
            jnp.where(to_first[0], conv_row, 0.0) + jnp.where(to_first[1], colour_row, 0.0)
        )
        g_rows.append(
            jnp.where(to_first[0], 0.0, conv_row) + jnp.where(to_first[1], 0.0, colour_row)
        )
    g_rows.append(jnp.zeros((8 - latents, width), F32))
    g_hidden = jnp.concatenate(g_rows, axis=0)
    for layer in reversed(range(layers)):
        g_pre = g_hidden * silu_slope(pre[layer])
        pack[pl.ds(layer * latents, latents), :] = g_pre[0:latents]
        pack[pl.ds((layers + layer) * latents, latents), :] = hid[layer][0:latents]
        if layer > 0:
            g_hidden = back(g_pre, map_full[layer])
    pack_out[...] = pack[...].astype(BF16)


def update_kernel(n_dp, samples, layers, places, where, *refs):
    packs, refs = refs[: len(places)], refs[len(places) :]
    (map_w, map_m, map_e, aff_w, aff_m, aff_e) = refs[:6]
    (map_b, map_bm, map_be, bias, bias_m, bias_e, rgb, rgb_m, rgb_e, w_avg) = refs[6:16]
    outs, refs = refs[16:39], refs[39:]
    map_new, aff_new, map_b_new, bias_new, rgb_new = (refs[4 * i : 4 * i + 4] for i in range(5))
    w_avg_new, loss_new, count_new, g_pre, hid, extra, sems = refs[20:]
    map_outs, aff_outs = outs[0:4], outs[4:8]
    map_b_outs, bias_outs, rgb_outs = outs[8:12], outs[12:16], outs[16:20]
    w_avg_out, loss_out, count_out = outs[20:23]
    latents = 2 * samples
    depth = layers * latents
    style_at, colour_at, w_at, lines = pack_places(samples, layers)
    style_at, colour_at, w_at = (at - 2 * depth for at in (style_at, colour_at, w_at))
    more = lines - 2 * depth
    dp = where[0]
    share, width = map_w.shape[1:]

    odd = lax.rem(dp, 2)
    for part, place in zip(packs, places):
        for index, (even_k, odd_k) in enumerate(place):
            owner = lax.bitwise_xor(dp, jnp.where(odd == 1, odd_k, even_k))
            top = index * lines
            for target, start, size in ((g_pre, 0, depth), (hid, depth, depth), (extra, 2 * depth, more)):
                at = pl.multiple_of(owner * size, size)
                target[pl.ds(at, size), :] = part[pl.ds(top + start, size), :]
    every = extra[...].astype(F32)
    kind = lax.rem(lax.broadcasted_iota(jnp.int32, every.shape, 0), more)

    def total_of(first, count):
        chosen = jnp.logical_and(kind >= first, kind < first + count)
        return jnp.sum(jnp.where(chosen, every, 0.0), axis=0, keepdims=True)

    total = total_of(style_at, 2 * samples)
    count = total[:, width - LANES // 2 : width - LANES // 2 + 1]
    inverse = 1.0 / count
    copies = []

    def send(buffers, targets, at, sem):
        for k, (buffer, target) in enumerate(zip(buffers, targets)):
            if at is not None:
                buffer, target = buffer.at[at], target.at[at]
            copy = pltpu.make_async_copy(buffer, target, sems.at[sem, k])
            copy.start()
            copies.append(copy)

    colour = total_of(colour_at, 2 * samples)
    for c in range(3):
        row = pl.ds(c, 1)
        lane = slice(c * LANES, (c + 1) * LANES)
        new = advance(bias[row, :], bias_m[row, :], bias_e[row, :], total[:, lane] * inverse, 50.0)
        for out, value in zip(bias_new[:3], new[:3]):
            out[row, :] = value
        new = advance(rgb[row, :], rgb_m[row, :], rgb_e[row, :], colour[:, lane] * inverse, 1.0)
        for out, value in zip(rgb_new[:3], new[:3]):
            out[row, :] = value
    bias_new[3][...] = bias_new[0][...].astype(BF16)
    rgb_new[3][...] = rgb_new[0][...].astype(BF16)
    mean = total_of(w_at, 3) * (1.0 / (n_dp * latents))
    w_avg_new[...] = w_avg[...] + (1.0 - AVERAGE_BETA) * (mean - w_avg[...])
    loss_new[0] = jnp.sum(total[:, width - LANES : width - LANES + 1])
    count_new[0] = jnp.sum(count)
    send(bias_new, bias_outs, None, layers // 2 + 2)
    send(rgb_new, rgb_outs, None, layers // 2 + 3)
    send((w_avg_new, loss_new, count_new), (w_avg_out, loss_out, count_out), None, layers // 2 + 4)

    own = pltpu.roll(hid[...].astype(F32), lax.rem(width - dp * share, width), 1)[:, :LANES]
    lane = lax.broadcasted_iota(jnp.int32, own.shape, 1)
    own = jnp.where(lane < share, own, jnp.where(lane == share, 1.0, 0.0))
    layer_of = lax.rem(lax.broadcasted_iota(jnp.int32, own.shape, 0), depth) // latents
    for layer in range(layers):
        mine = jnp.where(layer_of == layer, own, 0.0).astype(BF16)
        grads = dot_tn(mine, g_pre[...]) * inverse
        new = advance(map_w[layer], map_m[layer], map_e[layer], grads[0:share], 30.0)
        for out, value in zip(map_new, new):
            out[layer] = value
        row = pl.ds(layer, 1)
        new = advance(
            map_b[row, :], map_bm[row, :], map_be[row, :], grads[share : share + 1], 30.0
        )
        for out, value in zip(map_b_new[:3], new[:3]):
            out[row, :] = value
        if layer % 2:
            send(map_new, map_outs, pl.ds(layer - 1, 2), layer // 2)
    map_b_new[3][...] = map_b_new[0][...].astype(BF16)
    send(map_b_new, map_b_outs, None, layers // 2 + 5)
    for j in range(2):
        chosen = jnp.zeros(every.shape, F32)
        for piece in range(2):
            here = jnp.logical_and(kind >= style_at, kind < style_at + 2 * samples)
            here = jnp.logical_and(here, lax.rem(kind - style_at + 2, 2) == piece)
            moved = pltpu.roll(every, style_at + piece - j, 0)
            chosen = jnp.where(here, moved, chosen)
        grad = dot_tn(chosen.astype(BF16), extra[:, pl.ds(j * LANES, LANES)]) * inverse
        here = pl.ds(j * width, width)
        new = advance(aff_w[here, :], aff_m[here, :], aff_e[here, :], grad, 30.0)
        for out, value in zip(aff_new, new):
            out[here, :] = value
        send(aff_new, aff_outs, here, layers // 2 + j)
    for copy in copies:
        copy.wait()


def conv_kernel(turns, where, *refs):
    grads, refs = refs[: len(turns)], refs[len(turns) :]
    param, moment, average = refs[:3]
    outs, buffers, sems = refs[-9:-5], refs[-5:-1], refs[-1]
    half = grads[0].shape[0] - COUNT_ROWS
    depth = half // 9
    pair = lax.rem(where[0], 2)
    copies, at = [], 0
    for turn, (grad, (mine, ninths)) in enumerate(zip(grads, turns)):
        start = pl.multiple_of((pair if mine else 1 - pair) * half, half)
        inverse = 1.0 / grad[pl.ds(half, 16), :].astype(F32)[0:1]
        for n in ninths:
            here = pl.ds(at * depth, depth)
            there = pl.ds(pl.multiple_of(start + n * depth, depth), depth)
            at += 1
            value = grad[pl.ds(n * depth, depth), :].astype(F32) * inverse
            new = advance(param[there, :], moment[there, :], average[there, :], value, 5.0)
            for k in range(4):
                buffers[k][here, :] = new[k]
            if n % 3 == 2:
                for k in range(4):
                    copy = pltpu.make_async_copy(
                        buffers[k].at[pl.ds((at - 3) * depth, 3 * depth), :],
                        outs[k].at[pl.ds(pl.multiple_of(start + (n - 2) * depth, depth), 3 * depth), :],
                        sems.at[at // 3 - 1, k],
                    )
                    copy.start()
                    copies.append(copy)
    for copy in copies:
        copy.wait()


def local(
    features,
    z_table,
    seeds,
    crossover,
    counted,
    head,
    w_avg,
    map_w,
    map_w_mom,
    map_w_ema,
    map_b,
    map_b_mom,
    map_b_ema,
    aff_w,
    aff_w_mom,
    aff_w_ema,
    chan_bias,
    chan_bias_mom,
    chan_bias_ema,
    conv_w,
    conv_w_mom,
    conv_w_ema,
    rgb_w,
    rgb_w_mom,
    rgb_w_ema,
):
    samples, side = features.shape[0], features.shape[1]
    pixels = side * side
    layers, share, width = map_w.shape
    n_dp, n_ch = lax.axis_size("dp"), lax.axis_size("chan")
    latents = 2 * samples
    where = jnp.stack([lax.axis_index("dp"), lax.axis_index("chan")]).astype(jnp.int32)
    flat = lambda a: a.reshape(TAPS * width, LANES)

    half = width // 2
    pack_rows = samples * pixels + half + 16
    pack = pl.pallas_call(
        pack_kernel,
        out_shape=shape((pack_rows, LANES), BF16),
        in_specs=[SMEM] + [ANY] * 3,
        out_specs=VMEM,
        scratch_shapes=[
            pltpu.VMEM((half, LANES), F32),
            pltpu.VMEM(chan_bias.shape, F32),
            pltpu.SemaphoreType.DMA((3,)),
        ],
        compiler_params=params(4),
        cost_estimate=cost(1),
        name="pack",
    )(where, *hbm(aff_w, chan_bias, features.reshape(samples * pixels, LANES)))
    map_low = pl.pallas_call(
        low_kernel,
        out_shape=shape(map_w.shape, BF16),
        in_specs=[ANY],
        out_specs=VMEM,
        scratch_shapes=[pltpu.VMEM(map_w.shape, F32), pltpu.SemaphoreType.DMA((layers,))],
        compiler_params=params(8),
        cost_estimate=cost(1),
        name="low",
    )(*hbm(map_w))
    *chan_packs, last_step = spread_over_chan(pack, half + 16, map_low)
    blocks = spread_layers(map_low, "dp")
    kernel, square = pl.pallas_call(
        weights_kernel,
        out_shape=(shape((3, width, 3 * LANES), BF16), shape((width, LANES), F32)),
        in_specs=[ANY],
        out_specs=(VMEM, VMEM),
        scratch_shapes=[
            pltpu.VMEM((TAPS, width, LANES), F32),
            pltpu.SemaphoreType.DMA((TAPS,)),
        ],
        compiler_params=params(8),
        cost_estimate=cost(2),
        name="weights",
    )(*hbm(after(conv_w.reshape(TAPS, width, LANES), blocks[1][0])))
    second = last_step(blocks[2][0], kernel)
    places = [place for _, place in blocks]

    pre, hid, top, picked, map_full = pl.pallas_call(
        functools.partial(mapping_kernel, n_dp, samples, places),
        out_shape=(
            shape((layers, 8, width), F32),
            shape((layers, 8, width), F32),
            shape((8, width), F32),
            shape((2, 8, width), F32),
            shape((layers, width, width), BF16),
        ),
        in_specs=[SMEM] * 3 + [VMEM] * len(blocks) + [ANY, VMEM],
        out_specs=(VMEM,) * 5,
        scratch_shapes=[
            pltpu.VMEM((latents, 8, width), F32),
            pltpu.SemaphoreType.DMA((len(places),)),
            pltpu.SemaphoreType.DMA((latents,)),
        ],
        compiler_params=params(12),
        cost_estimate=cost(1),
        name="mapping",
    )(where, seeds.reshape(-1), crossover, *[block for block, _ in blocks], *hbm(z_table), map_b)

    both, first, first_pair = chan_packs
    feat_t, taps, style_rows, aff_full = pl.pallas_call(
        functools.partial(begin_kernel, n_ch, samples, side),
        out_shape=(
            shape((samples, width, pixels), BF16),
            shape((samples, pixels, 3 * LANES), F32),
            shape((8, width), F32),
            shape((width, width), BF16),
        ),
        in_specs=[SMEM] + [VMEM] * 5,
        out_specs=(VMEM,) * 4,
        scratch_shapes=[
            pltpu.VMEM((16, LANES), F32),
            pltpu.VMEM((samples, pixels + 2 * side, width), BF16),
        ],
        compiler_params=params(16),
        cost_estimate=cost(3),
        name="begin",
    )(where, both, first, first_pair, kernel, picked)
    second_pair = swap(after(second, taps)[samples * pixels :], "dp", 1)
    feat_t, style_rows, aff_full, wide, small, loss_rows = pl.pallas_call(
        functools.partial(main_kernel, n_ch, samples, side),
        out_shape=(
            shape((samples, width, pixels), BF16),
            shape((8, width), F32),
            shape((width, width), BF16),
            shape((samples, pixels + 16, LANES), F32),
            shape((8 * samples, LANES), F32),
            shape((8 * samples, LANES), F32),
        ),
        in_specs=[SMEM] + [VMEM] * 10 + [SMEM] + [VMEM] * 3,
        out_specs=(VMEM,) * 6,
        scratch_shapes=[
            pltpu.VMEM((16, LANES), F32),
            pltpu.VMEM((pack_rows, LANES), BF16),
            pltpu.VMEM((half + 16, LANES), BF16),
            pltpu.VMEM((samples, pixels + 2 * side, LANES), BF16),
            pltpu.VMEM((pixels + 16, 3 * LANES), F32),
        ],
        input_output_aliases={12: 0, 13: 1, 14: 2},
        compiler_params=params(20),
        cost_estimate=cost(3),
        name="main",
    )(
        where,
        second,
        second_pair,
        taps,
        kernel,
        square,
        aff_w,
        picked,
        chan_bias,
        head,
        rgb_w,
        counted,
        feat_t,
        style_rows,
        aff_full,
    )
    pair_losses = swap(loss_rows, "dp", 1)
    unit, to_sum = pl.pallas_call(
        functools.partial(factor_kernel, samples, side),
        out_shape=(
            shape((samples, 2, TAPS * width // 2, LANES), BF16),
            shape((8 * samples, LANES), F32),
        ),
        in_specs=[SMEM] + [VMEM] * 6,
        out_specs=(VMEM,) * 2,
        scratch_shapes=[pltpu.VMEM((pixels, TAPS * LANES), BF16)],
        compiler_params=params(16),
        cost_estimate=cost(2),
        name="factor",
    )(where, feat_t, wide, small, style_rows, kernel, aff_w)
    unit_pair = swap(unit[:, 1], "dp", 1)

    to_send = jnp.concatenate([to_sum, loss_rows[:4 * samples], pair_losses[:4 * samples]])
    sum_parts = spread_direct(to_send, "chan")
    masks = jnp.concatenate([loss_rows[4 * samples:], pair_losses[4 * samples:]])
    half_rows = TAPS * width // 2 + COUNT_ROWS
    total = pl.pallas_call(
        functools.partial(combine_kernel, n_ch, samples),
        out_shape=shape((half_rows, LANES), BF16),
        in_specs=[VMEM] * (n_ch + 3),
        out_specs=VMEM,
        compiler_params=params(8),
        cost_estimate=cost(1),
        name="combine",
    )(*sum_parts, masks, unit, unit_pair)

    lines = pack_places(samples, layers)[-1]
    pack = pl.pallas_call(
        functools.partial(mapping_back_kernel, n_ch, samples),
        out_shape=shape((lines, width), BF16),
        in_specs=[SMEM] * 2 + [VMEM] * (n_ch + 8),
        out_specs=VMEM,
        scratch_shapes=[pltpu.VMEM((8, width), F32), pltpu.VMEM((lines, width), F32)],
        compiler_params=params(12),
        cost_estimate=cost(2),
        name="mapping_back",
    )(where, crossover, *after(sum_parts, total), masks, pre, hid, top, picked, small, map_full, aff_full)
    spread_pack = spread(pack, "dp")
    packs = [part for part, _ in spread_pack]

    flat_aff = [a.reshape(2 * width, LANES) for a in (aff_w, aff_w_mom, aff_w_ema)]
    tiny = [
        map_b,
        map_b_mom,
        map_b_ema,
        chan_bias,
        chan_bias_mom,
        chan_bias_ema,
        rgb_w,
        rgb_w_mom,
        rgb_w_ema,
        w_avg.reshape(1, width),
    ]
    types = (F32, F32, F32, BF16)
    out_shape = (
        [shape(map_w.shape, t) for t in types]
        + [shape((2 * width, LANES), t) for t in types]
        + [shape(map_b.shape, t) for t in types]
        + [shape(chan_bias.shape, t) for t in types]
        + [shape(rgb_w.shape, t) for t in types]
        + [shape((1, width), F32), shape((1,), F32), shape((1,), F32)]
    )
    depth = layers * latents
    update = lambda: pl.pallas_call(
        functools.partial(update_kernel, n_dp, samples, layers, [p for _, p in spread_pack]),
        out_shape=out_shape,
        in_specs=[SMEM] + [VMEM] * (len(packs) + 6 + len(tiny)),
        out_specs=[ANY] * 23,
        scratch_shapes=[pltpu.VMEM(s.shape, s.dtype) for s in out_shape[:21]]
        + [
            pltpu.SMEM((1,), F32),
            pltpu.SMEM((1,), F32),
            pltpu.VMEM((n_dp * depth, width), BF16),
            pltpu.VMEM((n_dp * depth, width), BF16),
            pltpu.VMEM((n_dp * (lines - 2 * depth), width), BF16),
            pltpu.SemaphoreType.DMA((layers // 2 + 6, 4)),
        ],
        compiler_params=params(20),
        cost_estimate=cost(4),
        name="update",
    )(where, *packs, map_w, map_w_mom, map_w_ema, *flat_aff, *tiny)

    bits = [1 << b for b in range(1, n_dp.bit_length() - 1)]
    for turn, (even_bit, odd_bit) in enumerate(zip(bits, bits[::-1])):
        got = crossed(total, "dp", even_bit, odd_bit)
        if turn == len(bits) - 2:
            got = after(got, packs[1])
        if turn == len(bits) - 1:
            outs = update()
            got = after(got, *outs)
        total = (total.astype(F32) + got.astype(F32)).astype(BF16)
    other = swap(total, "dp", 1)

    conv_params = [flat(conv_w), flat(conv_w_mom), flat(conv_w_ema)]

    def conv_part(turns, grads, earlier):
        ninths = sum(len(n) for _, n in turns)
        return pl.pallas_call(
            functools.partial(conv_kernel, turns),
            out_shape=[shape((TAPS * width, LANES), t) for t in types],
            in_specs=[SMEM] + [VMEM] * (len(grads) + 3) + [ANY] * len(earlier),
            out_specs=[ANY] * 4,
            scratch_shapes=[pltpu.VMEM((ninths * TAPS * width // 18, LANES), t) for t in types]
            + [pltpu.SemaphoreType.DMA((ninths // 3, 4))],
            input_output_aliases={4 + len(grads) + k: k for k in range(len(earlier))},
            compiler_params=params(16),
            cost_estimate=cost(2),
            name="conv_rest" if earlier else "conv_first",
        )(where, *grads, *conv_params, *earlier)

    first_part = conv_part([(True, range(6))], [total], [])
    conv_outs = conv_part([(True, range(6, 9)), (False, range(9))], [total, other], first_part)

    map_outs, aff_outs = outs[0:4], [a.reshape(aff_w.shape) for a in outs[4:8]]
    conv_outs = [a.reshape(conv_w.shape) for a in conv_outs]
    return (
        *map_outs,
        *outs[8:12],
        *aff_outs,
        *outs[12:16],
        *conv_outs,
        *outs[16:20],
        outs[20].reshape(width),
        outs[21].reshape(()),
        outs[22].reshape(()),
    )


def solution(mesh):
    in_specs = (
        P("dp", None, None, "chan"),
        P(),
        P("dp", None),
        P("dp"),
        P("dp"),
        P(),
        P(),
        P(None, "dp", None),
        P(None, "dp", None),
        P(None, "dp", None),
        P(),
        P(),
        P(),
        P(None, None, "chan"),
        P(None, None, "chan"),
        P(None, None, "chan"),
        P(None, "chan"),
        P(None, "chan"),
        P(None, "chan"),
        P(None, None, None, "chan"),
        P(None, None, None, "chan"),
        P(None, None, None, "chan"),
        P(None, "chan"),
        P(None, "chan"),
        P(None, "chan"),
    )
    out_specs = (
        P(None, "dp", None),
        P(None, "dp", None),
        P(None, "dp", None),
        P(None, "dp", None),
        P(),
        P(),
        P(),
        P(),
        P(None, None, "chan"),
        P(None, None, "chan"),
        P(None, None, "chan"),
        P(None, None, "chan"),
        P(None, "chan"),
        P(None, "chan"),
        P(None, "chan"),
        P(None, "chan"),
        P(None, None, None, "chan"),
        P(None, None, None, "chan"),
        P(None, None, None, "chan"),
        P(None, None, None, "chan"),
        P(None, "chan"),
        P(None, "chan"),
        P(None, "chan"),
        P(None, "chan"),
        P(),
        P(),
        P(),
    )
    return jax.shard_map(local, mesh=mesh, in_specs=in_specs, out_specs=out_specs, check_vma=False)
```

```python
import functools

import jax
import jax.numpy as jnp
from jax import lax
from jax.experimental import pallas as pl
from jax.experimental.pallas import tpu as pltpu
from jax.sharding import PartitionSpec as P

MOMENTUM = 0.9
EMA_DECAY = 0.95
AVERAGE_BETA = 0.5
BF16 = jnp.bfloat16
F32 = jnp.float32
TAPS = 9
LANES = 128
COUNT_ROWS = 32
VMEM = pl.BlockSpec(memory_space=pltpu.VMEM)
SMEM = pl.BlockSpec(memory_space=pltpu.SMEM)
ANY = pl.BlockSpec(memory_space=pl.ANY)


def shape(dims, dtype):
    return jax.ShapeDtypeStruct(dims, dtype)


def params(mib):
    return pltpu.CompilerParams(vmem_limit_bytes=mib * 1024 * 1024)


def cost(micros):
    return pl.CostEstimate(flops=int(micros * 1e9), bytes_accessed=0, transcendentals=0)


def hbm(*values):
    return [pltpu.with_memory_space_constraint(value, pltpu.HBM) for value in values]


def after(values, *others):
    return lax.optimization_barrier((values, others))[0]


def swap(value, axis, distance):
    return lax.ppermute(
        value, axis, [(i, i ^ distance) for i in range(lax.axis_size(axis))]
    )


def spread(value, axis):
    size = lax.axis_size(axis)
    beside = swap(value, axis, 1)
    if size != 8:
        parts = [(value, [(0, 0)]), (beside, [(1, 1)])]
        for k in range(2, size, 2):
            part = swap(value, axis, k)
            parts += [(part, [(k, k)]), (swap(part, axis, 1), [(k + 1, k + 1)])]
        return parts
    near = jnp.concatenate([value, beside])
    far = crossed(near, axis, 4, 2)
    corner = crossed(far, axis, 2, 4)
    return [
        (near, [(0, 0), (1, 1)]),
        (far, [(4, 2), (5, 3)]),
        (corner, [(6, 6), (7, 7)]),
        (swap(far, axis, 1), [(3, 5), (2, 4)]),
    ]


def spread_direct(value, axis):
    return [value] + [swap(value, axis, k) for k in range(1, lax.axis_size(axis))]


def spread_over_chan(features, pack, ready):
    n_dp, n_ch = lax.axis_size("dp"), lax.axis_size("chan")
    cut = features.shape[0]
    both = lax.optimization_barrier(jnp.concatenate([pack, swap(features, "dp", 1)]))

    def joint(value, moves):
        pairs = [
            (d * n_ch + a, d * n_ch + b) for d in range(n_dp) for a, b in moves[d % 2]
        ]
        return lax.ppermute(value, ("dp", "chan"), pairs)

    first = joint(both, ([(c, c ^ 1) for c in range(4)], [(c, c ^ 2) for c in range(4)]))
    first_pair = swap(first[cut:], "dp", 1)
    odd = lax.rem(lax.axis_index("dp"), 2) == 1

    def last_step(*others):
        value = after(jnp.where(odd, first, both), *others)
        return joint(value, ([(1, 2), (2, 1)], [(1, 0), (2, 3)]))

    return both, first, first_pair, last_step


def crossed(value, axis, even_distance, odd_distance):
    size = lax.axis_size(axis)
    pairs = [(i, i ^ (odd_distance if i % 2 else even_distance)) for i in range(size)]
    return lax.ppermute(value, axis, pairs)


def spread_layers(value, axis):
    size = lax.axis_size(axis)
    beside = swap(value, axis, 1)
    parts = [(value, (0, 0, 0)), (beside, (0, 1, 1))]
    if size != 8:
        for k in range(2, size, 2):
            part = swap(value, axis, k)
            parts += [(part, (0, k, k)), (swap(part, axis, 1), (0, k + 1, k + 1))]
        return parts
    far = crossed(value, axis, 2, 4)
    far_beside = crossed(beside, axis, 2, 4)
    corner = crossed(far, axis, 4, 2)
    parts += [(far, (0, 2, 4)), (far_beside, (0, 3, 5)), (corner, (0, 6, 6))]
    parts += [(swap(far, axis, 1), (0, 5, 3)), (swap(far_beside, axis, 1), (0, 4, 2))]
    parts += [(swap(corner, axis, 1), (0, 7, 7))]
    return parts


def silu_slope(preact):
    sig = jax.nn.sigmoid(preact)
    return sig * (1.0 + preact * (1.0 - sig))


def pieces(value, count):
    out = []
    for _ in range(count):
        part = value.astype(BF16)
        out.append(part)
        value = value - part.astype(F32)
    return out


def advance(param, moment, average, grad, rate):
    moment_new = MOMENTUM * moment + grad
    param_new = param - rate * (grad + MOMENTUM * moment_new)
    average_new = EMA_DECAY * average + (1.0 - EMA_DECAY) * param_new
    return param_new, moment_new, average_new, param_new.astype(BF16)


def dot(a, b):
    return jnp.dot(a, b, preferred_element_type=F32)


def dot_nt(a, b):
    return lax.dot_general(a, b, (((1,), (1,)), ((), ())), preferred_element_type=F32)


def dot_tn(a, b):
    return lax.dot_general(a, b, (((0,), (0,)), ((), ())), preferred_element_type=F32)


def pack_kernel(where, aff_w, bias, features, pack, aff_stage, bias_stage, sems):
    half = aff_stage.shape[0] // 2
    rows = features.shape[0]
    pair = lax.rem(where[0], 2)
    feat_copy = pltpu.make_async_copy(features, pack.at[pl.ds(0, rows), :], sems.at[0])
    aff_copy = pltpu.make_async_copy(aff_w.at[0], aff_stage, sems.at[1])
    bias_copy = pltpu.make_async_copy(bias, bias_stage, sems.at[2])
    for copy in (feat_copy, aff_copy, bias_copy):
        copy.start()
    bias_copy.wait()
    hi, mid, lo = pieces(bias_stage[0:1, :], 3)
    lines = jnp.concatenate(
        [hi.astype(F32), mid.astype(F32), lo.astype(F32), jnp.zeros((13, LANES), F32)], axis=0
    )
    aff_copy.wait()
    for turn, owner in enumerate((pair, 1 - pair)):
        at = rows + turn * (half + 16)
        start = pl.multiple_of(owner * half, half)
        pack[pl.ds(at, half), :] = aff_stage[pl.ds(start, half), :].astype(BF16)
        pack[pl.ds(at + half, 16), :] = lines.astype(BF16)
    feat_copy.wait()


def low_kernel(map_w, map_low, stage, sems):
    layers = map_w.shape[0]
    copies = [
        pltpu.make_async_copy(map_w.at[layer], stage.at[layer], sems.at[layer])
        for layer in range(layers)
    ]
    for copy in copies:
        copy.start()
    for layer in range(layers):
        copies[layer].wait()
        map_low[layer] = stage[layer].astype(BF16)


def mapping_kernel(n_dp, samples, places, *refs):
    refs = list(refs)

    def take(count):
        got = refs[:count]
        del refs[:count]
        return got

    where, crossover = take(2)
    parts = take(len(places))
    latent_rows, map_b = take(2)
    pre_out, hid_out, top_out, picked_out, map_full, sem_map = refs
    layers, share, width = parts[0].shape
    dp = where[0]
    odd = lax.rem(dp, 2)
    moves = []
    for part, (first, even_k, odd_k) in zip(parts, places):
        k = jnp.where(odd == 1, odd_k, even_k)
        at = pl.multiple_of(lax.bitwise_xor(dp, k) * share, share)
        moves.append((part, first, pl.ds(at, share)))
    whole_tiles = share % 16 == 0
    if not whole_tiles:
        copies = [
            pltpu.make_async_copy(
                part, map_full.at[pl.ds(first, part.shape[0]), at, :], sem_map.at[i]
            )
            for i, (part, first, at) in enumerate(moves)
        ]
        for copy in copies:
            copy.start()
        for copy in copies:
            copy.wait()

    def bring(layer):
        for part, first, at in moves:
            if whole_tiles and first <= layer < first + part.shape[0]:
                map_full[layer, at, :] = part[layer - first]

    bring(0)
    bring(1)
    hidden = latent_rows[...]
    for layer in range(layers):
        low = hidden.astype(BF16)
        preact = dot(low, map_full[layer]) + map_b[pl.ds(layer, 1), :]
        if layer + 2 < layers:
            bring(layer + 2)
        hid_out[layer] = low.astype(F32)[0:8]
        pre_out[layer] = preact[0:8]
        hidden = preact * jax.nn.sigmoid(preact)
    top_out[...] = hidden[0:8]
    low = hidden.astype(BF16).astype(F32)
    for j in range(2):
        chosen = []
        for s in range(samples):
            first = crossover[s] > j
            chosen.append(
                jnp.where(first, low[2 * s : 2 * s + 1, :], low[2 * s + 1 : 2 * s + 2, :])
            )
        chosen.append(jnp.zeros((8 - samples, width), F32))
        picked_out[j] = jnp.concatenate(chosen, axis=0)


def weights_kernel(samples, seeds, conv_w, z_table, kernel, square, latent_rows, stage, rows, sems, sem_z):
    latents = 2 * samples
    z_copies = []
    for n in range(latents):
        at = pl.multiple_of((seeds[n] // 8) * 8, 8)
        z_copies.append(pltpu.make_async_copy(z_table.at[pl.ds(at, 8), :], rows.at[n], sem_z.at[n]))
    copies = [pltpu.make_async_copy(conv_w.at[t], stage.at[t], sems.at[t]) for t in range(TAPS)]
    for copy in z_copies + copies:
        copy.start()
    total = jnp.zeros(square.shape, F32)
    for tap in range(TAPS):
        copies[tap].wait()
        low = stage[tap].astype(BF16)
        kernel[tap // 3, :, pl.ds((tap % 3) * LANES, LANES)] = low
        wide = low.astype(F32)
        total = total + wide * wide
    square[...] = total
    normed = []
    for n in range(latents):
        z_copies[n].wait()
        row = rows[n, pl.ds(lax.rem(seeds[n], 8), 1), :]
        scale = lax.rsqrt(jnp.mean(row * row, axis=1, keepdims=True) + 1e-08)
        normed.append(row * scale)
    normed.append(jnp.zeros((16 - latents, rows.shape[2]), F32))
    latent_rows[...] = jnp.concatenate(normed, axis=0)


def bring_blocks(blocks, samples, side, where, picked, bias_full, style_rows, feat_t, aff_full, padded):
    width = aff_full.shape[0]
    half, pixels = width // 2, side * side
    dp, ch = where[0], where[1]
    pair = lax.rem(dp, 2)
    mine = pl.ds(pl.multiple_of(pair * half, half), half)
    other = pl.ds(pl.multiple_of((1 - pair) * half, half), half)
    chosen = picked[0].astype(BF16)
    for source, top, tail_at, other_source, other_tail_at, k in blocks:
        lane = pl.ds(pl.multiple_of(lax.bitwise_xor(ch, k) * LANES, LANES), LANES)
        aff_full[mine, lane] = source[pl.ds(tail_at, half), :]
        aff_full[other, lane] = other_source[pl.ds(other_tail_at, half), :]
        bias_full[...] = source[pl.ds(tail_at + half, 16), :].astype(F32)
        bias_row = bias_full[0:1, :] + bias_full[1:2, :] + bias_full[2:3, :]
        style = (dot(chosen, aff_full[:, lane]) + bias_row).astype(BF16)
        style_rows[:, lane] = style.astype(F32)
        for s in range(samples):
            value = source[pl.ds(top + s * pixels, pixels), :]
            feat_t[s, lane, :] = value.T
            padded[s, pl.ds(side, pixels), lane] = value * style[s : s + 1, :]


def begin_kernel(n_ch, samples, side, *refs):
    where, both, first, first_pair, kernel, picked = refs[:6]
    feat_t, taps, style_rows, aff_full, bias_full, padded = refs[6:]
    width = aff_full.shape[0]
    half, pixels = width // 2, side * side
    feats, tail_rows = samples * pixels, half + 16
    cut = first.shape[0] - first_pair.shape[0]
    partner_tail, partner_feats = feats + tail_rows, feats + 2 * tail_rows
    pair = lax.rem(where[0], 2)
    last = pl.ds(pl.multiple_of(lax.bitwise_xor(where[1], 3) * LANES, LANES), LANES)
    for s in range(samples):
        padded[s, pl.ds(0, side), :] = jnp.zeros((side, width), BF16)
        padded[s, pl.ds(side + pixels, side), :] = jnp.zeros((side, width), BF16)
        padded[s, pl.ds(side, pixels), last] = jnp.zeros((pixels, LANES), BF16)
    style_rows[...] = jnp.zeros_like(style_rows)
    blocks = (
        (both, 0, feats, both, partner_tail, 0),
        (first, 0, feats, first, partner_tail, 1 + pair),
        (first_pair, partner_feats - cut, partner_tail - cut, first_pair, feats - cut, 2 - pair),
    )
    bring_blocks(
        blocks, samples, side, where, picked, bias_full, style_rows, feat_t, aff_full, padded
    )
    chunk = min(256, pixels)
    for s in range(samples):
        for r in range(pixels // chunk):
            total = dot(padded[s, pl.ds(r * chunk, chunk), :], kernel[0])
            total = total + dot(padded[s, pl.ds(side + r * chunk, chunk), :], kernel[1])
            total = total + dot(padded[s, pl.ds(2 * side + r * chunk, chunk), :], kernel[2])
            taps[s, pl.ds(r * chunk, chunk), :] = total


def main_kernel(n_ch, samples, side, *refs):
    where, second, second_pair, earlier, kernel, square_in = refs[:6]
    aff_w, picked, bias, head, rgb_w, counted = refs[6:12]
    feat_t, style_rows, aff_full, wide, small, loss_rows = refs[15:21]
    bias_full, late, late_tail, padded, taps = refs[21:]
    width = aff_full.shape[0]
    half, pixels = width // 2, side * side
    feats, tail_rows = samples * pixels, half + 16
    cut = second.shape[0] - second_pair.shape[0]
    partner_tail, partner_feats = feats + tail_rows, feats + 2 * tail_rows
    dp, ch = where[0], where[1]
    pair = lax.rem(dp, 2)
    at_end = jnp.logical_or(ch == 0, ch == n_ch - 1)
    is_held = at_end == (pair == 1)

    @pl.when(is_held)
    def _():
        late[...] = second[pl.ds(0, feats + tail_rows), :]
        late_tail[...] = second[pl.ds(partner_tail, tail_rows), :]

    @pl.when(jnp.logical_not(is_held))
    def _():
        late[pl.ds(0, feats), :] = second_pair[pl.ds(partner_feats - cut, feats), :]
        late[pl.ds(feats, tail_rows), :] = second_pair[pl.ds(partner_tail - cut, tail_rows), :]
        late_tail[...] = second_pair[pl.ds(feats - cut, tail_rows), :]

    for s in range(samples):
        padded[s, pl.ds(0, side), :] = jnp.zeros((side, LANES), BF16)
        padded[s, pl.ds(side + pixels, side), :] = jnp.zeros((side, LANES), BF16)
    mine = pl.ds(pl.multiple_of(pair * half, half), half)
    other = pl.ds(pl.multiple_of((1 - pair) * half, half), half)
    lane = pl.ds(pl.multiple_of(lax.bitwise_xor(ch, 3) * LANES, LANES), LANES)
    aff_full[mine, lane] = late[pl.ds(feats, half), :]
    aff_full[other, lane] = late_tail[pl.ds(0, half), :]
    bias_full[...] = late[pl.ds(feats + half, 16), :].astype(F32)
    bias_row = bias_full[0:1, :] + bias_full[1:2, :] + bias_full[2:3, :]
    style = (dot(picked[0].astype(BF16), aff_full[:, lane]) + bias_row).astype(BF16)
    style_rows[:, lane] = style.astype(F32)
    for s in range(samples):
        value = late[pl.ds(s * pixels, pixels), :]
        feat_t[s, lane, :] = value.T
        padded[s, pl.ds(side, pixels), :] = value * style[s : s + 1, :]
    square = square_in[...]
    colour_aff = aff_w[1].astype(BF16)
    style1 = dot(picked[1].astype(BF16), colour_aff) + bias[1:2, :]
    style1 = style1.astype(BF16).astype(F32)
    colour = rgb_w[...].astype(BF16)
    colour_wide = colour.astype(F32)
    colour_rows = jnp.concatenate([colour_wide, jnp.zeros((13, LANES), F32)], axis=0).astype(BF16)
    head_rows = jnp.concatenate(
        [head[...].astype(F32), jnp.zeros((13, pixels), F32)], axis=0
    ).astype(BF16)
    conv_bias = bias[2:3, :]
    chunk = min(256, pixels)
    steps = pixels // chunk
    column = lax.rem(lax.broadcasted_iota(jnp.int32, (chunk, LANES), 0), side)
    not_first, not_last = column > 0, column < side - 1
    small[...] = jnp.zeros_like(small)
    loss_rows[...] = jnp.zeros_like(loss_rows)
    taps[pl.ds(0, 8), :] = jnp.zeros((8, 3 * LANES), F32)
    taps[pl.ds(8 + pixels, 8), :] = jnp.zeros((8, 3 * LANES), F32)

    for s in range(samples):
        wide[s, pl.ds(0, 8), :] = jnp.zeros((8, LANES), F32)
        wide[s, pl.ds(8 + pixels, 8), :] = jnp.zeros((8, LANES), F32)
        style_col = jnp.broadcast_to(style_rows[pl.ds(s, 1), :], (LANES, width)).T
        demod = lax.rsqrt(
            jnp.sum(style_col * style_col * square, axis=0, keepdims=True) + 1e-08
        )
        style_colour = style1[s : s + 1, :]
        for r in range(steps):
            total = earlier[s, pl.ds(r * chunk, chunk), :]
            for dy in range(3):
                total = total + dot(
                    padded[s, pl.ds(dy * side + r * chunk, chunk), :], kernel[dy, lane, :]
                )
            taps[pl.ds(8 + r * chunk, chunk), :] = total
        mixed = jnp.zeros((3, LANES), F32)
        g_style1 = jnp.zeros((1, LANES), F32)
        g_bias = jnp.zeros((1, LANES), F32)
        g_demod = jnp.zeros((1, LANES), F32)
        for r in range(steps):
            left = taps[pl.ds(7 + r * chunk, chunk), pl.ds(0, LANES)]
            centre = taps[pl.ds(8 + r * chunk, chunk), pl.ds(LANES, LANES)]
            right = taps[pl.ds(9 + r * chunk, chunk), pl.ds(2 * LANES, LANES)]
            conv_out = centre + jnp.where(not_first, left, 0.0) + jnp.where(not_last, right, 0.0)
            scaled = conv_out * demod + conv_bias
            sig = jax.nn.sigmoid(scaled)
            activated = scaled * sig
            act_mod = (activated * style_colour).astype(BF16)
            mixed = mixed + dot(head_rows[:, r * chunk : (r + 1) * chunk], act_mod)[0:3]
            g_act = dot_tn(head_rows[:, r * chunk : (r + 1) * chunk], colour_rows)
            g_style1 = g_style1 + jnp.sum(g_act * activated, axis=0, keepdims=True)
            g_scaled = g_act * style_colour * (sig * (1.0 + scaled * (1.0 - sig)))
            g_bias = g_bias + jnp.sum(g_scaled, axis=0, keepdims=True)
            g_demod = g_demod + jnp.sum(g_scaled * conv_out, axis=0, keepdims=True)
            wide[s, pl.ds(8 + r * chunk, chunk), :] = g_scaled * demod
        logit = jnp.sum(
            jnp.sum(mixed * colour_wide, axis=0, keepdims=True), axis=1, keepdims=True
        )
        loss_rows[pl.ds(s, 1), :] = jnp.broadcast_to(logit, (1, LANES))
        loss_rows[pl.ds(4 * samples + s, 1), :] = jnp.full((1, LANES), counted[s], jnp.int32).astype(F32)
        small[pl.ds(8 * s, 1), :] = g_style1
        small[pl.ds(8 * s + 1, 1), :] = g_bias
        small[pl.ds(8 * s + 2, 3), :] = mixed
        small[pl.ds(8 * s + 5, 1), :] = g_demod * demod * demod * demod


def factor_kernel(samples, side, where, feat_t, wide, small, style_rows, kernel, aff_w, unit, to_sum, shifted):
    width = feat_t.shape[1]
    pixels = side * side
    pair = lax.rem(where[0], 2)
    half = TAPS * width // 2
    chunk = min(256, pixels)
    steps = pixels // chunk
    column = lax.rem(lax.broadcasted_iota(jnp.int32, (chunk, LANES), 0), side)
    not_first, not_last = column > 0, column < side - 1
    to_sum[...] = jnp.zeros_like(to_sum)
    colour_aff = aff_w[1].astype(BF16).astype(F32)
    for s in range(samples):
        style_col = jnp.broadcast_to(style_rows[pl.ds(s, 1), :], (LANES, width)).T
        for r in range(steps):
            before = jnp.where(not_last, wide[s, pl.ds(9 + r * chunk, chunk), :], 0.0)
            centre = wide[s, pl.ds(8 + r * chunk, chunk), :]
            after_it = jnp.where(not_first, wide[s, pl.ds(7 + r * chunk, chunk), :], 0.0)
            for dx, value in enumerate((before, centre, after_it)):
                value = value.astype(BF16)
                for dy in range(3):
                    lane = pl.ds((3 * dy + dx) * LANES, LANES)
                    start = r * chunk + (dy - 1) * side
                    low_at, high_at = max(start, 0), min(start + chunk, pixels)
                    shifted[pl.ds(low_at, high_at - low_at), lane] = value[
                        low_at - start : high_at - start, :
                    ]
        for dx in range(3):
            blank = jnp.zeros((side, LANES), BF16)
            shifted[pl.ds(pixels - side, side), pl.ds(dx * LANES, LANES)] = blank
            shifted[pl.ds(0, side), pl.ds((6 + dx) * LANES, LANES)] = blank
        factor = small[pl.ds(8 * s + 5, 1), :]
        g_style = jnp.zeros((width, LANES), F32)
        for first in range(0, TAPS, 2):
            count = min(2, TAPS - first)
            block = dot(feat_t[s], shifted[:, pl.ds(first * LANES, count * LANES)])
            for tap in range(first, first + count):
                raw = block[:, (tap - first) * LANES : (tap - first + 1) * LANES]
                weight = kernel[tap // 3, :, pl.ds((tap % 3) * LANES, LANES)].astype(F32)
                inner = raw - style_col * (weight * factor)
                g_style = g_style + weight * inner
                value = (style_col * inner).astype(BF16)
                top = tap * width
                for h in range(2):
                    low_at, high_at = max(top, h * half), min(top + width, (h + 1) * half)
                    if low_at < high_at:
                        slot = 1 - pair if h else pair
                        unit[s, slot, pl.ds(low_at - h * half, high_at - low_at), :] = value[
                            low_at - top : high_at - top, :
                        ]
        for at, value in ((0, g_style), (4, colour_aff * small[pl.ds(8 * s, 1), :])):
            row = jnp.sum(value.T, axis=0, keepdims=True)
            for part in range(width // LANES):
                to_sum[pl.ds(8 * s + at + part, 1), :] = row[:, part * LANES : (part + 1) * LANES]


def summed(parts, row):
    values = [part[pl.ds(row, 1), :] for part in parts]
    while len(values) > 1:
        values = [values[i] + values[i + 1] for i in range(0, len(values), 2)]
    return values[0]


def logit_grad(parts, masks, samples, s):
    at = 4 * samples * (s // samples) + s % samples
    logit = summed(parts, 8 * samples + at)
    mask = masks[pl.ds(at, 1), :]
    return -mask * jax.nn.sigmoid(-logit), mask * jax.nn.softplus(-logit), mask


def combine_kernel(n_ch, samples, *refs):
    parts, (masks, unit, unit_pair, out) = refs[:n_ch], refs[n_ch:]
    half = unit_pair.shape[1]
    grads, total = [], jnp.zeros((1, LANES), F32)
    for s in range(2 * samples):
        grad, _, mask = logit_grad(parts, masks, samples, s)
        grads.append(grad)
        total = total + mask
    block = half // 9
    for b in range(9):
        here = pl.ds(b * block, block)
        value = jnp.zeros((block, LANES), F32)
        for s in range(samples):
            value = value + grads[s] * unit[s, 0, here, :].astype(F32)
            value = value + grads[samples + s] * unit_pair[s, here, :].astype(F32)
        out[here, :] = value.astype(BF16)
    out[pl.ds(half, COUNT_ROWS), :] = jnp.broadcast_to(total, (COUNT_ROWS, LANES)).astype(BF16)


def pack_places(samples, layers):
    latents = 2 * samples
    style = 2 * layers * latents + latents
    colour = style + 2 * samples
    w_total = colour + 2 * samples
    return style, colour, w_total, -(-(w_total + 3) // 16) * 16


def mapping_back_kernel(n_ch, samples, where, crossover, *refs):
    parts = refs[:n_ch]
    masks, pre, hid, top, picked, small, map_full, aff_full, pack_out, rows, pack = refs[n_ch:]
    layers, _, width = map_full.shape
    latents = 2 * samples
    style_at, colour_at, w_at, _ = pack_places(samples, layers)
    ch = where[1]
    grads = [logit_grad(parts, masks, samples, s) for s in range(samples)]

    def wide_sum(at):
        return jnp.concatenate([summed(parts, at + part) for part in range(width // LANES)], axis=1)

    pack[...] = jnp.zeros_like(pack)

    def put(line, lane, size, value, count):
        for i, part in enumerate(pieces(value, count)):
            pack[pl.ds(line + i, 1), pl.ds(lane, size)] = part.astype(F32)

    style_rows = []
    half_lane = lax.broadcasted_iota(jnp.int32, (1, LANES), 1) < LANES // 2
    for s in range(samples):
        grad = grads[s][0]
        style_row = grad[:, :1] * wide_sum(8 * s)
        rows[pl.ds(s, 1), :] = style_row
        style_rows.append(style_row)
        own = rows[pl.ds(s, 1), pl.ds(pl.multiple_of(ch * LANES, LANES), LANES)]
        short = grad
        put(style_at + 2 * s, 0, LANES, own, 2)
        put(style_at + 2 * s, LANES, LANES, short * small[pl.ds(8 * s, 1), :], 2)
        put(style_at + 2 * s, 2 * LANES, LANES, short * small[pl.ds(8 * s + 1, 1), :], 2)
        loss_count = jnp.where(half_lane, grads[s][1], grads[s][2])
        put(style_at + 2 * s, 3 * LANES, LANES, loss_count, 2)
        for c in range(3):
            value = short * small[pl.ds(8 * s + 2 + c, 1), :]
            put(colour_at + 2 * s, c * LANES, LANES, value, 2)
        for j in range(2):
            line = 2 * layers * latents + 2 * s + j
            pack[pl.ds(line, 1), :] = picked[j, pl.ds(s, 1), :]
    w_total = top[pl.ds(0, 1), :]
    for n in range(1, latents):
        w_total = w_total + top[pl.ds(n, 1), :]
    put(w_at, 0, width, w_total, 3)

    def back(value, weights):
        hi, lo = pieces(value, 2)
        both = jnp.concatenate([hi.astype(F32), lo.astype(F32)], axis=0).astype(BF16)
        out = dot_nt(both, weights)
        return out[0:8] + out[8:16]

    pad = [jnp.zeros((8 - samples, width), F32)]
    from_conv = back(jnp.concatenate(style_rows + pad, axis=0), aff_full[...])
    g_rows = []
    for s in range(samples):
        conv_row = from_conv[s : s + 1, :]
        colour_row = grads[s][0][:, :1] * wide_sum(8 * s + 4)
        to_first = [jnp.full((1, width), crossover[s], jnp.int32) > j for j in range(2)]
        g_rows.append(
            jnp.where(to_first[0], conv_row, 0.0) + jnp.where(to_first[1], colour_row, 0.0)
        )
        g_rows.append(
            jnp.where(to_first[0], 0.0, conv_row) + jnp.where(to_first[1], 0.0, colour_row)
        )
    g_rows.append(jnp.zeros((8 - latents, width), F32))
    g_hidden = jnp.concatenate(g_rows, axis=0)
    for layer in reversed(range(layers)):
        g_pre = g_hidden * silu_slope(pre[layer])
        pack[pl.ds(layer * latents, latents), :] = g_pre[0:latents]
        pack[pl.ds((layers + layer) * latents, latents), :] = hid[layer][0:latents]
        if layer > 0:
            g_hidden = back(g_pre, map_full[layer])
    pack_out[...] = pack[...].astype(BF16)


def update_kernel(n_dp, samples, layers, places, where, *refs):
    packs, refs = refs[: len(places)], refs[len(places) :]
    (map_w, map_m, map_e, aff_w, aff_m, aff_e) = refs[:6]
    (map_b, map_bm, map_be, bias, bias_m, bias_e, rgb, rgb_m, rgb_e, w_avg) = refs[6:16]
    outs, refs = refs[16:39], refs[39:]
    map_new, aff_new, map_b_new, bias_new, rgb_new = (refs[4 * i : 4 * i + 4] for i in range(5))
    w_avg_new, loss_new, count_new, g_pre, hid, extra, sems = refs[20:]
    map_outs, aff_outs = outs[0:4], outs[4:8]
    map_b_outs, bias_outs, rgb_outs = outs[8:12], outs[12:16], outs[16:20]
    w_avg_out, loss_out, count_out = outs[20:23]
    latents = 2 * samples
    depth = layers * latents
    style_at, colour_at, w_at, lines = pack_places(samples, layers)
    style_at, colour_at, w_at = (at - 2 * depth for at in (style_at, colour_at, w_at))
    more = lines - 2 * depth
    dp = where[0]
    share, width = map_w.shape[1:]

    odd = lax.rem(dp, 2)
    for part, place in zip(packs, places):
        for index, (even_k, odd_k) in enumerate(place):
            owner = lax.bitwise_xor(dp, jnp.where(odd == 1, odd_k, even_k))
            top = index * lines
            for target, start, size in ((g_pre, 0, depth), (hid, depth, depth), (extra, 2 * depth, more)):
                at = pl.multiple_of(owner * size, size)
                target[pl.ds(at, size), :] = part[pl.ds(top + start, size), :]
    every = extra[...].astype(F32)
    kind = lax.rem(lax.broadcasted_iota(jnp.int32, every.shape, 0), more)

    def total_of(first, count):
        chosen = jnp.logical_and(kind >= first, kind < first + count)
        return jnp.sum(jnp.where(chosen, every, 0.0), axis=0, keepdims=True)

    total = total_of(style_at, 2 * samples)
    count = total[:, width - LANES // 2 : width - LANES // 2 + 1]
    inverse = 1.0 / count
    copies = []

    def send(buffers, targets, at, sem):
        for k, (buffer, target) in enumerate(zip(buffers, targets)):
            if at is not None:
                buffer, target = buffer.at[at], target.at[at]
            copy = pltpu.make_async_copy(buffer, target, sems.at[sem, k])
            copy.start()
            copies.append(copy)

    colour = total_of(colour_at, 2 * samples)
    for c in range(3):
        row = pl.ds(c, 1)
        lane = slice(c * LANES, (c + 1) * LANES)
        new = advance(bias[row, :], bias_m[row, :], bias_e[row, :], total[:, lane] * inverse, 50.0)
        for out, value in zip(bias_new[:3], new[:3]):
            out[row, :] = value
        new = advance(rgb[row, :], rgb_m[row, :], rgb_e[row, :], colour[:, lane] * inverse, 1.0)
        for out, value in zip(rgb_new[:3], new[:3]):
            out[row, :] = value
    bias_new[3][...] = bias_new[0][...].astype(BF16)
    rgb_new[3][...] = rgb_new[0][...].astype(BF16)
    mean = total_of(w_at, 3) * (1.0 / (n_dp * latents))
    w_avg_new[...] = w_avg[...] + (1.0 - AVERAGE_BETA) * (mean - w_avg[...])
    loss_new[0] = jnp.sum(total[:, width - LANES : width - LANES + 1])
    count_new[0] = jnp.sum(count)
    send(bias_new, bias_outs, None, layers // 2 + 2)
    send(rgb_new, rgb_outs, None, layers // 2 + 3)
    send((w_avg_new, loss_new, count_new), (w_avg_out, loss_out, count_out), None, layers // 2 + 4)

    own = pltpu.roll(hid[...].astype(F32), lax.rem(width - dp * share, width), 1)[:, :LANES]
    lane = lax.broadcasted_iota(jnp.int32, own.shape, 1)
    own = jnp.where(lane < share, own, jnp.where(lane == share, 1.0, 0.0))
    layer_of = lax.rem(lax.broadcasted_iota(jnp.int32, own.shape, 0), depth) // latents
    for layer in range(layers):
        mine = jnp.where(layer_of == layer, own, 0.0).astype(BF16)
        grads = dot_tn(mine, g_pre[...]) * inverse
        new = advance(map_w[layer], map_m[layer], map_e[layer], grads[0:share], 30.0)
        for out, value in zip(map_new, new):
            out[layer] = value
        row = pl.ds(layer, 1)
        new = advance(
            map_b[row, :], map_bm[row, :], map_be[row, :], grads[share : share + 1], 30.0
        )
        for out, value in zip(map_b_new[:3], new[:3]):
            out[row, :] = value
        if layer % 2:
            send(map_new, map_outs, pl.ds(layer - 1, 2), layer // 2)
    map_b_new[3][...] = map_b_new[0][...].astype(BF16)
    send(map_b_new, map_b_outs, None, layers // 2 + 5)
    for j in range(2):
        chosen = jnp.zeros(every.shape, F32)
        for piece in range(2):
            here = jnp.logical_and(kind >= style_at, kind < style_at + 2 * samples)
            here = jnp.logical_and(here, lax.rem(kind - style_at + 2, 2) == piece)
            moved = pltpu.roll(every, style_at + piece - j, 0)
            chosen = jnp.where(here, moved, chosen)
        grad = dot_tn(chosen.astype(BF16), extra[:, pl.ds(j * LANES, LANES)]) * inverse
        here = pl.ds(j * width, width)
        new = advance(aff_w[here, :], aff_m[here, :], aff_e[here, :], grad, 30.0)
        for out, value in zip(aff_new, new):
            out[here, :] = value
        send(aff_new, aff_outs, here, layers // 2 + j)
    for copy in copies:
        copy.wait()


def conv_kernel(turns, where, *refs):
    grads, refs = refs[: len(turns)], refs[len(turns) :]
    param, moment, average = refs[:3]
    outs, buffers, sems = refs[-9:-5], refs[-5:-1], refs[-1]
    half = grads[0].shape[0] - COUNT_ROWS
    depth = half // 9
    pair = lax.rem(where[0], 2)
    copies, at = [], 0
    for turn, (grad, (mine, ninths)) in enumerate(zip(grads, turns)):
        start = pl.multiple_of((pair if mine else 1 - pair) * half, half)
        inverse = 1.0 / grad[pl.ds(half, 16), :].astype(F32)[0:1]
        for n in ninths:
            here = pl.ds(at * depth, depth)
            there = pl.ds(pl.multiple_of(start + n * depth, depth), depth)
            at += 1
            value = grad[pl.ds(n * depth, depth), :].astype(F32) * inverse
            new = advance(param[there, :], moment[there, :], average[there, :], value, 5.0)
            for k in range(4):
                buffers[k][here, :] = new[k]
            if n % 3 == 2:
                for k in range(4):
                    copy = pltpu.make_async_copy(
                        buffers[k].at[pl.ds((at - 3) * depth, 3 * depth), :],
                        outs[k].at[pl.ds(pl.multiple_of(start + (n - 2) * depth, depth), 3 * depth), :],
                        sems.at[at // 3 - 1, k],
                    )
                    copy.start()
                    copies.append(copy)
    for copy in copies:
        copy.wait()


def local(
    features,
    z_table,
    seeds,
    crossover,
    counted,
    head,
    w_avg,
    map_w,
    map_w_mom,
    map_w_ema,
    map_b,
    map_b_mom,
    map_b_ema,
    aff_w,
    aff_w_mom,
    aff_w_ema,
    chan_bias,
    chan_bias_mom,
    chan_bias_ema,
    conv_w,
    conv_w_mom,
    conv_w_ema,
    rgb_w,
    rgb_w_mom,
    rgb_w_ema,
):
    samples, side = features.shape[0], features.shape[1]
    pixels = side * side
    layers, share, width = map_w.shape
    n_dp, n_ch = lax.axis_size("dp"), lax.axis_size("chan")
    latents = 2 * samples
    where = jnp.stack([lax.axis_index("dp"), lax.axis_index("chan")]).astype(jnp.int32)
    flat = lambda a: a.reshape(TAPS * width, LANES)

    half = width // 2
    pack_rows = samples * pixels + half + 16
    flat_features = features.reshape(samples * pixels, LANES)
    pack = pl.pallas_call(
        pack_kernel,
        out_shape=shape((pack_rows + half + 16, LANES), BF16),
        in_specs=[SMEM] + [ANY] * 3,
        out_specs=VMEM,
        scratch_shapes=[
            pltpu.VMEM((width, LANES), F32),
            pltpu.VMEM(chan_bias.shape, F32),
            pltpu.SemaphoreType.DMA((3,)),
        ],
        compiler_params=params(4),
        cost_estimate=cost(0),
        name="pack",
    )(where, *hbm(aff_w, chan_bias, flat_features))
    map_low = pl.pallas_call(
        low_kernel,
        out_shape=shape(map_w.shape, BF16),
        in_specs=[ANY],
        out_specs=VMEM,
        scratch_shapes=[pltpu.VMEM(map_w.shape, F32), pltpu.SemaphoreType.DMA((layers,))],
        compiler_params=params(8),
        cost_estimate=cost(0),
        name="low",
    )(*hbm(after(map_w, pack)))
    *chan_packs, last_step = spread_over_chan(flat_features, pack, map_low)
    blocks = spread_layers(map_low, "dp")
    kernel, square, latent_rows = pl.pallas_call(
        functools.partial(weights_kernel, samples),
        out_shape=(
            shape((3, width, 3 * LANES), BF16),
            shape((width, LANES), F32),
            shape((16, width), F32),
        ),
        in_specs=[SMEM, ANY, ANY],
        out_specs=(VMEM,) * 3,
        scratch_shapes=[
            pltpu.VMEM((TAPS, width, LANES), F32),
            pltpu.VMEM((latents, 8, width), F32),
            pltpu.SemaphoreType.DMA((TAPS,)),
            pltpu.SemaphoreType.DMA((latents,)),
        ],
        compiler_params=params(8),
        cost_estimate=cost(0),
        name="weights",
    )(seeds.reshape(-1), *hbm(after(conv_w.reshape(TAPS, width, LANES), blocks[1][0]), z_table))
    second = last_step(blocks[2][0], kernel)
    places = [place for _, place in blocks]

    pre, hid, top, picked, map_full = pl.pallas_call(
        functools.partial(mapping_kernel, n_dp, samples, places),
        out_shape=(
            shape((layers, 8, width), F32),
            shape((layers, 8, width), F32),
            shape((8, width), F32),
            shape((2, 8, width), F32),
            shape((layers, width, width), BF16),
        ),
        in_specs=[SMEM] * 2 + [VMEM] * (len(blocks) + 2),
        out_specs=(VMEM,) * 5,
        scratch_shapes=[pltpu.SemaphoreType.DMA((len(places),))],
        compiler_params=params(12),
        cost_estimate=cost(0),
        name="mapping",
    )(where, crossover, *[block for block, _ in blocks], latent_rows, map_b)

    both, first, first_pair = chan_packs
    feat_t, taps, style_rows, aff_full = pl.pallas_call(
        functools.partial(begin_kernel, n_ch, samples, side),
        out_shape=(
            shape((samples, width, pixels), BF16),
            shape((samples, pixels, 3 * LANES), F32),
            shape((8, width), F32),
            shape((width, width), BF16),
        ),
        in_specs=[SMEM] + [VMEM] * 5,
        out_specs=(VMEM,) * 4,
        scratch_shapes=[
            pltpu.VMEM((16, LANES), F32),
            pltpu.VMEM((samples, pixels + 2 * side, width), BF16),
        ],
        compiler_params=params(16),
        cost_estimate=cost(0),
        name="begin",
    )(where, both, first, first_pair, kernel, picked)
    second_pair = swap(after(second, taps)[samples * pixels :], "dp", 1)
    feat_t, style_rows, aff_full, wide, small, loss_rows = pl.pallas_call(
        functools.partial(main_kernel, n_ch, samples, side),
        out_shape=(
            shape((samples, width, pixels), BF16),
            shape((8, width), F32),
            shape((width, width), BF16),
            shape((samples, pixels + 16, LANES), F32),
            shape((8 * samples, LANES), F32),
            shape((8 * samples, LANES), F32),
        ),
        in_specs=[SMEM] + [VMEM] * 10 + [SMEM] + [VMEM] * 3,
        out_specs=(VMEM,) * 6,
        scratch_shapes=[
            pltpu.VMEM((16, LANES), F32),
            pltpu.VMEM((pack_rows, LANES), BF16),
            pltpu.VMEM((half + 16, LANES), BF16),
            pltpu.VMEM((samples, pixels + 2 * side, LANES), BF16),
            pltpu.VMEM((pixels + 16, 3 * LANES), F32),
        ],
        input_output_aliases={12: 0, 13: 1, 14: 2},
        compiler_params=params(20),
        cost_estimate=cost(0),
        name="main",
    )(
        where,
        second,
        second_pair,
        taps,
        kernel,
        square,
        aff_w,
        picked,
        chan_bias,
        head,
        rgb_w,
        counted,
        feat_t,
        style_rows,
        aff_full,
    )
    pair_losses = swap(loss_rows, "dp", 1)
    unit, to_sum = pl.pallas_call(
        functools.partial(factor_kernel, samples, side),
        out_shape=(
            shape((samples, 2, TAPS * width // 2, LANES), BF16),
            shape((8 * samples, LANES), F32),
        ),
        in_specs=[SMEM] + [VMEM] * 6,
        out_specs=(VMEM,) * 2,
        scratch_shapes=[pltpu.VMEM((pixels, TAPS * LANES), BF16)],
        compiler_params=params(16),
        cost_estimate=cost(0),
        name="factor",
    )(where, feat_t, wide, small, style_rows, kernel, aff_w)
    unit_pair = swap(unit[:, 1], "dp", 1)

    to_send = jnp.concatenate([to_sum, loss_rows[:4 * samples], pair_losses[:4 * samples]])
    sum_parts = spread_direct(to_send, "chan")
    masks = jnp.concatenate([loss_rows[4 * samples:], pair_losses[4 * samples:]])
    half_rows = TAPS * width // 2 + COUNT_ROWS
    total = pl.pallas_call(
        functools.partial(combine_kernel, n_ch, samples),
        out_shape=shape((half_rows, LANES), BF16),
        in_specs=[VMEM] * (n_ch + 3),
        out_specs=VMEM,
        compiler_params=params(8),
        cost_estimate=cost(0),
        name="combine",
    )(*sum_parts, masks, unit, unit_pair)

    lines = pack_places(samples, layers)[-1]
    pack = pl.pallas_call(
        functools.partial(mapping_back_kernel, n_ch, samples),
        out_shape=shape((lines, width), BF16),
        in_specs=[SMEM] * 2 + [VMEM] * (n_ch + 8),
        out_specs=VMEM,
        scratch_shapes=[pltpu.VMEM((8, width), F32), pltpu.VMEM((lines, width), F32)],
        compiler_params=params(12),
        cost_estimate=cost(0),
        name="mapping_back",
    )(where, crossover, *after(sum_parts, total), masks, pre, hid, top, picked, small, map_full, aff_full)
    spread_pack = spread(pack, "dp")
    packs = [part for part, _ in spread_pack]

    flat_aff = [a.reshape(2 * width, LANES) for a in (aff_w, aff_w_mom, aff_w_ema)]
    tiny = [
        map_b,
        map_b_mom,
        map_b_ema,
        chan_bias,
        chan_bias_mom,
        chan_bias_ema,
        rgb_w,
        rgb_w_mom,
        rgb_w_ema,
        w_avg.reshape(1, width),
    ]
    types = (F32, F32, F32, BF16)
    out_shape = (
        [shape(map_w.shape, t) for t in types]
        + [shape((2 * width, LANES), t) for t in types]
        + [shape(map_b.shape, t) for t in types]
        + [shape(chan_bias.shape, t) for t in types]
        + [shape(rgb_w.shape, t) for t in types]
        + [shape((1, width), F32), shape((1,), F32), shape((1,), F32)]
    )
    depth = layers * latents
    update = lambda: pl.pallas_call(
        functools.partial(update_kernel, n_dp, samples, layers, [p for _, p in spread_pack]),
        out_shape=out_shape,
        in_specs=[SMEM] + [VMEM] * (len(packs) + 6 + len(tiny)),
        out_specs=[ANY] * 23,
        scratch_shapes=[pltpu.VMEM(s.shape, s.dtype) for s in out_shape[:21]]
        + [
            pltpu.SMEM((1,), F32),
            pltpu.SMEM((1,), F32),
            pltpu.VMEM((n_dp * depth, width), BF16),
            pltpu.VMEM((n_dp * depth, width), BF16),
            pltpu.VMEM((n_dp * (lines - 2 * depth), width), BF16),
            pltpu.SemaphoreType.DMA((layers // 2 + 6, 4)),
        ],
        compiler_params=params(20),
        cost_estimate=cost(12),
        name="update",
    )(where, *packs, map_w, map_w_mom, map_w_ema, *flat_aff, *tiny)

    bits = [1 << b for b in range(1, n_dp.bit_length() - 1)]
    for turn, (even_bit, odd_bit) in enumerate(zip(bits, bits[::-1])):
        got = crossed(total, "dp", even_bit, odd_bit)
        if turn == len(bits) - 2:
            got = after(got, packs[1])
        if turn == len(bits) - 1:
            outs = update()
            got = after(got, *outs)
        total = (total.astype(F32) + got.astype(F32)).astype(BF16)
    other = swap(total, "dp", 1)

    conv_params = [flat(conv_w), flat(conv_w_mom), flat(conv_w_ema)]

    def conv_part(turns, grads, earlier):
        ninths = sum(len(n) for _, n in turns)
        return pl.pallas_call(
            functools.partial(conv_kernel, turns),
            out_shape=[shape((TAPS * width, LANES), t) for t in types],
            in_specs=[SMEM] + [VMEM] * (len(grads) + 3) + [ANY] * len(earlier),
            out_specs=[ANY] * 4,
            scratch_shapes=[pltpu.VMEM((ninths * TAPS * width // 18, LANES), t) for t in types]
            + [pltpu.SemaphoreType.DMA((ninths // 3, 4))],
            input_output_aliases={4 + len(grads) + k: k for k in range(len(earlier))},
            compiler_params=params(16),
            cost_estimate=cost(0),
            name="conv_rest" if earlier else "conv_first",
        )(where, *grads, *conv_params, *earlier)

    first_part = conv_part([(True, range(6))], [total], [])
    conv_outs = conv_part([(True, range(6, 9)), (False, range(9))], [total, other], first_part)

    map_outs, aff_outs = outs[0:4], [a.reshape(aff_w.shape) for a in outs[4:8]]
    conv_outs = [a.reshape(conv_w.shape) for a in conv_outs]
    return (
        *map_outs,
        *outs[8:12],
        *aff_outs,
        *outs[12:16],
        *conv_outs,
        *outs[16:20],
        outs[20].reshape(width),
        outs[21].reshape(()),
        outs[22].reshape(()),
    )


def solution(mesh):
    in_specs = (
        P("dp", None, None, "chan"),
        P(),
        P("dp", None),
        P("dp"),
        P("dp"),
        P(),
        P(),
        P(None, "dp", None),
        P(None, "dp", None),
        P(None, "dp", None),
        P(),
        P(),
        P(),
        P(None, None, "chan"),
        P(None, None, "chan"),
        P(None, None, "chan"),
        P(None, "chan"),
        P(None, "chan"),
        P(None, "chan"),
        P(None, None, None, "chan"),
        P(None, None, None, "chan"),
        P(None, None, None, "chan"),
        P(None, "chan"),
        P(None, "chan"),
        P(None, "chan"),
    )
    out_specs = (
        P(None, "dp", None),
        P(None, "dp", None),
        P(None, "dp", None),
        P(None, "dp", None),
        P(),
        P(),
        P(),
        P(),
        P(None, None, "chan"),
        P(None, None, "chan"),
        P(None, None, "chan"),
        P(None, None, "chan"),
        P(None, "chan"),
        P(None, "chan"),
        P(None, "chan"),
        P(None, "chan"),
        P(None, None, None, "chan"),
        P(None, None, None, "chan"),
        P(None, None, None, "chan"),
        P(None, None, None, "chan"),
        P(None, "chan"),
        P(None, "chan"),
        P(None, "chan"),
        P(None, "chan"),
        P(),
        P(),
        P(),
    )
    return jax.shard_map(local, mesh=mesh, in_specs=in_specs, out_specs=out_specs, check_vma=False)
```

```python
import functools

import jax
import jax.numpy as jnp
from jax import lax
from jax.experimental import pallas as pl
from jax.experimental.pallas import tpu as pltpu
from jax.sharding import PartitionSpec as P

MOMENTUM = 0.9
EMA_DECAY = 0.95
AVERAGE_BETA = 0.5
BF16 = jnp.bfloat16
F32 = jnp.float32
TAPS = 9
LANES = 128
COUNT_ROWS = 32
VMEM = pl.BlockSpec(memory_space=pltpu.VMEM)
SMEM = pl.BlockSpec(memory_space=pltpu.SMEM)
ANY = pl.BlockSpec(memory_space=pl.ANY)


def shape(dims, dtype):
    return jax.ShapeDtypeStruct(dims, dtype)


def params(mib):
    return pltpu.CompilerParams(vmem_limit_bytes=mib * 1024 * 1024)


def cost(micros):
    return pl.CostEstimate(flops=int(micros * 1e9), bytes_accessed=0, transcendentals=0)


def hbm(*values):
    return [pltpu.with_memory_space_constraint(value, pltpu.HBM) for value in values]


def after(values, *others):
    return lax.optimization_barrier((values, others))[0]


def swap(value, axis, distance):
    return lax.ppermute(
        value, axis, [(i, i ^ distance) for i in range(lax.axis_size(axis))]
    )


def spread(value, axis):
    size = lax.axis_size(axis)
    beside = swap(value, axis, 1)
    if size != 8:
        parts = [(value, [(0, 0)]), (beside, [(1, 1)])]
        for k in range(2, size, 2):
            part = swap(value, axis, k)
            parts += [(part, [(k, k)]), (swap(part, axis, 1), [(k + 1, k + 1)])]
        return parts
    near = jnp.concatenate([value, beside])
    far = crossed(near, axis, 4, 2)
    corner = crossed(far, axis, 2, 4)
    return [
        (near, [(0, 0), (1, 1)]),
        (far, [(4, 2), (5, 3)]),
        (corner, [(6, 6), (7, 7)]),
        (swap(far, axis, 1), [(3, 5), (2, 4)]),
    ]


def spread_direct(value, axis):
    return [value] + [swap(value, axis, k) for k in range(1, lax.axis_size(axis))]


def spread_over_chan(features, pack, ready):
    n_dp, n_ch = lax.axis_size("dp"), lax.axis_size("chan")
    cut = features.shape[0]
    both = lax.optimization_barrier(jnp.concatenate([pack, swap(features, "dp", 1)]))

    def joint(value, moves):
        pairs = [
            (d * n_ch + a, d * n_ch + b) for d in range(n_dp) for a, b in moves[d % 2]
        ]
        return lax.ppermute(value, ("dp", "chan"), pairs)

    first = joint(both, ([(c, c ^ 1) for c in range(4)], [(c, c ^ 2) for c in range(4)]))
    first_pair = swap(first[cut:], "dp", 1)
    odd = lax.rem(lax.axis_index("dp"), 2) == 1

    def last_step(*others):
        value = after(jnp.where(odd, first, both), *others)
        return joint(value, ([(1, 2), (2, 1)], [(1, 0), (2, 3)]))

    return both, first, first_pair, last_step


def crossed(value, axis, even_distance, odd_distance):
    size = lax.axis_size(axis)
    pairs = [(i, i ^ (odd_distance if i % 2 else even_distance)) for i in range(size)]
    return lax.ppermute(value, axis, pairs)


def spread_layers(value, axis):
    size = lax.axis_size(axis)
    beside = swap(value, axis, 1)
    parts = [(value, (0, 0, 0)), (beside, (0, 1, 1))]
    if size != 8:
        for k in range(2, size, 2):
            part = swap(value, axis, k)
            parts += [(part, (0, k, k)), (swap(part, axis, 1), (0, k + 1, k + 1))]
        return parts
    far = crossed(value, axis, 2, 4)
    far_beside = crossed(beside, axis, 2, 4)
    corner = crossed(far, axis, 4, 2)
    parts += [(far, (0, 2, 4)), (far_beside, (0, 3, 5)), (corner, (0, 6, 6))]
    parts += [(swap(far, axis, 1), (0, 5, 3)), (swap(far_beside, axis, 1), (0, 4, 2))]
    parts += [(swap(corner, axis, 1), (0, 7, 7))]
    return parts


def silu_slope(preact):
    sig = jax.nn.sigmoid(preact)
    return sig * (1.0 + preact * (1.0 - sig))


def pieces(value, count):
    out = []
    for _ in range(count):
        part = value.astype(BF16)
        out.append(part)
        value = value - part.astype(F32)
    return out


def advance(param, moment, average, grad, rate):
    moment_new = MOMENTUM * moment + grad
    param_new = param - rate * (grad + MOMENTUM * moment_new)
    average_new = EMA_DECAY * average + (1.0 - EMA_DECAY) * param_new
    return param_new, moment_new, average_new, param_new.astype(BF16)


def dot(a, b):
    return jnp.dot(a, b, preferred_element_type=F32)


def dot_nt(a, b):
    return lax.dot_general(a, b, (((1,), (1,)), ((), ())), preferred_element_type=F32)


def dot_tn(a, b):
    return lax.dot_general(a, b, (((0,), (0,)), ((), ())), preferred_element_type=F32)


def pack_kernel(where, aff_w, bias, features, pack, aff_stage, bias_stage, sems):
    half = aff_stage.shape[0] // 2
    rows = features.shape[0]
    pair = lax.rem(where[0], 2)
    feat_copy = pltpu.make_async_copy(features, pack.at[pl.ds(0, rows), :], sems.at[0])
    aff_copy = pltpu.make_async_copy(aff_w.at[0], aff_stage, sems.at[1])
    bias_copy = pltpu.make_async_copy(bias, bias_stage, sems.at[2])
    for copy in (feat_copy, aff_copy, bias_copy):
        copy.start()
    bias_copy.wait()
    hi, mid, lo = pieces(bias_stage[0:1, :], 3)
    lines = jnp.concatenate(
        [hi.astype(F32), mid.astype(F32), lo.astype(F32), jnp.zeros((13, LANES), F32)], axis=0
    )
    aff_copy.wait()
    for turn, owner in enumerate((pair, 1 - pair)):
        at = rows + turn * (half + 16)
        start = pl.multiple_of(owner * half, half)
        pack[pl.ds(at, half), :] = aff_stage[pl.ds(start, half), :].astype(BF16)
        pack[pl.ds(at + half, 16), :] = lines.astype(BF16)
    feat_copy.wait()


def low_kernel(map_w, map_low, stage, sems):
    layers = map_w.shape[0]
    copies = [
        pltpu.make_async_copy(map_w.at[layer], stage.at[layer], sems.at[layer])
        for layer in range(layers)
    ]
    for copy in copies:
        copy.start()
    for layer in range(layers):
        copies[layer].wait()
        map_low[layer] = stage[layer].astype(BF16)


def mapping_kernel(n_dp, samples, places, *refs):
    refs = list(refs)

    def take(count):
        got = refs[:count]
        del refs[:count]
        return got

    where, crossover = take(2)
    parts = take(len(places))
    latent_rows, map_b = take(2)
    pre_out, hid_out, top_out, picked_out, map_full, sem_map = refs
    layers, share, width = parts[0].shape
    dp = where[0]
    odd = lax.rem(dp, 2)
    moves = []
    for part, (first, even_k, odd_k) in zip(parts, places):
        k = jnp.where(odd == 1, odd_k, even_k)
        at = pl.multiple_of(lax.bitwise_xor(dp, k) * share, share)
        moves.append((part, first, pl.ds(at, share)))
    whole_tiles = share % 16 == 0
    if not whole_tiles:
        copies = [
            pltpu.make_async_copy(
                part, map_full.at[pl.ds(first, part.shape[0]), at, :], sem_map.at[i]
            )
            for i, (part, first, at) in enumerate(moves)
        ]
        for copy in copies:
            copy.start()
        for copy in copies:
            copy.wait()

    def bring(layer):
        for part, first, at in moves:
            if whole_tiles and first <= layer < first + part.shape[0]:
                map_full[layer, at, :] = part[layer - first]

    bring(0)
    bring(1)
    hidden = latent_rows[...]
    for layer in range(layers):
        low = hidden.astype(BF16)
        preact = dot(low, map_full[layer]) + map_b[pl.ds(layer, 1), :]
        if layer + 2 < layers:
            bring(layer + 2)
        hid_out[layer] = low.astype(F32)[0:8]
        pre_out[layer] = preact[0:8]
        hidden = preact * jax.nn.sigmoid(preact)
    top_out[...] = hidden[0:8]
    low = hidden.astype(BF16).astype(F32)
    for j in range(2):
        chosen = []
        for s in range(samples):
            first = crossover[s] > j
            chosen.append(
                jnp.where(first, low[2 * s : 2 * s + 1, :], low[2 * s + 1 : 2 * s + 2, :])
            )
        chosen.append(jnp.zeros((8 - samples, width), F32))
        picked_out[j] = jnp.concatenate(chosen, axis=0)


def weights_kernel(samples, seeds, conv_w, z_table, kernel, square, latent_rows, stage, rows, sems, sem_z):
    latents = 2 * samples
    z_copies = []
    for n in range(latents):
        at = pl.multiple_of((seeds[n] // 8) * 8, 8)
        z_copies.append(pltpu.make_async_copy(z_table.at[pl.ds(at, 8), :], rows.at[n], sem_z.at[n]))
    copies = [pltpu.make_async_copy(conv_w.at[t], stage.at[t], sems.at[t]) for t in range(TAPS)]
    for copy in z_copies + copies:
        copy.start()
    total = jnp.zeros(square.shape, F32)
    for tap in range(TAPS):
        copies[tap].wait()
        low = stage[tap].astype(BF16)
        kernel[tap // 3, :, pl.ds((tap % 3) * LANES, LANES)] = low
        wide = low.astype(F32)
        total = total + wide * wide
    square[...] = total
    normed = []
    for n in range(latents):
        z_copies[n].wait()
        row = rows[n, pl.ds(lax.rem(seeds[n], 8), 1), :]
        scale = lax.rsqrt(jnp.mean(row * row, axis=1, keepdims=True) + 1e-08)
        normed.append(row * scale)
    normed.append(jnp.zeros((16 - latents, rows.shape[2]), F32))
    latent_rows[...] = jnp.concatenate(normed, axis=0)


def bring_blocks(
    blocks, samples, side, where, picked, bias_full, style_rows, feat_t, aff_full, kernel, padded, rows
):
    width = aff_full.shape[0]
    half, pixels = width // 2, side * side
    dp, ch = where[0], where[1]
    pair = lax.rem(dp, 2)
    mine = pl.ds(pl.multiple_of(pair * half, half), half)
    other = pl.ds(pl.multiple_of((1 - pair) * half, half), half)
    chosen = picked[0].astype(BF16)
    blank = jnp.zeros((side, padded.shape[2]), BF16)
    for s in range(samples):
        padded[s, pl.ds(0, side), :] = blank
        padded[s, pl.ds(side + pixels, side), :] = blank
    for slot, (source, top, tail_at, other_source, other_tail_at, k) in enumerate(blocks):
        lane = pl.ds(pl.multiple_of(lax.bitwise_xor(ch, k) * LANES, LANES), LANES)
        place = pl.ds(slot * LANES, LANES)
        aff_full[mine, lane] = source[pl.ds(tail_at, half), :]
        aff_full[other, lane] = other_source[pl.ds(other_tail_at, half), :]
        bias_full[...] = source[pl.ds(tail_at + half, 16), :].astype(F32)
        bias_row = bias_full[0:1, :] + bias_full[1:2, :] + bias_full[2:3, :]
        style = (dot(chosen, aff_full[:, lane]) + bias_row).astype(BF16)
        style_rows[:, lane] = style.astype(F32)
        for dy in range(3):
            rows[dy, place, :] = kernel[dy, lane, :]
        for s in range(samples):
            value = source[pl.ds(top + s * pixels, pixels), :]
            feat_t[s, lane, :] = value.T
            padded[s, pl.ds(side, pixels), place] = value * style[s : s + 1, :]


def begin_kernel(n_ch, samples, side, *refs):
    where, both, first, kernel, picked = refs[:5]
    feat_t, taps, style_rows, aff_full, bias_full, padded, rows = refs[5:]
    width = aff_full.shape[0]
    half, pixels = width // 2, side * side
    feats, tail_rows = samples * pixels, half + 16
    partner_tail = feats + tail_rows
    style_rows[...] = jnp.zeros_like(style_rows)
    blocks = (
        (both, 0, feats, both, partner_tail, 0),
        (first, 0, feats, first, partner_tail, 1 + lax.rem(where[0], 2)),
    )
    bring_blocks(
        blocks, samples, side, where, picked, bias_full, style_rows, feat_t, aff_full, kernel, padded, rows
    )
    chunk = min(256, pixels)
    for s in range(samples):
        for r in range(pixels // chunk):
            total = dot(padded[s, pl.ds(r * chunk, chunk), :], rows[0])
            total = total + dot(padded[s, pl.ds(side + r * chunk, chunk), :], rows[1])
            total = total + dot(padded[s, pl.ds(2 * side + r * chunk, chunk), :], rows[2])
            taps[s, pl.ds(r * chunk, chunk), :] = total


def main_kernel(n_ch, samples, side, *refs):
    where, first_pair, second, second_pair, earlier, kernel, square_in = refs[:7]
    aff_w, picked, bias, head, rgb_w, counted = refs[7:13]
    feat_t, style_rows, aff_full, wide, small, loss_rows = refs[16:22]
    bias_full, late, late_tail, padded, kernel_rows, taps = refs[22:]
    width = aff_full.shape[0]
    half, pixels = width // 2, side * side
    feats, tail_rows = samples * pixels, half + 16
    cut = second.shape[0] - second_pair.shape[0]
    partner_tail, partner_feats = feats + tail_rows, feats + 2 * tail_rows
    dp, ch = where[0], where[1]
    pair = lax.rem(dp, 2)
    at_end = jnp.logical_or(ch == 0, ch == n_ch - 1)
    is_held = at_end == (pair == 1)

    @pl.when(is_held)
    def _():
        late[...] = second[pl.ds(0, feats + tail_rows), :]
        late_tail[...] = second[pl.ds(partner_tail, tail_rows), :]

    @pl.when(jnp.logical_not(is_held))
    def _():
        late[pl.ds(0, feats), :] = second_pair[pl.ds(partner_feats - cut, feats), :]
        late[pl.ds(feats, tail_rows), :] = second_pair[pl.ds(partner_tail - cut, tail_rows), :]
        late_tail[...] = second_pair[pl.ds(feats - cut, tail_rows), :]

    blocks = (
        (first_pair, partner_feats - cut, partner_tail - cut, first_pair, feats - cut, 2 - pair),
        (late, 0, feats, late_tail, 0, 3),
    )
    bring_blocks(
        blocks, samples, side, where, picked, bias_full, style_rows, feat_t, aff_full, kernel, padded, kernel_rows
    )
    square = square_in[...]
    colour_aff = aff_w[1].astype(BF16)
    style1 = dot(picked[1].astype(BF16), colour_aff) + bias[1:2, :]
    style1 = style1.astype(BF16).astype(F32)
    colour = rgb_w[...].astype(BF16)
    colour_wide = colour.astype(F32)
    colour_rows = jnp.concatenate([colour_wide, jnp.zeros((13, LANES), F32)], axis=0).astype(BF16)
    head_rows = jnp.concatenate(
        [head[...].astype(F32), jnp.zeros((13, pixels), F32)], axis=0
    ).astype(BF16)
    conv_bias = bias[2:3, :]
    chunk = min(256, pixels)
    steps = pixels // chunk
    column = lax.rem(lax.broadcasted_iota(jnp.int32, (chunk, LANES), 0), side)
    not_first, not_last = column > 0, column < side - 1
    small[...] = jnp.zeros_like(small)
    loss_rows[...] = jnp.zeros_like(loss_rows)
    taps[pl.ds(0, 8), :] = jnp.zeros((8, 3 * LANES), F32)
    taps[pl.ds(8 + pixels, 8), :] = jnp.zeros((8, 3 * LANES), F32)

    for s in range(samples):
        wide[s, pl.ds(0, 8), :] = jnp.zeros((8, LANES), F32)
        wide[s, pl.ds(8 + pixels, 8), :] = jnp.zeros((8, LANES), F32)
        style_col = jnp.broadcast_to(style_rows[pl.ds(s, 1), :], (LANES, width)).T
        demod = lax.rsqrt(
            jnp.sum(style_col * style_col * square, axis=0, keepdims=True) + 1e-08
        )
        style_colour = style1[s : s + 1, :]
        for r in range(steps):
            total = earlier[s, pl.ds(r * chunk, chunk), :]
            for dy in range(3):
                total = total + dot(
                    padded[s, pl.ds(dy * side + r * chunk, chunk), :], kernel_rows[dy]
                )
            taps[pl.ds(8 + r * chunk, chunk), :] = total
        mixed = jnp.zeros((3, LANES), F32)
        g_style1 = jnp.zeros((1, LANES), F32)
        g_bias = jnp.zeros((1, LANES), F32)
        g_demod = jnp.zeros((1, LANES), F32)
        for r in range(steps):
            left = taps[pl.ds(7 + r * chunk, chunk), pl.ds(0, LANES)]
            centre = taps[pl.ds(8 + r * chunk, chunk), pl.ds(LANES, LANES)]
            right = taps[pl.ds(9 + r * chunk, chunk), pl.ds(2 * LANES, LANES)]
            conv_out = centre + jnp.where(not_first, left, 0.0) + jnp.where(not_last, right, 0.0)
            scaled = conv_out * demod + conv_bias
            sig = jax.nn.sigmoid(scaled)
            activated = scaled * sig
            act_mod = (activated * style_colour).astype(BF16)
            mixed = mixed + dot(head_rows[:, r * chunk : (r + 1) * chunk], act_mod)[0:3]
            g_act = dot_tn(head_rows[:, r * chunk : (r + 1) * chunk], colour_rows)
            g_style1 = g_style1 + jnp.sum(g_act * activated, axis=0, keepdims=True)
            g_scaled = g_act * style_colour * (sig * (1.0 + scaled * (1.0 - sig)))
            g_bias = g_bias + jnp.sum(g_scaled, axis=0, keepdims=True)
            g_demod = g_demod + jnp.sum(g_scaled * conv_out, axis=0, keepdims=True)
            wide[s, pl.ds(8 + r * chunk, chunk), :] = g_scaled * demod
        logit = jnp.sum(
            jnp.sum(mixed * colour_wide, axis=0, keepdims=True), axis=1, keepdims=True
        )
        loss_rows[pl.ds(s, 1), :] = jnp.broadcast_to(logit, (1, LANES))
        loss_rows[pl.ds(4 * samples + s, 1), :] = jnp.full((1, LANES), counted[s], jnp.int32).astype(F32)
        small[pl.ds(8 * s, 1), :] = g_style1
        small[pl.ds(8 * s + 1, 1), :] = g_bias
        small[pl.ds(8 * s + 2, 3), :] = mixed
        small[pl.ds(8 * s + 5, 1), :] = g_demod * demod * demod * demod


def factor_kernel(samples, side, where, feat_t, wide, small, style_rows, kernel, aff_w, unit, to_sum, shifted):
    width = feat_t.shape[1]
    pixels = side * side
    pair = lax.rem(where[0], 2)
    half = TAPS * width // 2
    chunk = min(256, pixels)
    steps = pixels // chunk
    column = lax.rem(lax.broadcasted_iota(jnp.int32, (chunk, LANES), 0), side)
    not_first, not_last = column > 0, column < side - 1
    to_sum[...] = jnp.zeros_like(to_sum)
    colour_aff = aff_w[1].astype(BF16).astype(F32)
    for s in range(samples):
        style_col = jnp.broadcast_to(style_rows[pl.ds(s, 1), :], (LANES, width)).T
        for r in range(steps):
            before = jnp.where(not_last, wide[s, pl.ds(9 + r * chunk, chunk), :], 0.0)
            centre = wide[s, pl.ds(8 + r * chunk, chunk), :]
            after_it = jnp.where(not_first, wide[s, pl.ds(7 + r * chunk, chunk), :], 0.0)
            for dx, value in enumerate((before, centre, after_it)):
                value = value.astype(BF16)
                for dy in range(3):
                    lane = pl.ds((3 * dy + dx) * LANES, LANES)
                    start = r * chunk + (dy - 1) * side
                    low_at, high_at = max(start, 0), min(start + chunk, pixels)
                    shifted[pl.ds(low_at, high_at - low_at), lane] = value[
                        low_at - start : high_at - start, :
                    ]
        for dx in range(3):
            blank = jnp.zeros((side, LANES), BF16)
            shifted[pl.ds(pixels - side, side), pl.ds(dx * LANES, LANES)] = blank
            shifted[pl.ds(0, side), pl.ds((6 + dx) * LANES, LANES)] = blank
        factor = small[pl.ds(8 * s + 5, 1), :]
        g_style = jnp.zeros((width, LANES), F32)
        for first in range(0, TAPS, 2):
            count = min(2, TAPS - first)
            block = dot(feat_t[s], shifted[:, pl.ds(first * LANES, count * LANES)])
            for tap in range(first, first + count):
                raw = block[:, (tap - first) * LANES : (tap - first + 1) * LANES]
                weight = kernel[tap // 3, :, pl.ds((tap % 3) * LANES, LANES)].astype(F32)
                inner = raw - style_col * (weight * factor)
                g_style = g_style + weight * inner
                value = (style_col * inner).astype(BF16)
                top = tap * width
                for h in range(2):
                    low_at, high_at = max(top, h * half), min(top + width, (h + 1) * half)
                    if low_at < high_at:
                        slot = 1 - pair if h else pair
                        unit[s, slot, pl.ds(low_at - h * half, high_at - low_at), :] = value[
                            low_at - top : high_at - top, :
                        ]
        for at, value in ((0, g_style), (4, colour_aff * small[pl.ds(8 * s, 1), :])):
            row = jnp.sum(value.T, axis=0, keepdims=True)
            for part in range(width // LANES):
                to_sum[pl.ds(8 * s + at + part, 1), :] = row[:, part * LANES : (part + 1) * LANES]


def summed(parts, row):
    values = [part[pl.ds(row, 1), :] for part in parts]
    while len(values) > 1:
        values = [values[i] + values[i + 1] for i in range(0, len(values), 2)]
    return values[0]


def logit_grad(parts, masks, samples, s):
    at = 4 * samples * (s // samples) + s % samples
    logit = summed(parts, 8 * samples + at)
    mask = masks[pl.ds(at, 1), :]
    return -mask * jax.nn.sigmoid(-logit), mask * jax.nn.softplus(-logit), mask


def combine_kernel(n_ch, samples, *refs):
    parts, (masks, unit, unit_pair, out) = refs[:n_ch], refs[n_ch:]
    half = unit_pair.shape[1]
    grads, total = [], jnp.zeros((1, LANES), F32)
    for s in range(2 * samples):
        grad, _, mask = logit_grad(parts, masks, samples, s)
        grads.append(grad)
        total = total + mask
    block = half // 9
    for b in range(9):
        here = pl.ds(b * block, block)
        value = jnp.zeros((block, LANES), F32)
        for s in range(samples):
            value = value + grads[s] * unit[s, 0, here, :].astype(F32)
            value = value + grads[samples + s] * unit_pair[s, here, :].astype(F32)
        out[here, :] = value.astype(BF16)
    out[pl.ds(half, COUNT_ROWS), :] = jnp.broadcast_to(total, (COUNT_ROWS, LANES)).astype(BF16)


def pack_places(samples, layers):
    latents = 2 * samples
    style = 2 * layers * latents + latents
    colour = style + 2 * samples
    w_total = colour + 2 * samples
    return style, colour, w_total, -(-(w_total + 3) // 16) * 16


def mapping_back_kernel(n_ch, samples, where, crossover, *refs):
    parts = refs[:n_ch]
    masks, pre, hid, top, picked, small, map_full, aff_full, pack_out, rows, pack = refs[n_ch:]
    layers, _, width = map_full.shape
    latents = 2 * samples
    style_at, colour_at, w_at, _ = pack_places(samples, layers)
    ch = where[1]
    grads = [logit_grad(parts, masks, samples, s) for s in range(samples)]

    def wide_sum(at):
        return jnp.concatenate([summed(parts, at + part) for part in range(width // LANES)], axis=1)

    pack[...] = jnp.zeros_like(pack)

    def put(line, lane, size, value, count):
        for i, part in enumerate(pieces(value, count)):
            pack[pl.ds(line + i, 1), pl.ds(lane, size)] = part.astype(F32)

    style_rows = []
    half_lane = lax.broadcasted_iota(jnp.int32, (1, LANES), 1) < LANES // 2
    for s in range(samples):
        grad = grads[s][0]
        style_row = grad[:, :1] * wide_sum(8 * s)
        rows[pl.ds(s, 1), :] = style_row
        style_rows.append(style_row)
        own = rows[pl.ds(s, 1), pl.ds(pl.multiple_of(ch * LANES, LANES), LANES)]
        short = grad
        put(style_at + 2 * s, 0, LANES, own, 2)
        put(style_at + 2 * s, LANES, LANES, short * small[pl.ds(8 * s, 1), :], 2)
        put(style_at + 2 * s, 2 * LANES, LANES, short * small[pl.ds(8 * s + 1, 1), :], 2)
        loss_count = jnp.where(half_lane, grads[s][1], grads[s][2])
        put(style_at + 2 * s, 3 * LANES, LANES, loss_count, 2)
        for c in range(3):
            value = short * small[pl.ds(8 * s + 2 + c, 1), :]
            put(colour_at + 2 * s, c * LANES, LANES, value, 2)
        for j in range(2):
            line = 2 * layers * latents + 2 * s + j
            pack[pl.ds(line, 1), :] = picked[j, pl.ds(s, 1), :]
    w_total = top[pl.ds(0, 1), :]
    for n in range(1, latents):
        w_total = w_total + top[pl.ds(n, 1), :]
    put(w_at, 0, width, w_total, 3)

    def back(value, weights):
        hi, lo = pieces(value, 2)
        both = jnp.concatenate([hi.astype(F32), lo.astype(F32)], axis=0).astype(BF16)
        out = dot_nt(both, weights)
        return out[0:8] + out[8:16]

    pad = [jnp.zeros((8 - samples, width), F32)]
    from_conv = back(jnp.concatenate(style_rows + pad, axis=0), aff_full[...])
    g_rows = []
    for s in range(samples):
        conv_row = from_conv[s : s + 1, :]
        colour_row = grads[s][0][:, :1] * wide_sum(8 * s + 4)
        to_first = [jnp.full((1, width), crossover[s], jnp.int32) > j for j in range(2)]
        g_rows.append(
            jnp.where(to_first[0], conv_row, 0.0) + jnp.where(to_first[1], colour_row, 0.0)
        )
        g_rows.append(
            jnp.where(to_first[0], 0.0, conv_row) + jnp.where(to_first[1], 0.0, colour_row)
        )
    g_rows.append(jnp.zeros((8 - latents, width), F32))
    g_hidden = jnp.concatenate(g_rows, axis=0)
    for layer in reversed(range(layers)):
        g_pre = g_hidden * silu_slope(pre[layer])
        pack[pl.ds(layer * latents, latents), :] = g_pre[0:latents]
        pack[pl.ds((layers + layer) * latents, latents), :] = hid[layer][0:latents]
        if layer > 0:
            g_hidden = back(g_pre, map_full[layer])
    pack_out[...] = pack[...].astype(BF16)


def update_kernel(n_dp, samples, layers, places, where, *refs):
    packs, refs = refs[: len(places)], refs[len(places) :]
    (map_w, map_m, map_e, aff_w, aff_m, aff_e) = refs[:6]
    (map_b, map_bm, map_be, bias, bias_m, bias_e, rgb, rgb_m, rgb_e, w_avg) = refs[6:16]
    outs, refs = refs[16:39], refs[39:]
    map_new, aff_new, map_b_new, bias_new, rgb_new = (refs[4 * i : 4 * i + 4] for i in range(5))
    w_avg_new, loss_new, count_new, g_pre, hid, extra, sems = refs[20:]
    map_outs, aff_outs = outs[0:4], outs[4:8]
    map_b_outs, bias_outs, rgb_outs = outs[8:12], outs[12:16], outs[16:20]
    w_avg_out, loss_out, count_out = outs[20:23]
    latents = 2 * samples
    depth = layers * latents
    style_at, colour_at, w_at, lines = pack_places(samples, layers)
    style_at, colour_at, w_at = (at - 2 * depth for at in (style_at, colour_at, w_at))
    more = lines - 2 * depth
    dp = where[0]
    share, width = map_w.shape[1:]

    odd = lax.rem(dp, 2)
    for part, place in zip(packs, places):
        for index, (even_k, odd_k) in enumerate(place):
            owner = lax.bitwise_xor(dp, jnp.where(odd == 1, odd_k, even_k))
            top = index * lines
            for target, start, size in ((g_pre, 0, depth), (hid, depth, depth), (extra, 2 * depth, more)):
                at = pl.multiple_of(owner * size, size)
                target[pl.ds(at, size), :] = part[pl.ds(top + start, size), :]
    every = extra[...].astype(F32)
    kind = lax.rem(lax.broadcasted_iota(jnp.int32, every.shape, 0), more)

    def total_of(first, count):
        chosen = jnp.logical_and(kind >= first, kind < first + count)
        return jnp.sum(jnp.where(chosen, every, 0.0), axis=0, keepdims=True)

    total = total_of(style_at, 2 * samples)
    count = total[:, width - LANES // 2 : width - LANES // 2 + 1]
    inverse = 1.0 / count
    copies = []

    def send(buffers, targets, at, sem):
        for k, (buffer, target) in enumerate(zip(buffers, targets)):
            if at is not None:
                buffer, target = buffer.at[at], target.at[at]
            copy = pltpu.make_async_copy(buffer, target, sems.at[sem, k])
            copy.start()
            copies.append(copy)

    colour = total_of(colour_at, 2 * samples)
    for c in range(3):
        row = pl.ds(c, 1)
        lane = slice(c * LANES, (c + 1) * LANES)
        new = advance(bias[row, :], bias_m[row, :], bias_e[row, :], total[:, lane] * inverse, 50.0)
        for out, value in zip(bias_new[:3], new[:3]):
            out[row, :] = value
        new = advance(rgb[row, :], rgb_m[row, :], rgb_e[row, :], colour[:, lane] * inverse, 1.0)
        for out, value in zip(rgb_new[:3], new[:3]):
            out[row, :] = value
    bias_new[3][...] = bias_new[0][...].astype(BF16)
    rgb_new[3][...] = rgb_new[0][...].astype(BF16)
    mean = total_of(w_at, 3) * (1.0 / (n_dp * latents))
    w_avg_new[...] = w_avg[...] + (1.0 - AVERAGE_BETA) * (mean - w_avg[...])
    loss_new[0] = jnp.sum(total[:, width - LANES : width - LANES + 1])
    count_new[0] = jnp.sum(count)
    send(bias_new, bias_outs, None, layers // 2 + 2)
    send(rgb_new, rgb_outs, None, layers // 2 + 3)
    send((w_avg_new, loss_new, count_new), (w_avg_out, loss_out, count_out), None, layers // 2 + 4)

    own = pltpu.roll(hid[...].astype(F32), lax.rem(width - dp * share, width), 1)[:, :LANES]
    lane = lax.broadcasted_iota(jnp.int32, own.shape, 1)
    own = jnp.where(lane < share, own, jnp.where(lane == share, 1.0, 0.0))
    layer_of = lax.rem(lax.broadcasted_iota(jnp.int32, own.shape, 0), depth) // latents
    for layer in range(layers):
        mine = jnp.where(layer_of == layer, own, 0.0).astype(BF16)
        grads = dot_tn(mine, g_pre[...]) * inverse
        new = advance(map_w[layer], map_m[layer], map_e[layer], grads[0:share], 30.0)
        for out, value in zip(map_new, new):
            out[layer] = value
        row = pl.ds(layer, 1)
        new = advance(
            map_b[row, :], map_bm[row, :], map_be[row, :], grads[share : share + 1], 30.0
        )
        for out, value in zip(map_b_new[:3], new[:3]):
            out[row, :] = value
        if layer % 2:
            send(map_new, map_outs, pl.ds(layer - 1, 2), layer // 2)
    map_b_new[3][...] = map_b_new[0][...].astype(BF16)
    send(map_b_new, map_b_outs, None, layers // 2 + 5)
    for j in range(2):
        chosen = jnp.zeros(every.shape, F32)
        for piece in range(2):
            here = jnp.logical_and(kind >= style_at, kind < style_at + 2 * samples)
            here = jnp.logical_and(here, lax.rem(kind - style_at + 2, 2) == piece)
            moved = pltpu.roll(every, style_at + piece - j, 0)
            chosen = jnp.where(here, moved, chosen)
        grad = dot_tn(chosen.astype(BF16), extra[:, pl.ds(j * LANES, LANES)]) * inverse
        here = pl.ds(j * width, width)
        new = advance(aff_w[here, :], aff_m[here, :], aff_e[here, :], grad, 30.0)
        for out, value in zip(aff_new, new):
            out[here, :] = value
        send(aff_new, aff_outs, here, layers // 2 + j)
    for copy in copies:
        copy.wait()


def conv_kernel(turns, where, *refs):
    grads, refs = refs[: len(turns)], refs[len(turns) :]
    param, moment, average = refs[:3]
    outs, buffers, sems = refs[-9:-5], refs[-5:-1], refs[-1]
    half = grads[0].shape[0] - COUNT_ROWS
    depth = half // 9
    pair = lax.rem(where[0], 2)
    copies, at = [], 0
    for turn, (grad, (mine, ninths)) in enumerate(zip(grads, turns)):
        start = pl.multiple_of((pair if mine else 1 - pair) * half, half)
        inverse = 1.0 / grad[pl.ds(half, 16), :].astype(F32)[0:1]
        for n in ninths:
            here = pl.ds(at * depth, depth)
            there = pl.ds(pl.multiple_of(start + n * depth, depth), depth)
            at += 1
            value = grad[pl.ds(n * depth, depth), :].astype(F32) * inverse
            new = advance(param[there, :], moment[there, :], average[there, :], value, 5.0)
            for k in range(4):
                buffers[k][here, :] = new[k]
            if n % 3 == 2:
                for k in range(4):
                    copy = pltpu.make_async_copy(
                        buffers[k].at[pl.ds((at - 3) * depth, 3 * depth), :],
                        outs[k].at[pl.ds(pl.multiple_of(start + (n - 2) * depth, depth), 3 * depth), :],
                        sems.at[at // 3 - 1, k],
                    )
                    copy.start()
                    copies.append(copy)
    for copy in copies:
        copy.wait()


def local(
    features,
    z_table,
    seeds,
    crossover,
    counted,
    head,
    w_avg,
    map_w,
    map_w_mom,
    map_w_ema,
    map_b,
    map_b_mom,
    map_b_ema,
    aff_w,
    aff_w_mom,
    aff_w_ema,
    chan_bias,
    chan_bias_mom,
    chan_bias_ema,
    conv_w,
    conv_w_mom,
    conv_w_ema,
    rgb_w,
    rgb_w_mom,
    rgb_w_ema,
):
    samples, side = features.shape[0], features.shape[1]
    pixels = side * side
    layers, share, width = map_w.shape
    n_dp, n_ch = lax.axis_size("dp"), lax.axis_size("chan")
    latents = 2 * samples
    where = jnp.stack([lax.axis_index("dp"), lax.axis_index("chan")]).astype(jnp.int32)
    flat = lambda a: a.reshape(TAPS * width, LANES)

    half = width // 2
    pack_rows = samples * pixels + half + 16
    flat_features = features.reshape(samples * pixels, LANES)
    pack = pl.pallas_call(
        pack_kernel,
        out_shape=shape((pack_rows + half + 16, LANES), BF16),
        in_specs=[SMEM] + [ANY] * 3,
        out_specs=VMEM,
        scratch_shapes=[
            pltpu.VMEM((width, LANES), F32),
            pltpu.VMEM(chan_bias.shape, F32),
            pltpu.SemaphoreType.DMA((3,)),
        ],
        compiler_params=params(4),
        cost_estimate=cost(0),
        name="pack",
    )(where, *hbm(aff_w, chan_bias, flat_features))
    map_low = pl.pallas_call(
        low_kernel,
        out_shape=shape(map_w.shape, BF16),
        in_specs=[ANY],
        out_specs=VMEM,
        scratch_shapes=[pltpu.VMEM(map_w.shape, F32), pltpu.SemaphoreType.DMA((layers,))],
        compiler_params=params(8),
        cost_estimate=cost(0),
        name="low",
    )(*hbm(after(map_w, pack)))
    *chan_packs, last_step = spread_over_chan(flat_features, pack, map_low)
    blocks = spread_layers(map_low, "dp")
    kernel, square, latent_rows = pl.pallas_call(
        functools.partial(weights_kernel, samples),
        out_shape=(
            shape((3, width, 3 * LANES), BF16),
            shape((width, LANES), F32),
            shape((16, width), F32),
        ),
        in_specs=[SMEM, ANY, ANY],
        out_specs=(VMEM,) * 3,
        scratch_shapes=[
            pltpu.VMEM((TAPS, width, LANES), F32),
            pltpu.VMEM((latents, 8, width), F32),
            pltpu.SemaphoreType.DMA((TAPS,)),
            pltpu.SemaphoreType.DMA((latents,)),
        ],
        compiler_params=params(8),
        cost_estimate=cost(0),
        name="weights",
    )(seeds.reshape(-1), *hbm(after(conv_w.reshape(TAPS, width, LANES), blocks[1][0]), z_table))
    second = last_step(blocks[2][0], kernel)
    places = [place for _, place in blocks]

    pre, hid, top, picked, map_full = pl.pallas_call(
        functools.partial(mapping_kernel, n_dp, samples, places),
        out_shape=(
            shape((layers, 8, width), F32),
            shape((layers, 8, width), F32),
            shape((8, width), F32),
            shape((2, 8, width), F32),
            shape((layers, width, width), BF16),
        ),
        in_specs=[SMEM] * 2 + [VMEM] * (len(blocks) + 2),
        out_specs=(VMEM,) * 5,
        scratch_shapes=[pltpu.SemaphoreType.DMA((len(places),))],
        compiler_params=params(12),
        cost_estimate=cost(0),
        name="mapping",
    )(where, crossover, *[block for block, _ in blocks], latent_rows, map_b)

    both, first, first_pair = chan_packs
    feat_t, taps, style_rows, aff_full = pl.pallas_call(
        functools.partial(begin_kernel, n_ch, samples, side),
        out_shape=(
            shape((samples, width, pixels), BF16),
            shape((samples, pixels, 3 * LANES), F32),
            shape((8, width), F32),
            shape((width, width), BF16),
        ),
        in_specs=[SMEM] + [VMEM] * 4,
        out_specs=(VMEM,) * 4,
        scratch_shapes=[
            pltpu.VMEM((16, LANES), F32),
            pltpu.VMEM((samples, pixels + 2 * side, 2 * LANES), BF16),
            pltpu.VMEM((3, 2 * LANES, 3 * LANES), BF16),
        ],
        compiler_params=params(16),
        cost_estimate=cost(0),
        name="begin",
    )(where, both, first, kernel, picked)
    second_pair = swap(after(second, taps)[samples * pixels :], "dp", 1)
    feat_t, style_rows, aff_full, wide, small, loss_rows = pl.pallas_call(
        functools.partial(main_kernel, n_ch, samples, side),
        out_shape=(
            shape((samples, width, pixels), BF16),
            shape((8, width), F32),
            shape((width, width), BF16),
            shape((samples, pixels + 16, LANES), F32),
            shape((8 * samples, LANES), F32),
            shape((8 * samples, LANES), F32),
        ),
        in_specs=[SMEM] + [VMEM] * 11 + [SMEM] + [VMEM] * 3,
        out_specs=(VMEM,) * 6,
        scratch_shapes=[
            pltpu.VMEM((16, LANES), F32),
            pltpu.VMEM((pack_rows, LANES), BF16),
            pltpu.VMEM((half + 16, LANES), BF16),
            pltpu.VMEM((samples, pixels + 2 * side, 2 * LANES), BF16),
            pltpu.VMEM((3, 2 * LANES, 3 * LANES), BF16),
            pltpu.VMEM((pixels + 16, 3 * LANES), F32),
        ],
        input_output_aliases={13: 0, 14: 1, 15: 2},
        compiler_params=params(20),
        cost_estimate=cost(0),
        name="main",
    )(
        where,
        first_pair,
        second,
        second_pair,
        taps,
        kernel,
        square,
        aff_w,
        picked,
        chan_bias,
        head,
        rgb_w,
        counted,
        feat_t,
        style_rows,
        aff_full,
    )
    pair_losses = swap(loss_rows, "dp", 1)
    unit, to_sum = pl.pallas_call(
        functools.partial(factor_kernel, samples, side),
        out_shape=(
            shape((samples, 2, TAPS * width // 2, LANES), BF16),
            shape((8 * samples, LANES), F32),
        ),
        in_specs=[SMEM] + [VMEM] * 6,
        out_specs=(VMEM,) * 2,
        scratch_shapes=[pltpu.VMEM((pixels, TAPS * LANES), BF16)],
        compiler_params=params(16),
        cost_estimate=cost(0),
        name="factor",
    )(where, feat_t, wide, small, style_rows, kernel, aff_w)
    unit_pair = swap(unit[:, 1], "dp", 1)

    to_send = jnp.concatenate([to_sum, loss_rows[:4 * samples], pair_losses[:4 * samples]])
    sum_parts = spread_direct(to_send, "chan")
    masks = jnp.concatenate([loss_rows[4 * samples:], pair_losses[4 * samples:]])
    half_rows = TAPS * width // 2 + COUNT_ROWS
    total = pl.pallas_call(
        functools.partial(combine_kernel, n_ch, samples),
        out_shape=shape((half_rows, LANES), BF16),
        in_specs=[VMEM] * (n_ch + 3),
        out_specs=VMEM,
        compiler_params=params(8),
        cost_estimate=cost(0),
        name="combine",
    )(*sum_parts, masks, unit, unit_pair)

    lines = pack_places(samples, layers)[-1]
    pack = pl.pallas_call(
        functools.partial(mapping_back_kernel, n_ch, samples),
        out_shape=shape((lines, width), BF16),
        in_specs=[SMEM] * 2 + [VMEM] * (n_ch + 8),
        out_specs=VMEM,
        scratch_shapes=[pltpu.VMEM((8, width), F32), pltpu.VMEM((lines, width), F32)],
        compiler_params=params(12),
        cost_estimate=cost(0),
        name="mapping_back",
    )(where, crossover, *after(sum_parts, total), masks, pre, hid, top, picked, small, map_full, aff_full)
    spread_pack = spread(pack, "dp")
    packs = [part for part, _ in spread_pack]

    flat_aff = [a.reshape(2 * width, LANES) for a in (aff_w, aff_w_mom, aff_w_ema)]
    tiny = [
        map_b,
        map_b_mom,
        map_b_ema,
        chan_bias,
        chan_bias_mom,
        chan_bias_ema,
        rgb_w,
        rgb_w_mom,
        rgb_w_ema,
        w_avg.reshape(1, width),
    ]
    types = (F32, F32, F32, BF16)
    out_shape = (
        [shape(map_w.shape, t) for t in types]
        + [shape((2 * width, LANES), t) for t in types]
        + [shape(map_b.shape, t) for t in types]
        + [shape(chan_bias.shape, t) for t in types]
        + [shape(rgb_w.shape, t) for t in types]
        + [shape((1, width), F32), shape((1,), F32), shape((1,), F32)]
    )
    depth = layers * latents
    update = lambda: pl.pallas_call(
        functools.partial(update_kernel, n_dp, samples, layers, [p for _, p in spread_pack]),
        out_shape=out_shape,
        in_specs=[SMEM] + [VMEM] * (len(packs) + 6 + len(tiny)),
        out_specs=[ANY] * 23,
        scratch_shapes=[pltpu.VMEM(s.shape, s.dtype) for s in out_shape[:21]]
        + [
            pltpu.SMEM((1,), F32),
            pltpu.SMEM((1,), F32),
            pltpu.VMEM((n_dp * depth, width), BF16),
            pltpu.VMEM((n_dp * depth, width), BF16),
            pltpu.VMEM((n_dp * (lines - 2 * depth), width), BF16),
            pltpu.SemaphoreType.DMA((layers // 2 + 6, 4)),
        ],
        compiler_params=params(20),
        cost_estimate=cost(12),
        name="update",
    )(where, *packs, map_w, map_w_mom, map_w_ema, *flat_aff, *tiny)

    bits = [1 << b for b in range(1, n_dp.bit_length() - 1)]
    for turn, (even_bit, odd_bit) in enumerate(zip(bits, bits[::-1])):
        got = crossed(total, "dp", even_bit, odd_bit)
        if turn == len(bits) - 2:
            got = after(got, packs[1])
        if turn == len(bits) - 1:
            outs = update()
            got = after(got, *outs)
        total = (total.astype(F32) + got.astype(F32)).astype(BF16)
    other = swap(total, "dp", 1)

    conv_params = [flat(conv_w), flat(conv_w_mom), flat(conv_w_ema)]

    def conv_part(turns, grads, earlier):
        ninths = sum(len(n) for _, n in turns)
        return pl.pallas_call(
            functools.partial(conv_kernel, turns),
            out_shape=[shape((TAPS * width, LANES), t) for t in types],
            in_specs=[SMEM] + [VMEM] * (len(grads) + 3) + [ANY] * len(earlier),
            out_specs=[ANY] * 4,
            scratch_shapes=[pltpu.VMEM((ninths * TAPS * width // 18, LANES), t) for t in types]
            + [pltpu.SemaphoreType.DMA((ninths // 3, 4))],
            input_output_aliases={4 + len(grads) + k: k for k in range(len(earlier))},
            compiler_params=params(16),
            cost_estimate=cost(0),
            name="conv_rest" if earlier else "conv_first",
        )(where, *grads, *conv_params, *earlier)

    first_part = conv_part([(True, range(6))], [total], [])
    conv_outs = conv_part([(True, range(6, 9)), (False, range(9))], [total, other], first_part)

    map_outs, aff_outs = outs[0:4], [a.reshape(aff_w.shape) for a in outs[4:8]]
    conv_outs = [a.reshape(conv_w.shape) for a in conv_outs]
    return (
        *map_outs,
        *outs[8:12],
        *aff_outs,
        *outs[12:16],
        *conv_outs,
        *outs[16:20],
        outs[20].reshape(width),
        outs[21].reshape(()),
        outs[22].reshape(()),
    )


def solution(mesh):
    in_specs = (
        P("dp", None, None, "chan"),
        P(),
        P("dp", None),
        P("dp"),
        P("dp"),
        P(),
        P(),
        P(None, "dp", None),
        P(None, "dp", None),
        P(None, "dp", None),
        P(),
        P(),
        P(),
        P(None, None, "chan"),
        P(None, None, "chan"),
        P(None, None, "chan"),
        P(None, "chan"),
        P(None, "chan"),
        P(None, "chan"),
        P(None, None, None, "chan"),
        P(None, None, None, "chan"),
        P(None, None, None, "chan"),
        P(None, "chan"),
        P(None, "chan"),
        P(None, "chan"),
    )
    out_specs = (
        P(None, "dp", None),
        P(None, "dp", None),
        P(None, "dp", None),
        P(None, "dp", None),
        P(),
        P(),
        P(),
        P(),
        P(None, None, "chan"),
        P(None, None, "chan"),
        P(None, None, "chan"),
        P(None, None, "chan"),
        P(None, "chan"),
        P(None, "chan"),
        P(None, "chan"),
        P(None, "chan"),
        P(None, None, None, "chan"),
        P(None, None, None, "chan"),
        P(None, None, None, "chan"),
        P(None, None, None, "chan"),
        P(None, "chan"),
        P(None, "chan"),
        P(None, "chan"),
        P(None, "chan"),
        P(),
        P(),
        P(),
    )
    return jax.shard_map(local, mesh=mesh, in_specs=in_specs, out_specs=out_specs, check_vma=False)
```

```python
import functools

import jax
import jax.numpy as jnp
from jax import lax
from jax.experimental import pallas as pl
from jax.experimental.pallas import tpu as pltpu
from jax.sharding import PartitionSpec as P

MOMENTUM = 0.9
EMA_DECAY = 0.95
AVERAGE_BETA = 0.5
BF16 = jnp.bfloat16
F32 = jnp.float32
TAPS = 9
LANES = 128
COUNT_ROWS = 32
VMEM = pl.BlockSpec(memory_space=pltpu.VMEM)
SMEM = pl.BlockSpec(memory_space=pltpu.SMEM)
ANY = pl.BlockSpec(memory_space=pl.ANY)


def shape(dims, dtype):
    return jax.ShapeDtypeStruct(dims, dtype)


def params(mib):
    return pltpu.CompilerParams(vmem_limit_bytes=mib * 1024 * 1024)


def cost(micros):
    return pl.CostEstimate(flops=int(micros * 1e9), bytes_accessed=0, transcendentals=0)


def hbm(*values):
    return [pltpu.with_memory_space_constraint(value, pltpu.HBM) for value in values]


def after(values, *others):
    return lax.optimization_barrier((values, others))[0]


def swap(value, axis, distance):
    return lax.ppermute(
        value, axis, [(i, i ^ distance) for i in range(lax.axis_size(axis))]
    )


def spread(value, axis):
    size = lax.axis_size(axis)
    beside = swap(value, axis, 1)
    if size != 8:
        parts = [(value, [(0, 0)]), (beside, [(1, 1)])]
        for k in range(2, size, 2):
            part = swap(value, axis, k)
            parts += [(part, [(k, k)]), (swap(part, axis, 1), [(k + 1, k + 1)])]
        return parts
    near = jnp.concatenate([value, beside])
    far = crossed(near, axis, 4, 2)
    corner = crossed(far, axis, 2, 4)
    return [
        (near, [(0, 0), (1, 1)]),
        (far, [(4, 2), (5, 3)]),
        (corner, [(6, 6), (7, 7)]),
        (swap(far, axis, 1), [(3, 5), (2, 4)]),
    ]


def spread_direct(value, axis):
    return [value] + [swap(value, axis, k) for k in range(1, lax.axis_size(axis))]


def spread_over_chan(features, pack, ready):
    n_dp, n_ch = lax.axis_size("dp"), lax.axis_size("chan")
    cut = features.shape[0]
    both = lax.optimization_barrier(jnp.concatenate([pack, swap(features, "dp", 1)]))

    def joint(value, moves):
        pairs = [
            (d * n_ch + a, d * n_ch + b) for d in range(n_dp) for a, b in moves[d % 2]
        ]
        return lax.ppermute(value, ("dp", "chan"), pairs)

    first = joint(both, ([(c, c ^ 1) for c in range(4)], [(c, c ^ 2) for c in range(4)]))
    first_pair = swap(first[cut:], "dp", 1)
    odd = lax.rem(lax.axis_index("dp"), 2) == 1

    def last_step(*others):
        value = after(jnp.where(odd, first, both), *others)
        return joint(value, ([(1, 2), (2, 1)], [(1, 0), (2, 3)]))

    return both, first, first_pair, last_step


def crossed(value, axis, even_distance, odd_distance):
    size = lax.axis_size(axis)
    pairs = [(i, i ^ (odd_distance if i % 2 else even_distance)) for i in range(size)]
    return lax.ppermute(value, axis, pairs)


def spread_layers(value, axis):
    size = lax.axis_size(axis)
    beside = swap(value, axis, 1)
    parts = [(value, (0, 0, 0)), (beside, (0, 1, 1))]
    if size != 8:
        for k in range(2, size, 2):
            part = swap(value, axis, k)
            parts += [(part, (0, k, k)), (swap(part, axis, 1), (0, k + 1, k + 1))]
        return parts
    far = crossed(value, axis, 2, 4)
    far_beside = crossed(beside, axis, 2, 4)
    corner = crossed(far, axis, 4, 2)
    parts += [(far, (0, 2, 4)), (far_beside, (0, 3, 5)), (corner, (0, 6, 6))]
    parts += [(swap(far, axis, 1), (0, 5, 3)), (swap(far_beside, axis, 1), (0, 4, 2))]
    parts += [(swap(corner, axis, 1), (0, 7, 7))]
    return parts


def silu_slope(preact):
    sig = jax.nn.sigmoid(preact)
    return sig * (1.0 + preact * (1.0 - sig))


def pieces(value, count):
    out = []
    for _ in range(count):
        part = value.astype(BF16)
        out.append(part)
        value = value - part.astype(F32)
    return out


def advance(param, moment, average, grad, rate):
    moment_new = MOMENTUM * moment + grad
    param_new = param - rate * (grad + MOMENTUM * moment_new)
    average_new = EMA_DECAY * average + (1.0 - EMA_DECAY) * param_new
    return param_new, moment_new, average_new, param_new.astype(BF16)


def dot(a, b):
    return jnp.dot(a, b, preferred_element_type=F32)


def dot_nt(a, b):
    return lax.dot_general(a, b, (((1,), (1,)), ((), ())), preferred_element_type=F32)


def dot_tn(a, b):
    return lax.dot_general(a, b, (((0,), (0,)), ((), ())), preferred_element_type=F32)


def pack_kernel(where, aff_w, bias, features, pack, aff_stage, bias_stage, sems):
    half = aff_stage.shape[0] // 2
    rows = features.shape[0]
    pair = lax.rem(where[0], 2)
    feat_copy = pltpu.make_async_copy(features, pack.at[pl.ds(0, rows), :], sems.at[0])
    aff_copy = pltpu.make_async_copy(aff_w.at[0], aff_stage, sems.at[1])
    bias_copy = pltpu.make_async_copy(bias, bias_stage, sems.at[2])
    for copy in (feat_copy, aff_copy, bias_copy):
        copy.start()
    bias_copy.wait()
    hi, mid, lo = pieces(bias_stage[0:1, :], 3)
    lines = jnp.concatenate(
        [hi.astype(F32), mid.astype(F32), lo.astype(F32), jnp.zeros((13, LANES), F32)], axis=0
    )
    aff_copy.wait()
    for turn, owner in enumerate((pair, 1 - pair)):
        at = rows + turn * (half + 16)
        start = pl.multiple_of(owner * half, half)
        pack[pl.ds(at, half), :] = aff_stage[pl.ds(start, half), :].astype(BF16)
        pack[pl.ds(at + half, 16), :] = lines.astype(BF16)
    feat_copy.wait()


def low_kernel(map_w, map_low, stage, sems):
    layers = map_w.shape[0]
    copies = [
        pltpu.make_async_copy(map_w.at[layer], stage.at[layer], sems.at[layer])
        for layer in range(layers)
    ]
    for copy in copies:
        copy.start()
    for layer in range(layers):
        copies[layer].wait()
        map_low[layer] = stage[layer].astype(BF16)


def mapping_kernel(n_dp, samples, places, *refs):
    refs = list(refs)

    def take(count):
        got = refs[:count]
        del refs[:count]
        return got

    where, crossover = take(2)
    parts = take(len(places))
    latent_rows, map_b = take(2)
    pre_out, hid_out, top_out, picked_out, map_full, sem_map = refs
    layers, share, width = parts[0].shape
    dp = where[0]
    odd = lax.rem(dp, 2)
    moves = []
    for part, (first, even_k, odd_k) in zip(parts, places):
        k = jnp.where(odd == 1, odd_k, even_k)
        at = pl.multiple_of(lax.bitwise_xor(dp, k) * share, share)
        moves.append((part, first, pl.ds(at, share)))
    whole_tiles = share % 16 == 0
    if not whole_tiles:
        copies = [
            pltpu.make_async_copy(
                part, map_full.at[pl.ds(first, part.shape[0]), at, :], sem_map.at[i]
            )
            for i, (part, first, at) in enumerate(moves)
        ]
        for copy in copies:
            copy.start()
        for copy in copies:
            copy.wait()

    def bring(layer):
        for part, first, at in moves:
            if whole_tiles and first <= layer < first + part.shape[0]:
                map_full[layer, at, :] = part[layer - first]

    bring(0)
    bring(1)
    hidden = latent_rows[...]
    for layer in range(layers):
        low = hidden.astype(BF16)
        preact = dot(low, map_full[layer]) + map_b[pl.ds(layer, 1), :]
        if layer + 2 < layers:
            bring(layer + 2)
        hid_out[layer] = low.astype(F32)[0:8]
        pre_out[layer] = preact[0:8]
        hidden = preact * jax.nn.sigmoid(preact)
    top_out[...] = hidden[0:8]
    low = hidden.astype(BF16).astype(F32)
    for j in range(2):
        chosen = []
        for s in range(samples):
            first = crossover[2 + s] > j
            chosen.append(
                jnp.where(first, low[2 * s : 2 * s + 1, :], low[2 * s + 1 : 2 * s + 2, :])
            )
        chosen.append(jnp.zeros((8 - samples, width), F32))
        picked_out[j] = jnp.concatenate(chosen, axis=0)


def weights_kernel(samples, seeds, conv_w, z_table, kernel, square, latent_rows, stage, rows, sems, sem_z):
    latents = 2 * samples
    z_copies = []
    for n in range(latents):
        at = pl.multiple_of((seeds[n] // 8) * 8, 8)
        z_copies.append(pltpu.make_async_copy(z_table.at[pl.ds(at, 8), :], rows.at[n], sem_z.at[n]))
    copies = [pltpu.make_async_copy(conv_w.at[t], stage.at[t], sems.at[t]) for t in range(TAPS)]
    for copy in z_copies + copies:
        copy.start()
    total = jnp.zeros(square.shape, F32)
    for tap in range(TAPS):
        copies[tap].wait()
        low = stage[tap].astype(BF16)
        kernel[tap // 3, :, pl.ds((tap % 3) * LANES, LANES)] = low
        wide = low.astype(F32)
        total = total + wide * wide
    square[...] = total
    normed = []
    for n in range(latents):
        z_copies[n].wait()
        row = rows[n, pl.ds(lax.rem(seeds[n], 8), 1), :]
        scale = lax.rsqrt(jnp.mean(row * row, axis=1, keepdims=True) + 1e-08)
        normed.append(row * scale)
    normed.append(jnp.zeros((16 - latents, rows.shape[2]), F32))
    latent_rows[...] = jnp.concatenate(normed, axis=0)


def bring_blocks(
    blocks, samples, side, where, picked, bias_full, style_rows, feat_t, aff_full, kernel, padded, rows
):
    width = aff_full.shape[0]
    half, pixels = width // 2, side * side
    dp, ch = where[0], where[1]
    pair = lax.rem(dp, 2)
    mine = pl.ds(pl.multiple_of(pair * half, half), half)
    other = pl.ds(pl.multiple_of((1 - pair) * half, half), half)
    chosen = picked[0].astype(BF16)
    blank = jnp.zeros((side, padded.shape[2]), BF16)
    for s in range(samples):
        padded[s, pl.ds(0, side), :] = blank
        padded[s, pl.ds(side + pixels, side), :] = blank
    for slot, (source, top, tail_at, other_source, other_tail_at, k) in enumerate(blocks):
        lane = pl.ds(pl.multiple_of(lax.bitwise_xor(ch, k) * LANES, LANES), LANES)
        place = pl.ds(slot * LANES, LANES)
        aff_full[mine, lane] = source[pl.ds(tail_at, half), :]
        aff_full[other, lane] = other_source[pl.ds(other_tail_at, half), :]
        bias_full[...] = source[pl.ds(tail_at + half, 16), :].astype(F32)
        bias_row = bias_full[0:1, :] + bias_full[1:2, :] + bias_full[2:3, :]
        style = (dot(chosen, aff_full[:, lane]) + bias_row).astype(BF16)
        style_rows[:, lane] = style.astype(F32)
        for dy in range(3):
            rows[dy, place, :] = kernel[dy, lane, :]
        for s in range(samples):
            value = source[pl.ds(top + s * pixels, pixels), :]
            feat_t[s, lane, :] = value.T
            padded[s, pl.ds(side, pixels), place] = value * style[s : s + 1, :]


def begin_kernel(n_ch, samples, side, *refs):
    where, both, first, kernel, picked = refs[:5]
    feat_t, taps, style_rows, aff_full, bias_full, padded, rows = refs[5:]
    width = aff_full.shape[0]
    half, pixels = width // 2, side * side
    feats, tail_rows = samples * pixels, half + 16
    partner_tail = feats + tail_rows
    style_rows[...] = jnp.zeros_like(style_rows)
    blocks = (
        (both, 0, feats, both, partner_tail, 0),
        (first, 0, feats, first, partner_tail, 1 + lax.rem(where[0], 2)),
    )
    bring_blocks(
        blocks, samples, side, where, picked, bias_full, style_rows, feat_t, aff_full, kernel, padded, rows
    )
    chunk = min(256, pixels)
    for s in range(samples):
        for r in range(pixels // chunk):
            total = dot(padded[s, pl.ds(r * chunk, chunk), :], rows[0])
            total = total + dot(padded[s, pl.ds(side + r * chunk, chunk), :], rows[1])
            total = total + dot(padded[s, pl.ds(2 * side + r * chunk, chunk), :], rows[2])
            taps[s, pl.ds(r * chunk, chunk), :] = total


def main_kernel(n_ch, samples, side, *refs):
    where, first_pair, second, second_pair, earlier, kernel, square_in = refs[:7]
    aff_w, picked, bias, head, rgb_w, counted = refs[7:13]
    feat_t, style_rows, aff_full, wide, small, loss_rows = refs[16:22]
    bias_full, late, late_tail, padded, kernel_rows, taps = refs[22:]
    width = aff_full.shape[0]
    half, pixels = width // 2, side * side
    feats, tail_rows = samples * pixels, half + 16
    cut = second.shape[0] - second_pair.shape[0]
    partner_tail, partner_feats = feats + tail_rows, feats + 2 * tail_rows
    dp, ch = where[0], where[1]
    pair = lax.rem(dp, 2)
    at_end = jnp.logical_or(ch == 0, ch == n_ch - 1)
    is_held = at_end == (pair == 1)

    @pl.when(is_held)
    def _():
        late[...] = second[pl.ds(0, feats + tail_rows), :]
        late_tail[...] = second[pl.ds(partner_tail, tail_rows), :]

    @pl.when(jnp.logical_not(is_held))
    def _():
        late[pl.ds(0, feats), :] = second_pair[pl.ds(partner_feats - cut, feats), :]
        late[pl.ds(feats, tail_rows), :] = second_pair[pl.ds(partner_tail - cut, tail_rows), :]
        late_tail[...] = second_pair[pl.ds(feats - cut, tail_rows), :]

    blocks = (
        (first_pair, partner_feats - cut, partner_tail - cut, first_pair, feats - cut, 2 - pair),
        (late, 0, feats, late_tail, 0, 3),
    )
    bring_blocks(
        blocks, samples, side, where, picked, bias_full, style_rows, feat_t, aff_full, kernel, padded, kernel_rows
    )
    square = square_in[...]
    colour_aff = aff_w[1].astype(BF16)
    style1 = dot(picked[1].astype(BF16), colour_aff) + bias[1:2, :]
    style1 = style1.astype(BF16).astype(F32)
    colour = rgb_w[...].astype(BF16)
    colour_wide = colour.astype(F32)
    colour_rows = jnp.concatenate([colour_wide, jnp.zeros((13, LANES), F32)], axis=0).astype(BF16)
    head_rows = jnp.concatenate(
        [head[...].astype(F32), jnp.zeros((13, pixels), F32)], axis=0
    ).astype(BF16)
    conv_bias = bias[2:3, :]
    chunk = min(256, pixels)
    steps = pixels // chunk
    column = lax.rem(lax.broadcasted_iota(jnp.int32, (chunk, LANES), 0), side)
    not_first, not_last = column > 0, column < side - 1
    small[...] = jnp.zeros_like(small)
    loss_rows[...] = jnp.zeros_like(loss_rows)
    taps[pl.ds(0, 8), :] = jnp.zeros((8, 3 * LANES), F32)
    taps[pl.ds(8 + pixels, 8), :] = jnp.zeros((8, 3 * LANES), F32)

    for s in range(samples):
        wide[s, pl.ds(0, 8), :] = jnp.zeros((8, LANES), F32)
        wide[s, pl.ds(8 + pixels, 8), :] = jnp.zeros((8, LANES), F32)
        style_col = jnp.broadcast_to(style_rows[pl.ds(s, 1), :], (LANES, width)).T
        demod = lax.rsqrt(
            jnp.sum(style_col * style_col * square, axis=0, keepdims=True) + 1e-08
        )
        style_colour = style1[s : s + 1, :]
        for r in range(steps):
            total = earlier[s, pl.ds(r * chunk, chunk), :]
            for dy in range(3):
                total = total + dot(
                    padded[s, pl.ds(dy * side + r * chunk, chunk), :], kernel_rows[dy]
                )
            taps[pl.ds(8 + r * chunk, chunk), :] = total
        mixed = jnp.zeros((3, LANES), F32)
        g_style1 = jnp.zeros((1, LANES), F32)
        g_bias = jnp.zeros((1, LANES), F32)
        g_demod = jnp.zeros((1, LANES), F32)
        for r in range(steps):
            left = taps[pl.ds(7 + r * chunk, chunk), pl.ds(0, LANES)]
            centre = taps[pl.ds(8 + r * chunk, chunk), pl.ds(LANES, LANES)]
            right = taps[pl.ds(9 + r * chunk, chunk), pl.ds(2 * LANES, LANES)]
            conv_out = centre + jnp.where(not_first, left, 0.0) + jnp.where(not_last, right, 0.0)
            scaled = conv_out * demod + conv_bias
            sig = jax.nn.sigmoid(scaled)
            activated = scaled * sig
            act_mod = (activated * style_colour).astype(BF16)
            mixed = mixed + dot(head_rows[:, r * chunk : (r + 1) * chunk], act_mod)[0:3]
            g_act = dot_tn(head_rows[:, r * chunk : (r + 1) * chunk], colour_rows)
            g_style1 = g_style1 + jnp.sum(g_act * activated, axis=0, keepdims=True)
            g_scaled = g_act * style_colour * (sig * (1.0 + scaled * (1.0 - sig)))
            g_bias = g_bias + jnp.sum(g_scaled, axis=0, keepdims=True)
            g_demod = g_demod + jnp.sum(g_scaled * conv_out, axis=0, keepdims=True)
            wide[s, pl.ds(8 + r * chunk, chunk), :] = g_scaled * demod
        logit = jnp.sum(
            jnp.sum(mixed * colour_wide, axis=0, keepdims=True), axis=1, keepdims=True
        )
        loss_rows[pl.ds(s, 1), :] = jnp.broadcast_to(logit, (1, LANES))
        loss_rows[pl.ds(4 * samples + s, 1), :] = jnp.full((1, LANES), counted[2 + samples + s], jnp.int32).astype(F32)
        small[pl.ds(8 * s, 1), :] = g_style1
        small[pl.ds(8 * s + 1, 1), :] = g_bias
        small[pl.ds(8 * s + 2, 3), :] = mixed
        small[pl.ds(8 * s + 5, 1), :] = g_demod * demod * demod * demod


def factor_kernel(samples, side, where, feat_t, wide, small, style_rows, kernel, aff_w, unit, to_sum, shifted):
    width = feat_t.shape[1]
    pixels = side * side
    pair = lax.rem(where[0], 2)
    half = TAPS * width // 2
    chunk = min(256, pixels)
    steps = pixels // chunk
    column = lax.rem(lax.broadcasted_iota(jnp.int32, (chunk, LANES), 0), side)
    not_first, not_last = column > 0, column < side - 1
    to_sum[...] = jnp.zeros_like(to_sum)
    colour_aff = aff_w[1].astype(BF16).astype(F32)
    for s in range(samples):
        style_col = jnp.broadcast_to(style_rows[pl.ds(s, 1), :], (LANES, width)).T
        for r in range(steps):
            before = jnp.where(not_last, wide[s, pl.ds(9 + r * chunk, chunk), :], 0.0)
            centre = wide[s, pl.ds(8 + r * chunk, chunk), :]
            after_it = jnp.where(not_first, wide[s, pl.ds(7 + r * chunk, chunk), :], 0.0)
            for dx, value in enumerate((before, centre, after_it)):
                value = value.astype(BF16)
                for dy in range(3):
                    lane = pl.ds((3 * dy + dx) * LANES, LANES)
                    start = r * chunk + (dy - 1) * side
                    low_at, high_at = max(start, 0), min(start + chunk, pixels)
                    shifted[pl.ds(low_at, high_at - low_at), lane] = value[
                        low_at - start : high_at - start, :
                    ]
        for dx in range(3):
            blank = jnp.zeros((side, LANES), BF16)
            shifted[pl.ds(pixels - side, side), pl.ds(dx * LANES, LANES)] = blank
            shifted[pl.ds(0, side), pl.ds((6 + dx) * LANES, LANES)] = blank
        factor = small[pl.ds(8 * s + 5, 1), :]
        g_style = jnp.zeros((width, LANES), F32)
        for first in range(0, TAPS, 2):
            count = min(2, TAPS - first)
            block = dot(feat_t[s], shifted[:, pl.ds(first * LANES, count * LANES)])
            for tap in range(first, first + count):
                raw = block[:, (tap - first) * LANES : (tap - first + 1) * LANES]
                weight = kernel[tap // 3, :, pl.ds((tap % 3) * LANES, LANES)].astype(F32)
                inner = raw - style_col * (weight * factor)
                g_style = g_style + weight * inner
                value = (style_col * inner).astype(BF16)
                top = tap * width
                for h in range(2):
                    low_at, high_at = max(top, h * half), min(top + width, (h + 1) * half)
                    if low_at < high_at:
                        slot = 1 - pair if h else pair
                        unit[s, slot, pl.ds(low_at - h * half, high_at - low_at), :] = value[
                            low_at - top : high_at - top, :
                        ]
        for at, value in ((0, g_style), (4, colour_aff * small[pl.ds(8 * s, 1), :])):
            row = jnp.sum(value.T, axis=0, keepdims=True)
            for part in range(width // LANES):
                to_sum[pl.ds(8 * s + at + part, 1), :] = row[:, part * LANES : (part + 1) * LANES]


def summed(parts, row):
    values = [part[pl.ds(row, 1), :] for part in parts]
    while len(values) > 1:
        values = [values[i] + values[i + 1] for i in range(0, len(values), 2)]
    return values[0]


def logit_grad(parts, masks, samples, s):
    at = 4 * samples * (s // samples) + s % samples
    logit = summed(parts, 8 * samples + at)
    mask = masks[pl.ds(at, 1), :]
    return -mask * jax.nn.sigmoid(-logit), mask * jax.nn.softplus(-logit), mask


def combine_kernel(n_ch, samples, *refs):
    parts, (masks, unit, unit_pair, out) = refs[:n_ch], refs[n_ch:]
    half = unit_pair.shape[1]
    grads, total = [], jnp.zeros((1, LANES), F32)
    for s in range(2 * samples):
        grad, _, mask = logit_grad(parts, masks, samples, s)
        grads.append(grad)
        total = total + mask
    block = half // 9
    for b in range(9):
        here = pl.ds(b * block, block)
        value = jnp.zeros((block, LANES), F32)
        for s in range(samples):
            value = value + grads[s] * unit[s, 0, here, :].astype(F32)
            value = value + grads[samples + s] * unit_pair[s, here, :].astype(F32)
        out[here, :] = value.astype(BF16)
    out[pl.ds(half, COUNT_ROWS), :] = jnp.broadcast_to(total, (COUNT_ROWS, LANES)).astype(BF16)


def pack_places(samples, layers):
    latents = 2 * samples
    style = 2 * layers * latents + latents
    colour = style + 2 * samples
    w_total = colour + 2 * samples
    return style, colour, w_total, -(-(w_total + 3) // 16) * 16


def mapping_back_kernel(n_ch, samples, where, crossover, *refs):
    parts = refs[:n_ch]
    masks, pre, hid, top, picked, small, map_full, aff_full, pack_out, rows, pack = refs[n_ch:]
    layers, _, width = map_full.shape
    latents = 2 * samples
    style_at, colour_at, w_at, _ = pack_places(samples, layers)
    ch = where[1]
    grads = [logit_grad(parts, masks, samples, s) for s in range(samples)]

    def wide_sum(at):
        return jnp.concatenate([summed(parts, at + part) for part in range(width // LANES)], axis=1)

    pack[...] = jnp.zeros_like(pack)

    def put(line, lane, size, value, count):
        for i, part in enumerate(pieces(value, count)):
            pack[pl.ds(line + i, 1), pl.ds(lane, size)] = part.astype(F32)

    style_rows = []
    half_lane = lax.broadcasted_iota(jnp.int32, (1, LANES), 1) < LANES // 2
    for s in range(samples):
        grad = grads[s][0]
        style_row = grad[:, :1] * wide_sum(8 * s)
        rows[pl.ds(s, 1), :] = style_row
        style_rows.append(style_row)
        own = rows[pl.ds(s, 1), pl.ds(pl.multiple_of(ch * LANES, LANES), LANES)]
        short = grad
        put(style_at + 2 * s, 0, LANES, own, 2)
        put(style_at + 2 * s, LANES, LANES, short * small[pl.ds(8 * s, 1), :], 2)
        put(style_at + 2 * s, 2 * LANES, LANES, short * small[pl.ds(8 * s + 1, 1), :], 2)
        loss_count = jnp.where(half_lane, grads[s][1], grads[s][2])
        put(style_at + 2 * s, 3 * LANES, LANES, loss_count, 2)
        for c in range(3):
            value = short * small[pl.ds(8 * s + 2 + c, 1), :]
            put(colour_at + 2 * s, c * LANES, LANES, value, 2)
        for j in range(2):
            line = 2 * layers * latents + 2 * s + j
            pack[pl.ds(line, 1), :] = picked[j, pl.ds(s, 1), :]
    w_total = top[pl.ds(0, 1), :]
    for n in range(1, latents):
        w_total = w_total + top[pl.ds(n, 1), :]
    put(w_at, 0, width, w_total, 3)

    def back(value, weights):
        hi, lo = pieces(value, 2)
        both = jnp.concatenate([hi.astype(F32), lo.astype(F32)], axis=0).astype(BF16)
        out = dot_nt(both, weights)
        return out[0:8] + out[8:16]

    pad = [jnp.zeros((8 - samples, width), F32)]
    from_conv = back(jnp.concatenate(style_rows + pad, axis=0), aff_full[...])
    g_rows = []
    for s in range(samples):
        conv_row = from_conv[s : s + 1, :]
        colour_row = grads[s][0][:, :1] * wide_sum(8 * s + 4)
        to_first = [jnp.full((1, width), crossover[2 + s], jnp.int32) > j for j in range(2)]
        g_rows.append(
            jnp.where(to_first[0], conv_row, 0.0) + jnp.where(to_first[1], colour_row, 0.0)
        )
        g_rows.append(
            jnp.where(to_first[0], 0.0, conv_row) + jnp.where(to_first[1], 0.0, colour_row)
        )
    g_rows.append(jnp.zeros((8 - latents, width), F32))
    g_hidden = jnp.concatenate(g_rows, axis=0)
    for layer in reversed(range(layers)):
        g_pre = g_hidden * silu_slope(pre[layer])
        pack[pl.ds(layer * latents, latents), :] = g_pre[0:latents]
        pack[pl.ds((layers + layer) * latents, latents), :] = hid[layer][0:latents]
        if layer > 0:
            g_hidden = back(g_pre, map_full[layer])
    pack_out[...] = pack[...].astype(BF16)


def update_kernel(n_dp, samples, layers, places, where, *refs):
    packs, refs = refs[: len(places)], refs[len(places) :]
    (map_w, map_m, map_e, aff_w, aff_m, aff_e) = refs[:6]
    (map_b, map_bm, map_be, bias, bias_m, bias_e, rgb, rgb_m, rgb_e, w_avg) = refs[6:16]
    outs, refs = refs[16:39], refs[39:]
    map_new, aff_new, map_b_new, bias_new, rgb_new = (refs[4 * i : 4 * i + 4] for i in range(5))
    w_avg_new, loss_new, count_new, g_pre, hid, extra, sems = refs[20:]
    map_outs, aff_outs = outs[0:4], outs[4:8]
    map_b_outs, bias_outs, rgb_outs = outs[8:12], outs[12:16], outs[16:20]
    w_avg_out, loss_out, count_out = outs[20:23]
    latents = 2 * samples
    depth = layers * latents
    style_at, colour_at, w_at, lines = pack_places(samples, layers)
    style_at, colour_at, w_at = (at - 2 * depth for at in (style_at, colour_at, w_at))
    more = lines - 2 * depth
    dp = where[0]
    share, width = map_w.shape[1:]

    odd = lax.rem(dp, 2)
    for part, place in zip(packs, places):
        for index, (even_k, odd_k) in enumerate(place):
            owner = lax.bitwise_xor(dp, jnp.where(odd == 1, odd_k, even_k))
            top = index * lines
            for target, start, size in ((g_pre, 0, depth), (hid, depth, depth), (extra, 2 * depth, more)):
                at = pl.multiple_of(owner * size, size)
                target[pl.ds(at, size), :] = part[pl.ds(top + start, size), :]
    every = extra[...].astype(F32)
    kind = lax.rem(lax.broadcasted_iota(jnp.int32, every.shape, 0), more)

    def total_of(first, count):
        chosen = jnp.logical_and(kind >= first, kind < first + count)
        return jnp.sum(jnp.where(chosen, every, 0.0), axis=0, keepdims=True)

    total = total_of(style_at, 2 * samples)
    count = total[:, width - LANES // 2 : width - LANES // 2 + 1]
    inverse = 1.0 / count
    copies = []

    def send(buffers, targets, at, sem):
        for k, (buffer, target) in enumerate(zip(buffers, targets)):
            if at is not None:
                buffer, target = buffer.at[at], target.at[at]
            copy = pltpu.make_async_copy(buffer, target, sems.at[sem, k])
            copy.start()
            copies.append(copy)

    colour = total_of(colour_at, 2 * samples)
    for c in range(3):
        row = pl.ds(c, 1)
        lane = slice(c * LANES, (c + 1) * LANES)
        new = advance(bias[row, :], bias_m[row, :], bias_e[row, :], total[:, lane] * inverse, 50.0)
        for out, value in zip(bias_new[:3], new[:3]):
            out[row, :] = value
        new = advance(rgb[row, :], rgb_m[row, :], rgb_e[row, :], colour[:, lane] * inverse, 1.0)
        for out, value in zip(rgb_new[:3], new[:3]):
            out[row, :] = value
    bias_new[3][...] = bias_new[0][...].astype(BF16)
    rgb_new[3][...] = rgb_new[0][...].astype(BF16)
    mean = total_of(w_at, 3) * (1.0 / (n_dp * latents))
    w_avg_new[...] = w_avg[...] + (1.0 - AVERAGE_BETA) * (mean - w_avg[...])
    loss_new[0] = jnp.sum(total[:, width - LANES : width - LANES + 1])
    count_new[0] = jnp.sum(count)
    send(bias_new, bias_outs, None, layers // 2 + 2)
    send(rgb_new, rgb_outs, None, layers // 2 + 3)
    send((w_avg_new, loss_new, count_new), (w_avg_out, loss_out, count_out), None, layers // 2 + 4)

    own = pltpu.roll(hid[...].astype(F32), lax.rem(width - dp * share, width), 1)[:, :LANES]
    lane = lax.broadcasted_iota(jnp.int32, own.shape, 1)
    own = jnp.where(lane < share, own, jnp.where(lane == share, 1.0, 0.0))
    layer_of = lax.rem(lax.broadcasted_iota(jnp.int32, own.shape, 0), depth) // latents
    for layer in range(layers):
        mine = jnp.where(layer_of == layer, own, 0.0).astype(BF16)
        grads = dot_tn(mine, g_pre[...]) * inverse
        new = advance(map_w[layer], map_m[layer], map_e[layer], grads[0:share], 30.0)
        for out, value in zip(map_new, new):
            out[layer] = value
        row = pl.ds(layer, 1)
        new = advance(
            map_b[row, :], map_bm[row, :], map_be[row, :], grads[share : share + 1], 30.0
        )
        for out, value in zip(map_b_new[:3], new[:3]):
            out[row, :] = value
        if layer % 2:
            send(map_new, map_outs, pl.ds(layer - 1, 2), layer // 2)
    map_b_new[3][...] = map_b_new[0][...].astype(BF16)
    send(map_b_new, map_b_outs, None, layers // 2 + 5)
    for j in range(2):
        chosen = jnp.zeros(every.shape, F32)
        for piece in range(2):
            here = jnp.logical_and(kind >= style_at, kind < style_at + 2 * samples)
            here = jnp.logical_and(here, lax.rem(kind - style_at + 2, 2) == piece)
            moved = pltpu.roll(every, style_at + piece - j, 0)
            chosen = jnp.where(here, moved, chosen)
        grad = dot_tn(chosen.astype(BF16), extra[:, pl.ds(j * LANES, LANES)]) * inverse
        here = pl.ds(j * width, width)
        new = advance(aff_w[here, :], aff_m[here, :], aff_e[here, :], grad, 30.0)
        for out, value in zip(aff_new, new):
            out[here, :] = value
        send(aff_new, aff_outs, here, layers // 2 + j)
    for copy in copies:
        copy.wait()


def conv_kernel(turns, where, *refs):
    grads, refs = refs[: len(turns)], refs[len(turns) :]
    param, moment, average = refs[:3]
    outs, buffers, sems = refs[-9:-5], refs[-5:-1], refs[-1]
    half = grads[0].shape[0] - COUNT_ROWS
    depth = half // 9
    pair = lax.rem(where[0], 2)
    copies, at = [], 0
    for turn, (grad, (mine, ninths)) in enumerate(zip(grads, turns)):
        start = pl.multiple_of((pair if mine else 1 - pair) * half, half)
        inverse = 1.0 / grad[pl.ds(half, 16), :].astype(F32)[0:1]
        for n in ninths:
            here = pl.ds(at * depth, depth)
            there = pl.ds(pl.multiple_of(start + n * depth, depth), depth)
            at += 1
            value = grad[pl.ds(n * depth, depth), :].astype(F32) * inverse
            new = advance(param[there, :], moment[there, :], average[there, :], value, 5.0)
            for k in range(4):
                buffers[k][here, :] = new[k]
            if n % 3 == 2:
                for k in range(4):
                    copy = pltpu.make_async_copy(
                        buffers[k].at[pl.ds((at - 3) * depth, 3 * depth), :],
                        outs[k].at[pl.ds(pl.multiple_of(start + (n - 2) * depth, depth), 3 * depth), :],
                        sems.at[at // 3 - 1, k],
                    )
                    copy.start()
                    copies.append(copy)
    for copy in copies:
        copy.wait()


def local(
    features,
    z_table,
    seeds,
    crossover,
    counted,
    head,
    w_avg,
    map_w,
    map_w_mom,
    map_w_ema,
    map_b,
    map_b_mom,
    map_b_ema,
    aff_w,
    aff_w_mom,
    aff_w_ema,
    chan_bias,
    chan_bias_mom,
    chan_bias_ema,
    conv_w,
    conv_w_mom,
    conv_w_ema,
    rgb_w,
    rgb_w_mom,
    rgb_w_ema,
):
    samples, side = features.shape[0], features.shape[1]
    pixels = side * side
    layers, share, width = map_w.shape
    n_dp, n_ch = lax.axis_size("dp"), lax.axis_size("chan")
    latents = 2 * samples
    where = jnp.stack([lax.axis_index("dp"), lax.axis_index("chan")]).astype(jnp.int32)
    flat = lambda a: a.reshape(TAPS * width, LANES)

    half = width // 2
    pack_rows = samples * pixels + half + 16
    flat_features = features.reshape(samples * pixels, LANES)
    pack = pl.pallas_call(
        pack_kernel,
        out_shape=shape((pack_rows + half + 16, LANES), BF16),
        in_specs=[SMEM] + [ANY] * 3,
        out_specs=VMEM,
        scratch_shapes=[
            pltpu.VMEM((width, LANES), F32),
            pltpu.VMEM(chan_bias.shape, F32),
            pltpu.SemaphoreType.DMA((3,)),
        ],
        compiler_params=params(4),
        cost_estimate=cost(0),
        name="pack",
    )(where, *hbm(aff_w, chan_bias, flat_features))
    map_low = pl.pallas_call(
        low_kernel,
        out_shape=shape(map_w.shape, BF16),
        in_specs=[ANY],
        out_specs=VMEM,
        scratch_shapes=[pltpu.VMEM(map_w.shape, F32), pltpu.SemaphoreType.DMA((layers,))],
        compiler_params=params(8),
        cost_estimate=cost(0),
        name="low",
    )(*hbm(after(map_w, pack)))
    *chan_packs, last_step = spread_over_chan(flat_features, pack, map_low)
    blocks = spread_layers(map_low, "dp")
    numbers = jnp.concatenate([where, *after([crossover, counted], blocks[1][0])])
    kernel, square, latent_rows = pl.pallas_call(
        functools.partial(weights_kernel, samples),
        out_shape=(
            shape((3, width, 3 * LANES), BF16),
            shape((width, LANES), F32),
            shape((16, width), F32),
        ),
        in_specs=[SMEM, ANY, ANY],
        out_specs=(VMEM,) * 3,
        scratch_shapes=[
            pltpu.VMEM((TAPS, width, LANES), F32),
            pltpu.VMEM((latents, 8, width), F32),
            pltpu.SemaphoreType.DMA((TAPS,)),
            pltpu.SemaphoreType.DMA((latents,)),
        ],
        compiler_params=params(8),
        cost_estimate=cost(0),
        name="weights",
    )(seeds.reshape(-1), *hbm(after(conv_w.reshape(TAPS, width, LANES), blocks[1][0], numbers), z_table))
    second = last_step(blocks[2][0], kernel)
    places = [place for _, place in blocks]

    pre, hid, top, picked, map_full = pl.pallas_call(
        functools.partial(mapping_kernel, n_dp, samples, places),
        out_shape=(
            shape((layers, 8, width), F32),
            shape((layers, 8, width), F32),
            shape((8, width), F32),
            shape((2, 8, width), F32),
            shape((layers, width, width), BF16),
        ),
        in_specs=[SMEM] * 2 + [VMEM] * (len(blocks) + 2),
        out_specs=(VMEM,) * 5,
        scratch_shapes=[pltpu.SemaphoreType.DMA((len(places),))],
        compiler_params=params(12),
        cost_estimate=cost(0),
        name="mapping",
    )(where, numbers, *[block for block, _ in blocks], latent_rows, map_b)

    both, first, first_pair = chan_packs
    feat_t, taps, style_rows, aff_full = pl.pallas_call(
        functools.partial(begin_kernel, n_ch, samples, side),
        out_shape=(
            shape((samples, width, pixels), BF16),
            shape((samples, pixels, 3 * LANES), F32),
            shape((8, width), F32),
            shape((width, width), BF16),
        ),
        in_specs=[SMEM] + [VMEM] * 4,
        out_specs=(VMEM,) * 4,
        scratch_shapes=[
            pltpu.VMEM((16, LANES), F32),
            pltpu.VMEM((samples, pixels + 2 * side, 2 * LANES), BF16),
            pltpu.VMEM((3, 2 * LANES, 3 * LANES), BF16),
        ],
        compiler_params=params(16),
        cost_estimate=cost(0),
        name="begin",
    )(where, both, first, kernel, picked)
    second_pair = swap(after(second, taps)[samples * pixels :], "dp", 1)
    feat_t, style_rows, aff_full, wide, small, loss_rows = pl.pallas_call(
        functools.partial(main_kernel, n_ch, samples, side),
        out_shape=(
            shape((samples, width, pixels), BF16),
            shape((8, width), F32),
            shape((width, width), BF16),
            shape((samples, pixels + 16, LANES), F32),
            shape((8 * samples, LANES), F32),
            shape((8 * samples, LANES), F32),
        ),
        in_specs=[SMEM] + [VMEM] * 11 + [SMEM] + [VMEM] * 3,
        out_specs=(VMEM,) * 6,
        scratch_shapes=[
            pltpu.VMEM((16, LANES), F32),
            pltpu.VMEM((pack_rows, LANES), BF16),
            pltpu.VMEM((half + 16, LANES), BF16),
            pltpu.VMEM((samples, pixels + 2 * side, 2 * LANES), BF16),
            pltpu.VMEM((3, 2 * LANES, 3 * LANES), BF16),
            pltpu.VMEM((pixels + 16, 3 * LANES), F32),
        ],
        input_output_aliases={13: 0, 14: 1, 15: 2},
        compiler_params=params(20),
        cost_estimate=cost(0),
        name="main",
    )(
        where,
        first_pair,
        second,
        second_pair,
        taps,
        kernel,
        square,
        aff_w,
        picked,
        chan_bias,
        head,
        rgb_w,
        numbers,
        feat_t,
        style_rows,
        aff_full,
    )
    pair_losses = swap(loss_rows, "dp", 1)
    unit, to_sum = pl.pallas_call(
        functools.partial(factor_kernel, samples, side),
        out_shape=(
            shape((samples, 2, TAPS * width // 2, LANES), BF16),
            shape((8 * samples, LANES), F32),
        ),
        in_specs=[SMEM] + [VMEM] * 6,
        out_specs=(VMEM,) * 2,
        scratch_shapes=[pltpu.VMEM((pixels, TAPS * LANES), BF16)],
        compiler_params=params(16),
        cost_estimate=cost(0),
        name="factor",
    )(where, feat_t, wide, small, style_rows, kernel, aff_w)
    unit_pair = swap(unit[:, 1], "dp", 1)

    to_send = jnp.concatenate([to_sum, loss_rows[:4 * samples], pair_losses[:4 * samples]])
    sum_parts = spread_direct(to_send, "chan")
    masks = jnp.concatenate([loss_rows[4 * samples:], pair_losses[4 * samples:]])
    half_rows = TAPS * width // 2 + COUNT_ROWS
    total = pl.pallas_call(
        functools.partial(combine_kernel, n_ch, samples),
        out_shape=shape((half_rows, LANES), BF16),
        in_specs=[VMEM] * (n_ch + 3),
        out_specs=VMEM,
        compiler_params=params(8),
        cost_estimate=cost(0),
        name="combine",
    )(*sum_parts, masks, unit, unit_pair)

    lines = pack_places(samples, layers)[-1]
    pack = pl.pallas_call(
        functools.partial(mapping_back_kernel, n_ch, samples),
        out_shape=shape((lines, width), BF16),
        in_specs=[SMEM] * 2 + [VMEM] * (n_ch + 8),
        out_specs=VMEM,
        scratch_shapes=[pltpu.VMEM((8, width), F32), pltpu.VMEM((lines, width), F32)],
        compiler_params=params(12),
        cost_estimate=cost(0),
        name="mapping_back",
    )(where, numbers, *after(sum_parts, total), masks, pre, hid, top, picked, small, map_full, aff_full)
    spread_pack = spread(pack, "dp")
    packs = [part for part, _ in spread_pack]

    flat_aff = [a.reshape(2 * width, LANES) for a in (aff_w, aff_w_mom, aff_w_ema)]
    tiny = [
        map_b,
        map_b_mom,
        map_b_ema,
        chan_bias,
        chan_bias_mom,
        chan_bias_ema,
        rgb_w,
        rgb_w_mom,
        rgb_w_ema,
        w_avg.reshape(1, width),
    ]
    types = (F32, F32, F32, BF16)
    out_shape = (
        [shape(map_w.shape, t) for t in types]
        + [shape((2 * width, LANES), t) for t in types]
        + [shape(map_b.shape, t) for t in types]
        + [shape(chan_bias.shape, t) for t in types]
        + [shape(rgb_w.shape, t) for t in types]
        + [shape((1, width), F32), shape((1,), F32), shape((1,), F32)]
    )
    depth = layers * latents
    update = lambda: pl.pallas_call(
        functools.partial(update_kernel, n_dp, samples, layers, [p for _, p in spread_pack]),
        out_shape=out_shape,
        in_specs=[SMEM] + [VMEM] * (len(packs) + 6 + len(tiny)),
        out_specs=[ANY] * 23,
        scratch_shapes=[pltpu.VMEM(s.shape, s.dtype) for s in out_shape[:21]]
        + [
            pltpu.SMEM((1,), F32),
            pltpu.SMEM((1,), F32),
            pltpu.VMEM((n_dp * depth, width), BF16),
            pltpu.VMEM((n_dp * depth, width), BF16),
            pltpu.VMEM((n_dp * (lines - 2 * depth), width), BF16),
            pltpu.SemaphoreType.DMA((layers // 2 + 6, 4)),
        ],
        compiler_params=params(20),
        cost_estimate=cost(12),
        name="update",
    )(where, *packs, map_w, map_w_mom, map_w_ema, *flat_aff, *tiny)

    bits = [1 << b for b in range(1, n_dp.bit_length() - 1)]
    for turn, (even_bit, odd_bit) in enumerate(zip(bits, bits[::-1])):
        got = crossed(total, "dp", even_bit, odd_bit)
        if turn == len(bits) - 2:
            got = after(got, packs[1])
        if turn == len(bits) - 1:
            outs = update()
            got = after(got, *outs)
        total = (total.astype(F32) + got.astype(F32)).astype(BF16)
    other = swap(total, "dp", 1)

    conv_params = [flat(conv_w), flat(conv_w_mom), flat(conv_w_ema)]

    def conv_part(turns, grads, earlier):
        ninths = sum(len(n) for _, n in turns)
        return pl.pallas_call(
            functools.partial(conv_kernel, turns),
            out_shape=[shape((TAPS * width, LANES), t) for t in types],
            in_specs=[SMEM] + [VMEM] * (len(grads) + 3) + [ANY] * len(earlier),
            out_specs=[ANY] * 4,
            scratch_shapes=[pltpu.VMEM((ninths * TAPS * width // 18, LANES), t) for t in types]
            + [pltpu.SemaphoreType.DMA((ninths // 3, 4))],
            input_output_aliases={4 + len(grads) + k: k for k in range(len(earlier))},
            compiler_params=params(16),
            cost_estimate=cost(0),
            name="conv_rest" if earlier else "conv_first",
        )(where, *grads, *conv_params, *earlier)

    first_part = conv_part([(True, range(6))], [total], [])
    conv_outs = conv_part([(True, range(6, 9)), (False, range(9))], [total, other], first_part)

    map_outs, aff_outs = outs[0:4], [a.reshape(aff_w.shape) for a in outs[4:8]]
    conv_outs = [a.reshape(conv_w.shape) for a in conv_outs]
    return (
        *map_outs,
        *outs[8:12],
        *aff_outs,
        *outs[12:16],
        *conv_outs,
        *outs[16:20],
        outs[20].reshape(width),
        outs[21].reshape(()),
        outs[22].reshape(()),
    )


def solution(mesh):
    in_specs = (
        P("dp", None, None, "chan"),
        P(),
        P("dp", None),
        P("dp"),
        P("dp"),
        P(),
        P(),
        P(None, "dp", None),
        P(None, "dp", None),
        P(None, "dp", None),
        P(),
        P(),
        P(),
        P(None, None, "chan"),
        P(None, None, "chan"),
        P(None, None, "chan"),
        P(None, "chan"),
        P(None, "chan"),
        P(None, "chan"),
        P(None, None, None, "chan"),
        P(None, None, None, "chan"),
        P(None, None, None, "chan"),
        P(None, "chan"),
        P(None, "chan"),
        P(None, "chan"),
    )
    out_specs = (
        P(None, "dp", None),
        P(None, "dp", None),
        P(None, "dp", None),
        P(None, "dp", None),
        P(),
        P(),
        P(),
        P(),
        P(None, None, "chan"),
        P(None, None, "chan"),
        P(None, None, "chan"),
        P(None, None, "chan"),
        P(None, "chan"),
        P(None, "chan"),
        P(None, "chan"),
        P(None, "chan"),
        P(None, None, None, "chan"),
        P(None, None, None, "chan"),
        P(None, None, None, "chan"),
        P(None, None, None, "chan"),
        P(None, "chan"),
        P(None, "chan"),
        P(None, "chan"),
        P(None, "chan"),
        P(),
        P(),
        P(),
    )
    return jax.shard_map(local, mesh=mesh, in_specs=in_specs, out_specs=out_specs, check_vma=False)
```
